256 devices in a mesh: section: 16 (over z, core), tensor: 16 (over y, x).
Axes of the slice: x: 4, y: 4, z: 8, core: 2. Of those that a mesh axis runs over, the one named last changes fastest.
Arguments:
- teacher_hidden: bfloat16 [640, 8192], P('tensor', 'section'), may hold values from -6 to 6
- student_hidden: bfloat16 [640, 4096], P('tensor', 'section'), may hold values from -6 to 6
- teacher_head: bfloat16 [8192, 65536], P('section', 'tensor'), may hold values from -0.143631065 to 0.143631065
- student_head: bfloat16 [4096, 65536], P('section', 'tensor'), may hold values from -0.203125 to 0.203125
- targets: int32 [640], P('section'), may hold values from 0 to 65535
Outputs:
- loss: float32 [], replicated
- grad_hidden: bfloat16 [640, 4096], P('tensor', 'section')
- grad_head: bfloat16 [4096, 65536], P('section', 'tensor')
The draws below stay inside these ranges and needn't reach their ends.
All inputs are finite; a program needn't handle non-finite values.
Results may differ from the reference program's by a relative error of at most 0.0034.
Values may be sent and summed in bfloat16 or wider, within the bound.
No kernel may reach another device: no remote copies, remote signals or barrier semaphores. Data moves between devices by JAX's collectives and lax.ppermute only.
A program may use at most 128 MiB of HBM per device.

```python
import math
import jax
import jax.numpy as jnp
import numpy as np

DT = 8192
DS = 4096
VOCAB = 65536
TOKENS = 640


def aligned_rows(key):
    key = jax.random.fold_in(key, 101)
    period = min(64, max(TOKENS // 4, 1))
    offset = jax.random.randint(key, (), 0, period)
    row_ids = jnp.arange(TOKENS, dtype=jnp.int32)
    chosen = row_ids % period == offset
    level = row_ids // period % 3
    strength = jnp.where(level == 0, 2.0, jnp.where(level == 1, 2.8, 3.6)).astype(jnp.float32)
    return (chosen, strength)


def shared_direction(key, marker, width):
    key = jax.random.fold_in(key, marker)
    first_key, second_key = jax.random.split(key)
    magnitude = jax.random.uniform(first_key, (width,), jnp.float32, 0.5, 1.5)
    flips = jnp.where(jax.random.bernoulli(second_key, 0.5, (width,)), 1.0, -1.0)
    return magnitude * flips


def special_columns(key):
    key = jax.random.fold_in(key, 103)
    return jax.random.permutation(key, VOCAB)[:3].astype(jnp.int32)


def column_scale(width):
    return min(164.0 / width, 7.5 / width ** 0.5)


def aligned_columns(background, direction, columns, scale):
    column_ids = jnp.arange(background.shape[1], dtype=jnp.int32)[None, :]
    result = background
    for position, factor in enumerate((1.0, 0.9952, 0.9904)):
        result = jnp.where(column_ids == columns[position], scale * factor * direction[:, None], result)
    return result


def with_rows(key, background, marker, width):
    chosen, strength = aligned_rows(key)
    direction = shared_direction(key, marker, width)
    return jnp.where(chosen[:, None], strength[:, None] * direction[None, :], background)


def draw_teacher_hidden(key, part):
    own_key = jax.random.fold_in(key, 11)
    background = jnp.clip(jax.random.normal(own_key, (TOKENS, DT), jnp.float32), -6.0, 6.0)
    return with_rows(key, background, 201, DT).astype(jnp.bfloat16)


def draw_student_hidden(key, part):
    own_key = jax.random.fold_in(key, 12)
    background = jnp.clip(jax.random.normal(own_key, (TOKENS, DS), jnp.float32), -6.0, 6.0)
    return with_rows(key, background, 202, DS).astype(jnp.bfloat16)


def draw_teacher_head(key, part):
    own_key = jax.random.fold_in(key, 13)
    spread = 2.0 / DT ** 0.5
    background = spread * jnp.clip(jax.random.normal(own_key, (DT, VOCAB), jnp.float32), -6.0, 6.0)
    direction = shared_direction(key, 201, DT)
    return aligned_columns(background, direction, special_columns(key), column_scale(DT)).astype(jnp.bfloat16)


def draw_student_head(key, part):
    own_key = jax.random.fold_in(key, 14)
    spread = 2.0 / DS ** 0.5
    background = spread * jnp.clip(jax.random.normal(own_key, (DS, VOCAB), jnp.float32), -6.0, 6.0)
    direction = shared_direction(key, 202, DS)
    return aligned_columns(background, direction, special_columns(key), column_scale(DS)).astype(jnp.bfloat16)


def set_ends(values, key, smallest, high):
    shape = values.shape
    spot = [jax.random.randint(jax.random.fold_in(key, axis), (), 0, shape[axis]) for axis in range(len(shape))]
    values = values.at[tuple(spot)].set(smallest)
    longest = shape.index(max(shape))
    spot[longest] = (spot[longest] + 1) % shape[longest]
    return values.at[tuple(spot)].set(high)


def cumulative_ranks(count, lean):
    weights = [(1 << 20) // math.isqrt(rank ** lean) + 1 for rank in range(1, count + 1)]
    deviation = 1 + sum(weights) // (1 << 30)
    return np.cumsum(np.array([max(1, weight // deviation) for weight in weights]))


def ranked_ids(key, dims, number_of, slope):
    listing = cumulative_ranks(number_of, slope)
    lot = jax.random.randint(jax.random.fold_in(key, 1), dims, 0, int(listing[number_of - 1]))
    grade = jnp.searchsorted(jnp.asarray(listing, jnp.int32), lot, side="right")
    return jax.random.permutation(jax.random.fold_in(key, 2), number_of)[grade].astype(jnp.int32)


def setup_inputs(seed: int = 0) -> dict:
    key_of = jax.random.split(jax.random.key(seed), 6)
    return {
        "teacher_hidden": draw_teacher_hidden(jax.random.fold_in(key_of[5], 71), 0),
        "student_hidden": draw_student_hidden(jax.random.fold_in(key_of[5], 71), 0),
        "teacher_head": draw_teacher_head(jax.random.fold_in(key_of[5], 71), 0),
        "student_head": draw_student_head(jax.random.fold_in(key_of[5], 71), 0),
        "targets": set_ends(ranked_ids(key_of[4], (TOKENS,), VOCAB, 2), jax.random.fold_in(key_of[4], 3), 0, VOCAB - 1).astype(jnp.int32),
    }


tau = 2.0


def lax_dot_t(left, right):
    return jax.lax.dot_general(left, right, (((1,), (1,)), ((), ())), preferred_element_type=jnp.float32)


def reference(teacher_hidden, student_hidden, teacher_head, student_head, targets):
    teacher_logits = jnp.dot(teacher_hidden, teacher_head, preferred_element_type=jnp.float32)
    student_logits = jnp.dot(student_hidden, student_head, preferred_element_type=jnp.float32)
    log_p = jax.nn.log_softmax(teacher_logits / tau, axis=-1)
    log_q = jax.nn.log_softmax(student_logits / tau, axis=-1)
    log_s = jax.nn.log_softmax(student_logits, axis=-1)
    onehot = (jnp.arange(VOCAB, dtype=jnp.int32)[None, :] == targets[:, None]).astype(jnp.float32)
    p_prob = jnp.exp(log_p)
    row_loss = tau * tau * jnp.sum(p_prob * (log_p - log_q), axis=-1) - jnp.sum(onehot * log_s, axis=-1)
    loss = jnp.sum(row_loss) / TOKENS
    logit_grad = (tau * (jnp.exp(log_q) - p_prob) + jnp.exp(log_s) - onehot).astype(jnp.bfloat16)
    grad_hidden = lax_dot_t(logit_grad, student_head).astype(jnp.bfloat16)
    grad_head = jnp.dot(student_hidden.T, logit_grad, preferred_element_type=jnp.float32).astype(jnp.bfloat16)
    return loss, grad_hidden, grad_head
```

```python
import jax
import jax.numpy as jnp
from jax import lax
from jax.sharding import PartitionSpec as P

tau = 2.0
f32 = jnp.float32
bf16 = jnp.bfloat16


def shards(teacher_hidden, student_hidden, teacher_head, student_head, targets):
    tensor_size = lax.axis_size("tensor")
    section_size = lax.axis_size("section")
    chips = section_size // 2
    half_way = chips // 2
    me = lax.axis_index("section")
    z, core = me // 2, me % 2
    tok_block, dt = teacher_hidden.shape
    ds = student_hidden.shape[1]
    voc_local = teacher_head.shape[1]
    half = voc_local // 2

    def along(x, step):
        perm = [
            (s, ((s // 2 + step) % chips) * 2 + s % 2) for s in range(section_size)
        ]
        return lax.ppermute(x, "section", perm)

    def swap(x):
        return lax.ppermute(x, "section", [(s, s ^ 1) for s in range(section_size)])

    def spread(x, axis):
        n = lax.axis_size(axis)
        return lax.all_to_all(
            jnp.broadcast_to(x[None], (n,) + x.shape), axis, 0, 0
        )

    student_head_sib = swap(student_head)
    teacher_head_sib = swap(teacher_head)
    hidden = spread(jnp.concatenate([teacher_hidden, student_hidden], axis=1), "tensor")

    def rolled(x, which):
        pair = x.reshape((chips, 2) + x.shape[1:])
        twice = jnp.concatenate([pair, pair], axis=0)
        out = lax.dynamic_slice(
            twice, (z, which, 0, 0), (chips, 1) + x.shape[1:]
        )
        return out.reshape((chips * x.shape[1],) + x.shape[2:])

    mine = rolled(hidden, core)
    others = rolled(hidden, 1 - core)
    mine_sib = swap(others)

    def logits_part(own, own_head, sib, sib_head):
        out = jnp.dot(own, own_head, preferred_element_type=f32) + jnp.dot(
            sib, sib_head, preferred_element_type=f32
        )
        return out.reshape(chips, tok_block, voc_local)

    student_part = logits_part(
        mine[:, dt:], student_head, mine_sib[:, dt:], student_head_sib
    )
    teacher_part = logits_part(
        mine[:, :dt], teacher_head, mine_sib[:, :dt], teacher_head_sib
    )

    def ring(part):
        right = along(part[half_way][:, :half], 1)
        left = along(part[half_way][:, half:], -1)
        for hop in range(1, half_way):
            mine_r, mine_l = part[half_way - hop], part[half_way + hop]
            if hop == 1:
                right = jnp.concatenate([right + mine_r[:, :half], mine_r[:, half:]], 1)
                left = jnp.concatenate([mine_l[:, :half], left + mine_l[:, half:]], 1)
            else:
                right = right + mine_r
                left = left + mine_l
            right, left = along(right, 1), along(left, -1)
        return part[0] + right + left

    student_logits = ring(student_part)
    teacher_logits = ring(teacher_part)

    offset = lax.axis_index("tensor") * voc_local
    column_ids = offset + lax.broadcasted_iota(jnp.int32, (tok_block, voc_local), 1)
    onehot = (column_ids == targets[:, None]).astype(f32)
    t_max = jnp.max(teacher_logits, axis=1)
    s_max = jnp.max(student_logits, axis=1)
    p_terms = jnp.exp((teacher_logits - t_max[:, None]) / tau)
    q_terms = jnp.exp((student_logits - s_max[:, None]) / tau)
    s_terms = jnp.exp(student_logits - s_max[:, None])
    stats = jnp.stack(
        [
            t_max,
            s_max,
            jnp.sum(p_terms, axis=1),
            jnp.sum(q_terms, axis=1),
            jnp.sum(s_terms, axis=1),
            jnp.sum(p_terms * (teacher_logits - student_logits), axis=1),
            jnp.sum(onehot * student_logits, axis=1),
            jnp.zeros_like(t_max),
        ]
    )
    every = spread(stats, "tensor")
    teacher_max = jnp.max(every[:, 0], axis=0)
    student_max = jnp.max(every[:, 1], axis=0)
    t_weight = jnp.exp((every[:, 0] - teacher_max) / tau)
    q_weight = jnp.exp((every[:, 1] - student_max) / tau)
    s_weight = jnp.exp(every[:, 1] - student_max)
    p_total = jnp.sum(t_weight * every[:, 2], axis=0)
    q_total = jnp.sum(q_weight * every[:, 3], axis=0)
    s_total = jnp.sum(s_weight * every[:, 4], axis=0)
    cross = jnp.sum(t_weight * every[:, 5], axis=0)
    picked = jnp.sum(every[:, 6], axis=0)
    kl_rows = (
        cross / (tau * p_total)
        - (teacher_max - student_max) / tau
        - jnp.log(p_total)
        + jnp.log(q_total)
    )
    row_loss = tau * tau * kl_rows + student_max + jnp.log(s_total) - picked

    p_prob = jnp.exp((teacher_logits - teacher_max[:, None]) / tau) / p_total[:, None]
    q_prob = jnp.exp((student_logits - student_max[:, None]) / tau) / q_total[:, None]
    s_prob = jnp.exp(student_logits - student_max[:, None]) / s_total[:, None]
    grad = (tau * (q_prob - p_prob) + s_prob - onehot).astype(bf16)

    pieces = [None] * chips
    pieces[0] = grad
    right = left = grad
    for hop in range(1, half_way):
        right, left = along(right, 1), along(left, -1)
        pieces[chips - hop], pieces[hop] = right, left
    pieces[half_way] = jnp.concatenate(
        [along(right[:, :half], 1), along(left[:, half:], -1)], axis=1
    )
    lg = jnp.concatenate(pieces, axis=0)
    lg_sib = swap(lg)

    loss_parts = spread(jnp.full((8, 128), jnp.sum(row_loss), f32), "section")
    loss = jnp.sum(loss_parts[:, 0, 0]) / (tok_block * section_size)

    def back(x):
        return lax.dot_general(
            x, student_head, (((1,), (1,)), ((), ())), preferred_element_type=f32
        ).reshape(chips, 1, tok_block, ds)

    rows_own, rows_sib = back(lg), back(lg_sib)
    rows = jnp.where(
        core == 0,
        jnp.concatenate([rows_own, rows_sib], axis=1),
        jnp.concatenate([rows_sib, rows_own], axis=1),
    )
    rows = jnp.concatenate([rows, rows], axis=0)
    rows = lax.dynamic_slice(
        rows, ((chips - z) % chips, 0, 0, 0), (chips, 2, tok_block, ds)
    ).reshape(tensor_size, tok_block, ds)
    grad_hidden = jnp.sum(lax.all_to_all(rows, "tensor", 0, 0), axis=0).astype(bf16)

    def outer(x, g):
        return lax.dot_general(
            x, g, (((0,), (0,)), ((), ())), preferred_element_type=f32
        )

    grad_head = (outer(mine[:, dt:], lg) + outer(others[:, dt:], lg_sib)).astype(bf16)
    return loss, grad_hidden, grad_head


def solution(mesh):
    placed = (
        P("tensor", "section"),
        P("tensor", "section"),
        P("section", "tensor"),
        P("section", "tensor"),
        P("section"),
    )
    return jax.shard_map(
        shards,
        mesh=mesh,
        in_specs=placed,
        out_specs=(P(), P("tensor", "section"), P("section", "tensor")),
        check_vma=False,
    )
```

```python
import jax
import jax.numpy as jnp
from jax import lax
from jax.experimental import pallas as pl
from jax.experimental.pallas import tpu as pltpu
from jax.sharding import PartitionSpec as P

tau = 2.0
f32 = jnp.float32
bf16 = jnp.bfloat16
i16 = jnp.int16

LEVELS = 32767.0
CODES = 128
LIMIT = 1000.0
STRIP = 512
PARAMS = pltpu.CompilerParams(vmem_limit_bytes=48 * 1024 * 1024)


def row_codes(ref):
    w = ref.shape[1] - CODES
    codes = ref[:, w:].astype(jnp.int32).astype(f32)
    middle = codes[:, 0:1] * 0.25
    scale = codes[:, 32:33] * (0.5 / LEVELS)
    return middle, scale, codes[:, 64:65]


def encode(x_ref, columns, o_ref, spent):
    lo, hi = columns
    top = bottom = None
    for at in range(lo, hi, STRIP):
        x = x_ref[:, at : at + STRIP]
        top = x if top is None else jnp.maximum(top, x)
        bottom = x if bottom is None else jnp.minimum(bottom, x)
    top = jnp.max(top, axis=1, keepdims=True)
    bottom = jnp.min(bottom, axis=1, keepdims=True)
    middle_code = jnp.round((top + bottom) * 2.0)
    middle = middle_code * 0.25
    reach = jnp.maximum(top - middle, middle - bottom)
    reach_code = jnp.floor(reach * 2.0) + 1.0
    spent_code = jnp.minimum(spent + reach_code, LEVELS)
    inverse = (2.0 * LEVELS) / reach_code
    for at in range(lo, hi, STRIP):
        code = jnp.round((x_ref[:, at : at + STRIP] - middle) * inverse)
        o_ref[:, at - lo : at - lo + STRIP] = code.astype(jnp.int32).astype(i16)
    lane = lax.broadcasted_iota(jnp.int32, (x_ref.shape[0], CODES), 1)
    codes = jnp.where(lane < 32, middle_code, jnp.where(lane < 64, reach_code, spent_code))
    o_ref[:, hi - lo :] = codes.astype(jnp.int32).astype(i16)


def first_kernel(part_ref, right_ref, left_ref):
    width = part_ref.shape[2]
    none = jnp.zeros((part_ref.shape[1], 1), f32)
    encode(part_ref.at[0], (0, width // 2), right_ref, none)
    encode(part_ref.at[0], (width // 2, width), left_ref, none)


def hop_kernel(r_ref, l_ref, pr_ref, pl_ref, ro_ref, lo_ref, sum_ref):
    width = pr_ref.shape[2]
    for in_ref, part_ref, out_ref, at_end in (
        (r_ref, pr_ref, ro_ref, False),
        (l_ref, pl_ref, lo_ref, True),
    ):
        carried = in_ref.shape[1] - CODES
        start = width - carried if at_end else 0
        middle, scale, spent = row_codes(in_ref)
        for at in range(0, width, STRIP):
            x = part_ref[0, :, at : at + STRIP]
            if start <= at < start + carried:
                code = in_ref[:, at - start : at - start + STRIP]
                x = x + (middle + code.astype(jnp.int32).astype(f32) * scale)
            sum_ref[:, at : at + STRIP] = x
        encode(sum_ref, (0, width), out_ref, spent)


def meet_kernel(
    rt_ref, lt_ref, pt_ref, rs_ref, ls_ref, ps_ref, target_ref, t_ref, s_ref, stats_ref
):
    rows, width = t_ref.shape
    tops, spents = [], []
    for r_ref, l_ref, part_ref, out_ref in (
        (rt_ref, lt_ref, pt_ref, t_ref),
        (rs_ref, ls_ref, ps_ref, s_ref),
    ):
        r_middle, r_scale, r_spent = row_codes(r_ref)
        l_middle, l_scale, l_spent = row_codes(l_ref)
        top = None
        for at in range(0, width, STRIP):
            strip = slice(at, at + STRIP)
            x = (
                part_ref[0, :, strip]
                + (r_middle + r_ref[:, strip].astype(jnp.int32).astype(f32) * r_scale)
                + (l_middle + l_ref[:, strip].astype(jnp.int32).astype(f32) * l_scale)
            )
            out_ref[:, strip] = x
            top = x if top is None else jnp.maximum(top, x)
        tops.append(jnp.max(top, axis=1, keepdims=True))
        spents.append((r_spent + l_spent) * 0.5)
    t_max, s_max = tops
    target = target_ref[:, 0:1]
    sums = None
    for at in range(0, width, 128):
        t, s = t_ref[:, at : at + 128], s_ref[:, at : at + 128]
        p = jnp.exp((t - t_max) * (1.0 / tau))
        q = jnp.exp((s - s_max) * (1.0 / tau))
        ids = at + lax.broadcasted_iota(jnp.int32, t.shape, 1)
        terms = (p, q, q * q, p * (t - s), jnp.where(ids == target, s, 0.0))
        sums = terms if sums is None else [a + b for a, b in zip(sums, terms)]
    lane = lax.broadcasted_iota(jnp.int32, (rows, 128), 1)
    kinds = [t_max, s_max] + [jnp.sum(a, axis=1, keepdims=True) for a in sums]
    kinds.append(jnp.maximum(spents[0], spents[1]))
    table = jnp.zeros((rows, 128), f32)
    for k, value in enumerate(kinds):
        table = jnp.where(lane == k, value, table)
    table = jnp.concatenate([table, jnp.zeros((128 - rows, 128), f32)], axis=0)
    stats_ref[...] = table.T[0:8, :]


def whole(x):
    return pl.BlockSpec(x.shape, lambda i: (0,) * len(x.shape))


def part_at(part, j):
    return pl.BlockSpec((1,) + part.shape[1:], lambda i: (j, 0, 0))


def first(part, j):
    rows, width = part.shape[1:]
    out = jax.ShapeDtypeStruct((rows, width // 2 + CODES), i16)
    return pl.pallas_call(
        first_kernel,
        out_shape=(out, out),
        in_specs=[part_at(part, j)],
        out_specs=(whole(out), whole(out)),
        grid=(1,),
        compiler_params=PARAMS,
        name="first",
    )(part)


def hop(right, left, part, jr, jl):
    rows, width = part.shape[1:]
    out = jax.ShapeDtypeStruct((rows, width + CODES), i16)
    return pl.pallas_call(
        hop_kernel,
        out_shape=(out, out),
        in_specs=[whole(right), whole(left), part_at(part, jr), part_at(part, jl)],
        out_specs=(whole(out), whole(out)),
        scratch_shapes=[pltpu.VMEM((rows, width), f32)],
        grid=(1,),
        compiler_params=PARAMS,
        name="hop",
    )(right, left, part, part)


def meet(teacher, student, target):
    (rt, lt, pt), (rs, ls, ps) = teacher, student
    rows, width = pt.shape[1:]
    logits = jax.ShapeDtypeStruct((rows, width), f32)
    stats = jax.ShapeDtypeStruct((8, 128), f32)
    return pl.pallas_call(
        meet_kernel,
        out_shape=(logits, logits, stats),
        in_specs=[
            whole(rt), whole(lt), part_at(pt, 0), whole(rs), whole(ls), part_at(ps, 0),
            whole(target),
        ],
        out_specs=(whole(logits), whole(logits), whole(stats)),
        grid=(1,),
        compiler_params=PARAMS,
        name="meet",
    )(rt, lt, pt, rs, ls, ps, target)


def shards(teacher_hidden, student_hidden, teacher_head, student_head, targets):
    tensor_size = lax.axis_size("tensor")
    section_size = lax.axis_size("section")
    chips = section_size // 2
    half_way = chips // 2
    me = lax.axis_index("section")
    z, core = me // 2, me % 2
    tok_block, dt = teacher_hidden.shape
    ds = student_hidden.shape[1]
    voc_local = teacher_head.shape[1]
    half = voc_local // 2

    def along(x, step):
        perm = [
            (s, ((s // 2 + step) % chips) * 2 + s % 2) for s in range(section_size)
        ]
        return lax.ppermute(x, "section", perm)

    def swap(x):
        return lax.ppermute(x, "section", [(s, s ^ 1) for s in range(section_size)])

    def spread(x, axis):
        n = lax.axis_size(axis)
        return lax.all_to_all(
            jnp.broadcast_to(x[None], (n,) + x.shape), axis, 0, 0
        )

    student_head_sib = swap(student_head)
    teacher_head_sib = swap(teacher_head)
    hidden = spread(jnp.concatenate([teacher_hidden, student_hidden], axis=1), "tensor")

    def rolled(x, which):
        pair = x.reshape((chips, 2) + x.shape[1:])
        twice = jnp.concatenate([pair, pair], axis=0)
        out = lax.dynamic_slice(
            twice, (z, which, 0, 0), (chips, 1) + x.shape[1:]
        )
        return out.reshape((chips * x.shape[1],) + x.shape[2:])

    mine = rolled(hidden, core)
    others = rolled(hidden, 1 - core)
    mine_sib = swap(others)

    def logits_part(own, own_head, sib, sib_head):
        out = jnp.dot(own, own_head, preferred_element_type=f32) + jnp.dot(
            sib, sib_head, preferred_element_type=f32
        )
        return out.reshape(chips, tok_block, voc_local)

    student_part = logits_part(
        mine[:, dt:], student_head, mine_sib[:, dt:], student_head_sib
    )
    teacher_part = logits_part(
        mine[:, :dt], teacher_head, mine_sib[:, :dt], teacher_head_sib
    )

    def ring(part):
        right, left = first(part, half_way)
        right, left = along(right, 1), along(left, -1)
        for step in range(1, half_way):
            right, left = hop(right, left, part, half_way - step, half_way + step)
            right, left = along(right, 1), along(left, -1)
        return right, left, part

    def ring_wide(part):
        right = along(part[half_way][:, :half], 1)
        left = along(part[half_way][:, half:], -1)
        for step in range(1, half_way):
            mine_r, mine_l = part[half_way - step], part[half_way + step]
            if step == 1:
                right = jnp.concatenate([right + mine_r[:, :half], mine_r[:, half:]], 1)
                left = jnp.concatenate([mine_l[:, :half], left + mine_l[:, half:]], 1)
            else:
                right = right + mine_r
                left = left + mine_l
            right, left = along(right, 1), along(left, -1)
        return part[0] + right + left

    offset = lax.axis_index("tensor") * voc_local
    target_here = jnp.broadcast_to((targets - offset)[:, None], (tok_block, 128))
    column_ids = lax.broadcasted_iota(jnp.int32, (tok_block, voc_local), 1)
    onehot = (column_ids == target_here[:, :1]).astype(f32)

    def statistics(teacher_logits, student_logits):
        t_max = jnp.max(teacher_logits, axis=1)
        s_max = jnp.max(student_logits, axis=1)
        p_terms = jnp.exp((teacher_logits - t_max[:, None]) / tau)
        q_terms = jnp.exp((student_logits - s_max[:, None]) / tau)
        s_terms = jnp.exp(student_logits - s_max[:, None])
        stats = jnp.stack(
            [
                t_max,
                s_max,
                jnp.sum(p_terms, axis=1),
                jnp.sum(q_terms, axis=1),
                jnp.sum(s_terms, axis=1),
                jnp.sum(p_terms * (teacher_logits - student_logits), axis=1),
                jnp.sum(onehot * student_logits, axis=1),
                jnp.zeros_like(t_max),
            ]
        )
        return jnp.pad(stats, ((0, 0), (0, 128 - tok_block)))

    def gradients(teacher_logits, student_logits, stats):
        every = spread(stats, "tensor")[:, :, :tok_block]
        teacher_max = jnp.max(every[:, 0], axis=0)
        student_max = jnp.max(every[:, 1], axis=0)
        t_weight = jnp.exp((every[:, 0] - teacher_max) / tau)
        q_weight = jnp.exp((every[:, 1] - student_max) / tau)
        s_weight = jnp.exp(every[:, 1] - student_max)
        p_total = jnp.sum(t_weight * every[:, 2], axis=0)
        q_total = jnp.sum(q_weight * every[:, 3], axis=0)
        s_total = jnp.sum(s_weight * every[:, 4], axis=0)
        cross = jnp.sum(t_weight * every[:, 5], axis=0)
        picked = jnp.sum(every[:, 6], axis=0)
        spent = jnp.max(every[:, 7])
        kl_rows = (
            cross / (tau * p_total)
            - (teacher_max - student_max) / tau
            - jnp.log(p_total)
            + jnp.log(q_total)
        )
        row_loss = tau * tau * kl_rows + student_max + jnp.log(s_total) - picked

        p_prob = jnp.exp((teacher_logits - teacher_max[:, None]) / tau) / p_total[:, None]
        q_prob = jnp.exp((student_logits - student_max[:, None]) / tau) / q_total[:, None]
        s_prob = jnp.exp(student_logits - student_max[:, None]) / s_total[:, None]
        grad = (tau * (q_prob - p_prob) + s_prob - onehot).astype(bf16)

        pieces = [None] * chips
        pieces[0] = grad
        right = left = grad
        for step in range(1, half_way):
            right, left = along(right, 1), along(left, -1)
            pieces[chips - step], pieces[step] = right, left
        pieces[half_way] = jnp.concatenate(
            [along(right[:, :half], 1), along(left[:, half:], -1)], axis=1
        )
        lg = jnp.concatenate(pieces, axis=0)
        lg_sib = swap(lg)

        lane = lax.broadcasted_iota(jnp.int32, (8, 128), 1)
        shared = spread(jnp.where(lane == 0, jnp.sum(row_loss), spent), "section")
        loss = jnp.sum(shared[:, 0, 0]) / (tok_block * section_size)
        spent = jnp.max(shared[:, 0, 1])

        def back(x):
            return lax.dot_general(
                x, student_head, (((1,), (1,)), ((), ())), preferred_element_type=f32
            ).reshape(chips, 1, tok_block, ds)

        rows_own, rows_sib = back(lg), back(lg_sib)
        rows = jnp.where(
            core == 0,
            jnp.concatenate([rows_own, rows_sib], axis=1),
            jnp.concatenate([rows_sib, rows_own], axis=1),
        )
        rows = jnp.concatenate([rows, rows], axis=0)
        rows = lax.dynamic_slice(
            rows, ((chips - z) % chips, 0, 0, 0), (chips, 2, tok_block, ds)
        ).reshape(tensor_size, tok_block, ds)
        grad_hidden = jnp.sum(lax.all_to_all(rows, "tensor", 0, 0), axis=0).astype(bf16)

        def outer(x, g):
            return lax.dot_general(
                x, g, (((0,), (0,)), ((), ())), preferred_element_type=f32
            )

        grad_head = (outer(mine[:, dt:], lg) + outer(others[:, dt:], lg_sib)).astype(bf16)
        return (loss, grad_hidden, grad_head), spent

    teacher_logits, student_logits, stats = meet(
        ring(teacher_part), ring(student_part), target_here
    )
    fine, spent = gradients(teacher_logits, student_logits, stats)

    def wide():
        teacher, student = ring_wide(teacher_part), ring_wide(student_part)
        return gradients(teacher, student, statistics(teacher, student))[0]

    return lax.cond(spent > LIMIT, wide, lambda: fine)


def solution(mesh):
    placed = (
        P("tensor", "section"),
        P("tensor", "section"),
        P("section", "tensor"),
        P("section", "tensor"),
        P("section"),
    )
    return jax.shard_map(
        shards,
        mesh=mesh,
        in_specs=placed,
        out_specs=(P(), P("tensor", "section"), P("section", "tensor")),
        check_vma=False,
    )
```

```python
import jax
import jax.numpy as jnp
from jax import lax
from jax.experimental import pallas as pl
from jax.experimental.pallas import tpu as pltpu
from jax.sharding import PartitionSpec as P

tau = 2.0
f32 = jnp.float32
bf16 = jnp.bfloat16
i16 = jnp.int16

LEVELS = 32767.0
CODES = 128
LIMIT = 1000.0
STRIP = 512
PARAMS = pltpu.CompilerParams(vmem_limit_bytes=48 * 1024 * 1024)


def row_codes(ref):
    w = ref.shape[1] - CODES
    codes = ref[:, w:].astype(jnp.int32).astype(f32)
    middle = codes[:, 0:1] * 0.25
    scale = codes[:, 32:33] * (0.5 / LEVELS)
    return middle, scale, codes[:, 64:65]


def encode(x_ref, columns, o_ref, spent):
    lo, hi = columns
    top = bottom = None
    for at in range(lo, hi, STRIP):
        x = x_ref[:, at : at + STRIP]
        top = x if top is None else jnp.maximum(top, x)
        bottom = x if bottom is None else jnp.minimum(bottom, x)
    top = jnp.max(top, axis=1, keepdims=True)
    bottom = jnp.min(bottom, axis=1, keepdims=True)
    middle_code = jnp.round((top + bottom) * 2.0)
    middle = middle_code * 0.25
    reach = jnp.maximum(top - middle, middle - bottom)
    reach_code = jnp.floor(reach * 2.0) + 1.0
    spent_code = jnp.minimum(spent + reach_code, LEVELS)
    inverse = (2.0 * LEVELS) / reach_code
    for at in range(lo, hi, STRIP):
        code = jnp.round((x_ref[:, at : at + STRIP] - middle) * inverse)
        o_ref[:, at - lo : at - lo + STRIP] = code.astype(jnp.int32).astype(i16)
    lane = lax.broadcasted_iota(jnp.int32, (x_ref.shape[0], CODES), 1)
    codes = jnp.where(lane < 32, middle_code, jnp.where(lane < 64, reach_code, spent_code))
    o_ref[:, hi - lo :] = codes.astype(jnp.int32).astype(i16)


def first_kernel(part_ref, right_ref, left_ref):
    width = part_ref.shape[2]
    none = jnp.zeros((part_ref.shape[1], 1), f32)
    encode(part_ref.at[0], (0, width // 2), right_ref, none)
    encode(part_ref.at[0], (width // 2, width), left_ref, none)


def hop_kernel(r_ref, l_ref, pr_ref, pl_ref, ro_ref, lo_ref, sum_ref):
    width = pr_ref.shape[2]
    for in_ref, part_ref, out_ref, at_end in (
        (r_ref, pr_ref, ro_ref, False),
        (l_ref, pl_ref, lo_ref, True),
    ):
        carried = in_ref.shape[1] - CODES
        start = width - carried if at_end else 0
        middle, scale, spent = row_codes(in_ref)
        for at in range(0, width, STRIP):
            x = part_ref[0, :, at : at + STRIP]
            if start <= at < start + carried:
                code = in_ref[:, at - start : at - start + STRIP]
                x = x + (middle + code.astype(jnp.int32).astype(f32) * scale)
            sum_ref[:, at : at + STRIP] = x
        encode(sum_ref, (0, width), out_ref, spent)


def meet_kernel(
    rt_ref, lt_ref, pt_ref, rs_ref, ls_ref, ps_ref, target_ref, t_ref, s_ref, stats_ref
):
    rows, width = t_ref.shape
    tops, spents = [], []
    for r_ref, l_ref, part_ref, out_ref in (
        (rt_ref, lt_ref, pt_ref, t_ref),
        (rs_ref, ls_ref, ps_ref, s_ref),
    ):
        r_middle, r_scale, r_spent = row_codes(r_ref)
        l_middle, l_scale, l_spent = row_codes(l_ref)
        top = None
        for at in range(0, width, STRIP):
            strip = slice(at, at + STRIP)
            x = (
                part_ref[0, :, strip]
                + (r_middle + r_ref[:, strip].astype(jnp.int32).astype(f32) * r_scale)
                + (l_middle + l_ref[:, strip].astype(jnp.int32).astype(f32) * l_scale)
            )
            out_ref[:, strip] = x
            top = x if top is None else jnp.maximum(top, x)
        tops.append(jnp.max(top, axis=1, keepdims=True))
        spents.append((r_spent + l_spent) * 0.5)
    t_max, s_max = tops
    target = target_ref[:, 0:1]
    sums = None
    for at in range(0, width, 128):
        t, s = t_ref[:, at : at + 128], s_ref[:, at : at + 128]
        p = jnp.exp((t - t_max) * (1.0 / tau))
        q = jnp.exp((s - s_max) * (1.0 / tau))
        ids = at + lax.broadcasted_iota(jnp.int32, t.shape, 1)
        terms = (p, q, q * q, p * (t - s), jnp.where(ids == target, s, 0.0))
        sums = terms if sums is None else [a + b for a, b in zip(sums, terms)]
    lane = lax.broadcasted_iota(jnp.int32, (rows, 128), 1)
    kinds = [t_max, s_max] + [jnp.sum(a, axis=1, keepdims=True) for a in sums]
    kinds.append(jnp.maximum(spents[0], spents[1]))
    table = jnp.zeros((rows, 128), f32)
    for k, value in enumerate(kinds):
        table = jnp.where(lane == k, value, table)
    table = jnp.concatenate([table, jnp.zeros((128 - rows, 128), f32)], axis=0)
    stats_ref[...] = table.T[0:8, :]


def grad_kernel(t_ref, s_ref, every_ref, target_ref, o_ref):
    rows, width = t_ref.shape
    t_tops, s_tops = every_ref[:, 0, :], every_ref[:, 1, :]
    t_max = jnp.max(t_tops, axis=0, keepdims=True)
    s_max = jnp.max(s_tops, axis=0, keepdims=True)
    t_weight = jnp.exp((t_tops - t_max) * (1.0 / tau))
    q_weight = jnp.exp((s_tops - s_max) * (1.0 / tau))
    s_weight = jnp.exp(s_tops - s_max)

    def total(k, weight):
        return jnp.sum(every_ref[:, k, :] * weight, axis=0, keepdims=True)

    p_total, q_total = total(2, t_weight), total(3, q_weight)
    s_total, cross = total(4, s_weight), total(5, t_weight)
    picked = jnp.sum(every_ref[:, 6, :], axis=0, keepdims=True)
    spent = jnp.max(every_ref[:, 7, :], axis=0, keepdims=True)
    kl_rows = (
        cross / (tau * p_total)
        - (t_max - s_max) / tau
        - jnp.log(p_total)
        + jnp.log(q_total)
    )
    row_loss = tau * tau * kl_rows + s_max + jnp.log(s_total) - picked
    flag = jnp.where(spent > LIMIT, 1.0, 0.0)
    lines = [t_max, s_max, tau / p_total, tau / q_total, 1.0 / s_total, row_loss, flag]
    lines.append(jnp.zeros((128 - len(lines), 128), f32))
    table = jnp.concatenate(lines, axis=0).T[:rows]
    t_max, s_max, p_scale, q_scale, s_scale, row_loss, flag = (
        table[:, k : k + 1] for k in range(7)
    )
    target = target_ref[:, 0:1]
    for at in range(0, width, STRIP):
        t, s = t_ref[:, at : at + STRIP], s_ref[:, at : at + STRIP]
        p = jnp.exp((t - t_max) * (1.0 / tau))
        q = jnp.exp((s - s_max) * (1.0 / tau))
        ids = at + lax.broadcasted_iota(jnp.int32, t.shape, 1)
        grad = q * q_scale - p * p_scale + (q * q) * s_scale
        grad = grad - jnp.where(ids == target, 1.0, 0.0)
        o_ref[:, at : at + STRIP] = grad.astype(bf16)
    high = row_loss.astype(bf16).astype(f32)
    mid = (row_loss - high).astype(bf16).astype(f32)
    low = row_loss - high - mid
    lane = lax.broadcasted_iota(jnp.int32, (rows, CODES), 1)
    extra = jnp.where(
        lane == 0,
        high,
        jnp.where(lane == 1, mid, jnp.where(lane == 2, low, jnp.where(lane == 3, flag, 0.0))),
    )
    o_ref[:, width:] = extra.astype(bf16)


def whole(x):
    return pl.BlockSpec(x.shape, lambda i: (0,) * len(x.shape))


def part_at(part, j):
    return pl.BlockSpec((1,) + part.shape[1:], lambda i: (j, 0, 0))


def first(part, j):
    rows, width = part.shape[1:]
    out = jax.ShapeDtypeStruct((rows, width // 2 + CODES), i16)
    return pl.pallas_call(
        first_kernel,
        out_shape=(out, out),
        in_specs=[part_at(part, j)],
        out_specs=(whole(out), whole(out)),
        grid=(1,),
        compiler_params=PARAMS,
        name="first",
    )(part)


def hop(right, left, part, jr, jl):
    rows, width = part.shape[1:]
    out = jax.ShapeDtypeStruct((rows, width + CODES), i16)
    return pl.pallas_call(
        hop_kernel,
        out_shape=(out, out),
        in_specs=[whole(right), whole(left), part_at(part, jr), part_at(part, jl)],
        out_specs=(whole(out), whole(out)),
        scratch_shapes=[pltpu.VMEM((rows, width), f32)],
        grid=(1,),
        compiler_params=PARAMS,
        name="hop",
    )(right, left, part, part)


def meet(teacher, student, target):
    (rt, lt, pt), (rs, ls, ps) = teacher, student
    rows, width = pt.shape[1:]
    logits = jax.ShapeDtypeStruct((rows, width), f32)
    stats = jax.ShapeDtypeStruct((8, 128), f32)
    return pl.pallas_call(
        meet_kernel,
        out_shape=(logits, logits, stats),
        in_specs=[
            whole(rt), whole(lt), part_at(pt, 0), whole(rs), whole(ls), part_at(ps, 0),
            whole(target),
        ],
        out_specs=(whole(logits), whole(logits), whole(stats)),
        grid=(1,),
        compiler_params=PARAMS,
        name="meet",
    )(rt, lt, pt, rs, ls, ps, target)


def payload(teacher_logits, student_logits, every, target):
    rows, width = teacher_logits.shape
    out = jax.ShapeDtypeStruct((rows, width + CODES), bf16)
    return pl.pallas_call(
        grad_kernel,
        out_shape=out,
        in_specs=[whole(x) for x in (teacher_logits, student_logits, every, target)],
        out_specs=whole(out),
        grid=(1,),
        compiler_params=PARAMS,
        name="payload",
    )(teacher_logits, student_logits, every, target)


def shards(teacher_hidden, student_hidden, teacher_head, student_head, targets):
    tensor_size = lax.axis_size("tensor")
    section_size = lax.axis_size("section")
    chips = section_size // 2
    half_way = chips // 2
    me = lax.axis_index("section")
    z, core = me // 2, me % 2
    tok_block, dt = teacher_hidden.shape
    ds = student_hidden.shape[1]
    voc_local = teacher_head.shape[1]
    half = voc_local // 2

    def along(x, step):
        perm = [
            (s, ((s // 2 + step) % chips) * 2 + s % 2) for s in range(section_size)
        ]
        return lax.ppermute(x, "section", perm)

    def swap(x):
        return lax.ppermute(x, "section", [(s, s ^ 1) for s in range(section_size)])

    def spread(x, axis):
        n = lax.axis_size(axis)
        return lax.all_to_all(
            jnp.broadcast_to(x[None], (n,) + x.shape), axis, 0, 0
        )

    student_head_sib = swap(student_head)
    teacher_head_sib = swap(teacher_head)
    student_all = spread(student_hidden, "tensor")
    teacher_hidden, student_all = lax.optimization_barrier((teacher_hidden, student_all))
    teacher_all = spread(teacher_hidden, "tensor")

    def rolled(x, which):
        pair = x.reshape((chips, 2) + x.shape[1:])
        twice = jnp.concatenate([pair, pair], axis=0)
        out = lax.dynamic_slice(
            twice, (z, which, 0, 0), (chips, 1) + x.shape[1:]
        )
        return out.reshape((chips * x.shape[1],) + x.shape[2:])

    def logits_part(hidden, head, head_sib):
        mine, others = rolled(hidden, core), rolled(hidden, 1 - core)
        out = jnp.dot(mine, head, preferred_element_type=f32) + jnp.dot(
            swap(others), head_sib, preferred_element_type=f32
        )
        return mine, others, out.reshape(chips, tok_block, voc_local)

    student_mine, student_others, student_part = logits_part(
        student_all, student_head, student_head_sib
    )
    _, _, teacher_part = logits_part(teacher_all, teacher_head, teacher_head_sib)

    def ring(part):
        right, left = first(part, half_way)
        right, left = along(right, 1), along(left, -1)
        for step in range(1, half_way):
            right, left = hop(right, left, part, half_way - step, half_way + step)
            right, left = along(right, 1), along(left, -1)
        return right, left, part

    def ring_wide(part):
        right = along(part[half_way][:, :half], 1)
        left = along(part[half_way][:, half:], -1)
        for step in range(1, half_way):
            mine_r, mine_l = part[half_way - step], part[half_way + step]
            if step == 1:
                right = jnp.concatenate([right + mine_r[:, :half], mine_r[:, half:]], 1)
                left = jnp.concatenate([mine_l[:, :half], left + mine_l[:, half:]], 1)
            else:
                right = right + mine_r
                left = left + mine_l
            right, left = along(right, 1), along(left, -1)
        return part[0] + right + left

    offset = lax.axis_index("tensor") * voc_local
    target_here = jnp.broadcast_to((targets - offset)[:, None], (tok_block, 128))

    def statistics(teacher_logits, student_logits):
        column_ids = lax.broadcasted_iota(jnp.int32, (tok_block, voc_local), 1)
        onehot = (column_ids == target_here[:, :1]).astype(f32)
        t_max = jnp.max(teacher_logits, axis=1)
        s_max = jnp.max(student_logits, axis=1)
        p_terms = jnp.exp((teacher_logits - t_max[:, None]) / tau)
        q_terms = jnp.exp((student_logits - s_max[:, None]) / tau)
        s_terms = jnp.exp(student_logits - s_max[:, None])
        stats = jnp.stack(
            [
                t_max,
                s_max,
                jnp.sum(p_terms, axis=1),
                jnp.sum(q_terms, axis=1),
                jnp.sum(s_terms, axis=1),
                jnp.sum(p_terms * (teacher_logits - student_logits), axis=1),
                jnp.sum(onehot * student_logits, axis=1),
                jnp.zeros_like(t_max),
            ]
        )
        return jnp.pad(stats, ((0, 0), (0, 128 - tok_block)))

    def gradients(teacher_logits, student_logits, stats):
        own = payload(teacher_logits, student_logits, spread(stats, "tensor"), target_here)

        pieces = [None] * chips
        pieces[0] = right = left = own
        for step in range(1, half_way):
            right, left = along(right, 1), along(left, -1)
            pieces[chips - step], pieces[step] = right, left
        pieces[half_way] = jnp.concatenate(
            [along(right[:, :half], 1), along(left[:, half:], -1)], axis=1
        )
        near = [0] + [j for k in range(1, half_way - 1) for j in (chips - k, k)]
        far = [j for j in range(chips) if j not in near]

        def blocks(x, order):
            x = x.reshape(chips, tok_block, ds)
            return jnp.concatenate([x[j] for j in order], axis=0)

        groups = []
        for order in (near, far):
            mine = jnp.concatenate([pieces[j] for j in order], axis=0)
            groups.append((blocks(student_mine, order), mine))
            groups.append((blocks(student_others, order), swap(mine)))

        extra = sum(
            jnp.sum(g[:, voc_local:].astype(f32), axis=0) for _, g in groups
        )
        loss = (extra[0] + extra[1] + extra[2]) / (tok_block * section_size)

        def back(g):
            return lax.dot_general(
                g[:, :voc_local],
                student_head,
                (((1,), (1,)), ((), ())),
                preferred_element_type=f32,
            )

        def in_order(near_rows, far_rows):
            rows = jnp.concatenate([near_rows, far_rows], axis=0)
            rows = rows.reshape(chips, tok_block, ds)
            order = near + far
            return jnp.stack([rows[order.index(j)] for j in range(chips)])

        rows_own = in_order(back(groups[0][1]), back(groups[2][1]))
        rows_sib = in_order(back(groups[1][1]), back(groups[3][1]))
        rows = jnp.where(
            core == 0,
            jnp.stack([rows_own, rows_sib], axis=1),
            jnp.stack([rows_sib, rows_own], axis=1),
        )
        rows = jnp.concatenate([rows, rows], axis=0)
        rows = lax.dynamic_slice(
            rows, ((chips - z) % chips, 0, 0, 0), (chips, 2, tok_block, ds)
        ).reshape(tensor_size, tok_block, ds)
        grad_hidden = jnp.sum(lax.all_to_all(rows, "tensor", 0, 0), axis=0).astype(bf16)

        grad_head = sum(
            lax.dot_general(
                x,
                g[:, :voc_local],
                (((0,), (0,)), ((), ())),
                preferred_element_type=f32,
            )
            for x, g in groups
        ).astype(bf16)
        return (loss, grad_hidden, grad_head), extra[3]

    teacher_logits, student_logits, stats = meet(
        ring(teacher_part), ring(student_part), target_here
    )
    fine, flags = gradients(teacher_logits, student_logits, stats)

    def wide():
        teacher, student = ring_wide(teacher_part), ring_wide(student_part)
        return gradients(teacher, student, statistics(teacher, student))[0]

    return lax.cond(flags > 0.0, wide, lambda: fine)


def solution(mesh):
    placed = (
        P("tensor", "section"),
        P("tensor", "section"),
        P("section", "tensor"),
        P("section", "tensor"),
        P("section"),
    )
    return jax.shard_map(
        shards,
        mesh=mesh,
        in_specs=placed,
        out_specs=(P(), P("tensor", "section"), P("section", "tensor")),
        check_vma=False,
    )
```

```python
import functools

import jax
import jax.numpy as jnp
from jax import lax
from jax.experimental import pallas as pl
from jax.experimental.pallas import tpu as pltpu
from jax.sharding import PartitionSpec as P

tau = 2.0
f32 = jnp.float32
bf16 = jnp.bfloat16
i16 = jnp.int16

LEVELS = 32767.0
CODES = 128
LIMIT = 1000.0
STRIP = 512
PARAMS = pltpu.CompilerParams(vmem_limit_bytes=20 * 1024 * 1024)


def row_codes(ref):
    w = ref.shape[1] - CODES
    codes = ref[:, w:].astype(jnp.int32).astype(f32)
    middle = codes[:, 0:1] * 0.25
    scale = codes[:, 32:33] * (0.5 / LEVELS)
    return middle, scale, codes[:, 64:65]


def encode(x_ref, columns, o_ref, spent):
    lo, hi = columns
    top = bottom = None
    for at in range(lo, hi, STRIP):
        x = x_ref[:, at : at + STRIP]
        top = x if top is None else jnp.maximum(top, x)
        bottom = x if bottom is None else jnp.minimum(bottom, x)
    top = jnp.max(top, axis=1, keepdims=True)
    bottom = jnp.min(bottom, axis=1, keepdims=True)
    middle_code = jnp.round((top + bottom) * 2.0)
    middle = middle_code * 0.25
    reach = jnp.maximum(top - middle, middle - bottom)
    reach_code = jnp.floor(reach * 2.0) + 1.0
    spent_code = jnp.minimum(spent + reach_code, LEVELS)
    inverse = (2.0 * LEVELS) / reach_code
    for at in range(lo, hi, STRIP):
        code = jnp.round((x_ref[:, at : at + STRIP] - middle) * inverse)
        o_ref[:, at - lo : at - lo + STRIP] = code.astype(jnp.int32).astype(i16)
    lane = lax.broadcasted_iota(jnp.int32, (x_ref.shape[0], CODES), 1)
    codes = jnp.where(lane < 32, middle_code, jnp.where(lane < 64, reach_code, spent_code))
    o_ref[:, hi - lo :] = codes.astype(jnp.int32).astype(i16)


def first_kernel(part_ref, right_ref, left_ref):
    width = part_ref.shape[2]
    none = jnp.zeros((part_ref.shape[1], 1), f32)
    encode(part_ref.at[0], (0, width // 2), right_ref, none)
    encode(part_ref.at[0], (width // 2, width), left_ref, none)


def hop_kernel(r_ref, l_ref, pr_ref, pl_ref, ro_ref, lo_ref, sum_ref):
    width = pr_ref.shape[2]
    for in_ref, part_ref, out_ref, at_end in (
        (r_ref, pr_ref, ro_ref, False),
        (l_ref, pl_ref, lo_ref, True),
    ):
        carried = in_ref.shape[1] - CODES
        start = width - carried if at_end else 0
        middle, scale, spent = row_codes(in_ref)
        for at in range(0, width, STRIP):
            x = part_ref[0, :, at : at + STRIP]
            if start <= at < start + carried:
                code = in_ref[:, at - start : at - start + STRIP]
                x = x + (middle + code.astype(jnp.int32).astype(f32) * scale)
            sum_ref[:, at : at + STRIP] = x
        encode(sum_ref, (0, width), out_ref, spent)


def meet_kernel(
    rt_ref, lt_ref, pt_ref, rs_ref, ls_ref, ps_ref, target_ref, t_ref, s_ref, stats_ref
):
    rows, width = t_ref.shape
    tops, spents = [], []
    for r_ref, l_ref, part_ref, out_ref in (
        (rt_ref, lt_ref, pt_ref, t_ref),
        (rs_ref, ls_ref, ps_ref, s_ref),
    ):
        r_middle, r_scale, r_spent = row_codes(r_ref)
        l_middle, l_scale, l_spent = row_codes(l_ref)
        top = None
        for at in range(0, width, STRIP):
            strip = slice(at, at + STRIP)
            x = (
                part_ref[0, :, strip]
                + (r_middle + r_ref[:, strip].astype(jnp.int32).astype(f32) * r_scale)
                + (l_middle + l_ref[:, strip].astype(jnp.int32).astype(f32) * l_scale)
            )
            out_ref[:, strip] = x
            top = x if top is None else jnp.maximum(top, x)
        tops.append(jnp.max(top, axis=1, keepdims=True))
        spents.append((r_spent + l_spent) * 0.5)
    t_max, s_max = tops
    target = target_ref[:, 0:1]
    sums = None
    for at in range(0, width, 128):
        t, s = t_ref[:, at : at + 128], s_ref[:, at : at + 128]
        p = jnp.exp((t - t_max) * (1.0 / tau))
        q = jnp.exp((s - s_max) * (1.0 / tau))
        ids = at + lax.broadcasted_iota(jnp.int32, t.shape, 1)
        terms = (p, q, q * q, p * (t - s), jnp.where(ids == target, s, 0.0))
        sums = terms if sums is None else [a + b for a, b in zip(sums, terms)]
    lane = lax.broadcasted_iota(jnp.int32, (rows, 128), 1)
    kinds = [t_max, s_max] + [jnp.sum(a, axis=1, keepdims=True) for a in sums]
    kinds.append(jnp.maximum(spents[0], spents[1]))
    table = jnp.zeros((rows, 128), f32)
    for k, value in enumerate(kinds):
        table = jnp.where(lane == k, value, table)
    table = jnp.concatenate([table, jnp.zeros((128 - rows, 128), f32)], axis=0)
    stats_ref[...] = table.T[0:8, :]


def grad_kernel(t_ref, s_ref, every_ref, target_ref, a_ref, b_ref):
    rows, width = t_ref.shape
    t_tops, s_tops = every_ref[:, 0, :], every_ref[:, 1, :]
    t_max = jnp.max(t_tops, axis=0, keepdims=True)
    s_max = jnp.max(s_tops, axis=0, keepdims=True)
    t_weight = jnp.exp((t_tops - t_max) * (1.0 / tau))
    q_weight = jnp.exp((s_tops - s_max) * (1.0 / tau))
    s_weight = jnp.exp(s_tops - s_max)

    def total(k, weight):
        return jnp.sum(every_ref[:, k, :] * weight, axis=0, keepdims=True)

    p_total, q_total = total(2, t_weight), total(3, q_weight)
    s_total, cross = total(4, s_weight), total(5, t_weight)
    picked = jnp.sum(every_ref[:, 6, :], axis=0, keepdims=True)
    spent = jnp.max(every_ref[:, 7, :], axis=0, keepdims=True)
    kl_rows = (
        cross / (tau * p_total)
        - (t_max - s_max) / tau
        - jnp.log(p_total)
        + jnp.log(q_total)
    )
    row_loss = tau * tau * kl_rows + s_max + jnp.log(s_total) - picked
    flag = jnp.where(spent > LIMIT, 1.0, 0.0)
    lines = [t_max, s_max, tau / p_total, tau / q_total, 1.0 / s_total, row_loss, flag]
    lines.append(jnp.zeros((128 - len(lines), 128), f32))
    table = jnp.concatenate(lines, axis=0).T[:rows]
    t_max, s_max, p_scale, q_scale, s_scale, row_loss, flag = (
        table[:, k : k + 1] for k in range(7)
    )
    target = target_ref[:, 0:1]
    for at in range(0, width, STRIP):
        t, s = t_ref[:, at : at + STRIP], s_ref[:, at : at + STRIP]
        p = jnp.exp((t - t_max) * (1.0 / tau))
        q = jnp.exp((s - s_max) * (1.0 / tau))
        ids = at + lax.broadcasted_iota(jnp.int32, t.shape, 1)
        grad = q * q_scale - p * p_scale + (q * q) * s_scale
        grad = grad - jnp.where(ids == target, 1.0, 0.0)
        o_ref, to = (a_ref, at) if at < width // 2 else (b_ref, at - width // 2)
        o_ref[:, to : to + STRIP] = grad.astype(bf16)
    high = row_loss.astype(bf16).astype(f32)
    mid = (row_loss - high).astype(bf16).astype(f32)
    low = row_loss - high - mid
    lane = lax.broadcasted_iota(jnp.int32, (rows, CODES), 1)
    extra = jnp.where(
        lane == 0,
        high,
        jnp.where(lane == 1, mid, jnp.where(lane == 2, low, jnp.where(lane == 3, flag, 0.0))),
    )
    b_ref[:, width // 2 :] = extra.astype(bf16)


def whole(x):
    return pl.BlockSpec(x.shape, lambda i: (0,) * len(x.shape))


def part_at(part, j):
    return pl.BlockSpec((1,) + part.shape[1:], lambda i: (j, 0, 0))


def first(part, j):
    rows, width = part.shape[1:]
    out = jax.ShapeDtypeStruct((rows, width // 2 + CODES), i16)
    return pl.pallas_call(
        first_kernel,
        out_shape=(out, out),
        in_specs=[part_at(part, j)],
        out_specs=(whole(out), whole(out)),
        grid=(1,),
        compiler_params=PARAMS,
        name="first",
    )(part)


def hop(right, left, part, jr, jl):
    rows, width = part.shape[1:]
    out = jax.ShapeDtypeStruct((rows, width + CODES), i16)
    return pl.pallas_call(
        hop_kernel,
        out_shape=(out, out),
        in_specs=[whole(right), whole(left), part_at(part, jr), part_at(part, jl)],
        out_specs=(whole(out), whole(out)),
        scratch_shapes=[pltpu.VMEM((rows, width), f32)],
        grid=(1,),
        compiler_params=PARAMS,
        name="hop",
    )(right, left, part, part)


def meet(teacher, student, target):
    (rt, lt, pt), (rs, ls, ps) = teacher, student
    rows, width = pt.shape[1:]
    logits = jax.ShapeDtypeStruct((rows, width), f32)
    stats = jax.ShapeDtypeStruct((8, 128), f32)
    return pl.pallas_call(
        meet_kernel,
        out_shape=(logits, logits, stats),
        in_specs=[
            whole(rt), whole(lt), part_at(pt, 0), whole(rs), whole(ls), part_at(ps, 0),
            whole(target),
        ],
        out_specs=(whole(logits), whole(logits), whole(stats)),
        grid=(1,),
        compiler_params=PARAMS,
        name="meet",
    )(rt, lt, pt, rs, ls, ps, target)


def payload(teacher_logits, student_logits, every, target):
    rows, width = teacher_logits.shape
    out = (
        jax.ShapeDtypeStruct((rows, width // 2), bf16),
        jax.ShapeDtypeStruct((rows, width // 2 + CODES), bf16),
    )
    return pl.pallas_call(
        grad_kernel,
        out_shape=out,
        in_specs=[whole(x) for x in (teacher_logits, student_logits, every, target)],
        out_specs=tuple(whole(x) for x in out),
        grid=(1,),
        compiler_params=PARAMS,
        name="payload",
    )(teacher_logits, student_logits, every, target)


def product_kernel(own_ref, sib_ref, head_ref, head_sib_ref, o_ref):
    x = jnp.dot(own_ref[...], head_ref[...], preferred_element_type=f32)
    x = x + jnp.dot(sib_ref[...], head_sib_ref[...], preferred_element_type=f32)
    o_ref[...] = x.reshape(o_ref.shape)


def product(own, sib, head, head_sib, blocks):
    tokens, depth = own.shape
    width = head.shape[1]
    rows = tokens // blocks
    strip = pl.BlockSpec((depth, STRIP), lambda i: (0, i))
    return pl.pallas_call(
        product_kernel,
        out_shape=jax.ShapeDtypeStruct((blocks, rows, width), f32),
        in_specs=[whole(own), whole(sib), strip, strip],
        out_specs=pl.BlockSpec((blocks, rows, STRIP), lambda i: (0, 0, i)),
        grid=(width // STRIP,),
        compiler_params=PARAMS,
        cost_estimate=pl.CostEstimate(
            flops=4 * tokens * depth * width,
            bytes_accessed=4 * depth * width + 4 * tokens * width,
            transcendentals=0,
        ),
        name="product",
    )(own, sib, head, head_sib)


def back_kernel(order, place_ref, head_a_ref, head_b_ref, *refs):
    *groups, o_ref = refs
    z, core = place_ref[0], place_ref[1]
    chips, rows = o_ref.shape[0] // 2, o_ref.shape[1]
    depth = head_a_ref.shape[0]
    for k, (a_ref, b_ref) in enumerate(zip(groups[0::2], groups[1::2])):
        x = jnp.dot(a_ref[...], head_a_ref[...], preferred_element_type=f32)
        x = x + jnp.dot(b_ref[:, :depth], head_b_ref[...], preferred_element_type=f32)
        which = core if k % 2 == 0 else 1 - core
        for i, j in enumerate(order[k // 2]):
            at = 2 * lax.rem(z + j, chips) + which
            o_ref[pl.ds(at, 1)] = x[i * rows : (i + 1) * rows][None]


def back(order, place, head_t, groups, rows):
    depth, width = head_t.shape
    half = pl.BlockSpec((depth // 2, width), lambda i: (0, 0))
    rest = pl.BlockSpec((depth // 2, width), lambda i: (1, 0))
    out = jax.ShapeDtypeStruct((2 * sum(len(x) for x in order), rows, width), f32)
    arrays = [x for group in groups for x in group]
    return pl.pallas_call(
        functools.partial(back_kernel, order),
        out_shape=out,
        in_specs=[pl.BlockSpec(memory_space=pltpu.SMEM), half, rest]
        + [whole(x) for x in arrays],
        out_specs=whole(out),
        grid=(1,),
        compiler_params=PARAMS,
        name="back",
    )(place, head_t, head_t, *arrays)


def outer_kernel(n, *refs):
    hidden, arrays, o_ref = refs[:n], refs[n:-1], refs[-1]
    half = o_ref.shape[1] // 2
    for side in range(2):
        for at in range(0, half, STRIP):
            total = sum(
                jnp.dot(
                    hidden[k][...],
                    arrays[2 * k + side][:, at : at + STRIP],
                    preferred_element_type=f32,
                )
                for k in range(n)
            )
            to = side * half + at
            o_ref[:, to : to + STRIP] = total.astype(bf16)


def outer(hidden, groups):
    out = jax.ShapeDtypeStruct((hidden[0].shape[0], 2 * groups[0][0].shape[1]), bf16)
    arrays = list(hidden) + [x for group in groups for x in group]
    return pl.pallas_call(
        functools.partial(outer_kernel, len(hidden)),
        out_shape=out,
        in_specs=[whole(x) for x in arrays],
        out_specs=whole(out),
        grid=(1,),
        compiler_params=PARAMS,
        cost_estimate=pl.CostEstimate(
            flops=2 * out.shape[0] * out.shape[1] * sum(x.shape[1] for x in hidden),
            bytes_accessed=sum(2 * x.size for x in arrays) + 2 * out.size,
            transcendentals=0,
        ),
        name="outer",
    )(*arrays)


def shards(teacher_hidden, student_hidden, teacher_head, student_head, targets):
    tensor_size = lax.axis_size("tensor")
    section_size = lax.axis_size("section")
    chips = section_size // 2
    half_way = chips // 2
    me = lax.axis_index("section")
    z, core = me // 2, me % 2
    tok_block, dt = teacher_hidden.shape
    ds = student_hidden.shape[1]
    voc_local = teacher_head.shape[1]
    half = voc_local // 2

    def along(x, step):
        perm = [
            (s, ((s // 2 + step) % chips) * 2 + s % 2) for s in range(section_size)
        ]
        return lax.ppermute(x, "section", perm)

    def swap(x):
        return lax.ppermute(x, "section", [(s, s ^ 1) for s in range(section_size)])

    def spread(x, axis):
        n = lax.axis_size(axis)
        return lax.all_to_all(
            jnp.broadcast_to(x[None], (n,) + x.shape), axis, 0, 0
        )

    student_head_sib = swap(student_head)
    teacher_head_sib = swap(teacher_head)
    hidden = spread(jnp.concatenate([teacher_hidden, student_hidden], axis=1), "tensor")

    def rolled(x, which):
        pair = x.reshape((chips, 2) + x.shape[1:])
        twice = jnp.concatenate([pair, pair], axis=0)
        out = lax.dynamic_slice(
            twice, (z, which, 0, 0), (chips, 1) + x.shape[1:]
        )
        return out.reshape((chips * x.shape[1],) + x.shape[2:])

    mine, others = rolled(hidden, core), rolled(hidden, 1 - core)
    mine_sib = swap(others)
    student_part = product(
        mine[:, dt:], mine_sib[:, dt:], student_head, student_head_sib, chips
    )
    teacher_part = product(
        mine[:, :dt], mine_sib[:, :dt], teacher_head, teacher_head_sib, chips
    )

    near = [0] + [j for k in range(1, half_way - 1) for j in (chips - k, k)]
    far = [chips - half_way + 1, half_way - 1, half_way]
    place = jnp.stack([z, core]).astype(jnp.int32)
    head_t = student_head.T
    hidden_t = [
        jnp.concatenate(
            [x[j * tok_block : (j + 1) * tok_block, dt:] for j in order], axis=0
        ).T
        for order in (near, far)
        for x in (mine, others)
    ]

    def ring(part, meanwhile):
        right, left = first(part, half_way)
        right, left = along(right, 1), along(left, -1)
        for step in range(1, half_way):
            right, left = hop(right, left, part, half_way - step, half_way + step)
            if step == 2:
                right, left, meanwhile = lax.optimization_barrier((right, left, meanwhile))
            right, left = along(right, 1), along(left, -1)
        return (right, left, part), meanwhile

    def ring_wide(part):
        right = along(part[half_way][:, :half], 1)
        left = along(part[half_way][:, half:], -1)
        for step in range(1, half_way):
            mine_r, mine_l = part[half_way - step], part[half_way + step]
            if step == 1:
                right = jnp.concatenate([right + mine_r[:, :half], mine_r[:, half:]], 1)
                left = jnp.concatenate([mine_l[:, :half], left + mine_l[:, half:]], 1)
            else:
                right = right + mine_r
                left = left + mine_l
            right, left = along(right, 1), along(left, -1)
        return part[0] + right + left

    offset = lax.axis_index("tensor") * voc_local
    target_here = jnp.broadcast_to((targets - offset)[:, None], (tok_block, 128))

    def statistics(teacher_logits, student_logits):
        column_ids = lax.broadcasted_iota(jnp.int32, (tok_block, voc_local), 1)
        onehot = (column_ids == target_here[:, :1]).astype(f32)
        t_max = jnp.max(teacher_logits, axis=1)
        s_max = jnp.max(student_logits, axis=1)
        p_terms = jnp.exp((teacher_logits - t_max[:, None]) / tau)
        q_terms = jnp.exp((student_logits - s_max[:, None]) / tau)
        s_terms = jnp.exp(student_logits - s_max[:, None])
        stats = jnp.stack(
            [
                t_max,
                s_max,
                jnp.sum(p_terms, axis=1),
                jnp.sum(q_terms, axis=1),
                jnp.sum(s_terms, axis=1),
                jnp.sum(p_terms * (teacher_logits - student_logits), axis=1),
                jnp.sum(onehot * student_logits, axis=1),
                jnp.zeros_like(t_max),
            ]
        )
        return jnp.pad(stats, ((0, 0), (0, 128 - tok_block)))

    def gradients(teacher_logits, student_logits, stats):
        own = payload(teacher_logits, student_logits, spread(stats, "tensor"), target_here)

        pieces = [[None] * chips, [None] * chips]
        right, left = list(own), list(own)
        pieces[0][0], pieces[1][0] = own
        for step in range(1, half_way):
            for side in range(2):
                right[side] = along(right[side], 1)
                left[side] = along(left[side], -1)
                pieces[side][chips - step], pieces[side][step] = right[side], left[side]
        pieces[0][half_way] = along(right[0], 1)
        pieces[1][half_way] = along(left[1], -1)

        groups = []
        for order in (near, far):
            group = [jnp.concatenate([x[j] for j in order], axis=0) for x in pieces]
            groups += [group, [swap(x) for x in group]]

        rows = back((near, far), place, head_t, groups, tok_block)
        extra = sum(
            jnp.sum(g[1][:, half:].astype(f32), axis=0) for g in groups
        )
        loss = (extra[0] + extra[1] + extra[2]) / (tok_block * section_size)
        grad_hidden = jnp.sum(lax.all_to_all(rows, "tensor", 0, 0), axis=0).astype(bf16)
        grad_head = outer(hidden_t, groups)
        return (loss, grad_hidden, grad_head), extra[3]

    student, hidden_t = ring(student_part, hidden_t)
    teacher, head_t = ring(teacher_part, head_t)
    teacher_logits, student_logits, stats = meet(teacher, student, target_here)
    fine, flags = gradients(teacher_logits, student_logits, stats)

    def wide():
        teacher, student = ring_wide(teacher_part), ring_wide(student_part)
        return gradients(teacher, student, statistics(teacher, student))[0]

    return lax.cond(flags > 0.0, wide, lambda: fine)


def solution(mesh):
    placed = (
        P("tensor", "section"),
        P("tensor", "section"),
        P("section", "tensor"),
        P("section", "tensor"),
        P("section"),
    )
    return jax.shard_map(
        shards,
        mesh=mesh,
        in_specs=placed,
        out_specs=(P(), P("tensor", "section"), P("section", "tensor")),
        check_vma=False,
    )
```

```python
import functools

import jax
import jax.numpy as jnp
from jax import lax
from jax.experimental import pallas as pl
from jax.experimental.pallas import tpu as pltpu
from jax.sharding import PartitionSpec as P

tau = 2.0
f32 = jnp.float32
bf16 = jnp.bfloat16
i16 = jnp.int16

LEVELS = 32767.0
CODES = 128
LIMIT = 1000.0
STRIP = 512
PARAMS = pltpu.CompilerParams(vmem_limit_bytes=20 * 1024 * 1024)


def row_codes(ref):
    w = ref.shape[1] - CODES
    codes = ref[:, w:].astype(jnp.int32).astype(f32)
    middle = codes[:, 0:1] * 0.25
    scale = codes[:, 32:33] * (0.5 / LEVELS)
    return middle, scale, codes[:, 64:65]


def encode(x_ref, columns, o_ref, spent):
    lo, hi = columns
    top = bottom = None
    for at in range(lo, hi, STRIP):
        x = x_ref[:, at : at + STRIP]
        top = x if top is None else jnp.maximum(top, x)
        bottom = x if bottom is None else jnp.minimum(bottom, x)
    top = jnp.max(top, axis=1, keepdims=True)
    bottom = jnp.min(bottom, axis=1, keepdims=True)
    middle_code = jnp.round((top + bottom) * 2.0)
    middle = middle_code * 0.25
    reach = jnp.maximum(top - middle, middle - bottom)
    reach_code = jnp.floor(reach * 2.0) + 1.0
    spent_code = jnp.minimum(spent + reach_code, LEVELS)
    inverse = (2.0 * LEVELS) / reach_code
    for at in range(lo, hi, STRIP):
        code = jnp.round((x_ref[:, at : at + STRIP] - middle) * inverse)
        o_ref[:, at - lo : at - lo + STRIP] = code.astype(jnp.int32).astype(i16)
    lane = lax.broadcasted_iota(jnp.int32, (x_ref.shape[0], CODES), 1)
    codes = jnp.where(lane < 32, middle_code, jnp.where(lane < 64, reach_code, spent_code))
    o_ref[:, hi - lo :] = codes.astype(jnp.int32).astype(i16)


def first_kernel(j, part_ref, right_ref, left_ref):
    width = part_ref.shape[2]
    none = jnp.zeros((part_ref.shape[1], 1), f32)
    encode(part_ref.at[j], (0, width // 2), right_ref, none)
    encode(part_ref.at[j], (width // 2, width), left_ref, none)


def hop_kernel(jr, jl, r_ref, l_ref, part_ref, ro_ref, lo_ref, sum_ref):
    width = part_ref.shape[2]
    for in_ref, j, out_ref, at_end in (
        (r_ref, jr, ro_ref, False),
        (l_ref, jl, lo_ref, True),
    ):
        carried = in_ref.shape[1] - CODES
        start = width - carried if at_end else 0
        middle, scale, spent = row_codes(in_ref)
        for at in range(0, width, STRIP):
            x = part_ref[j, :, at : at + STRIP]
            if start <= at < start + carried:
                code = in_ref[:, at - start : at - start + STRIP]
                x = x + (middle + code.astype(jnp.int32).astype(f32) * scale)
            sum_ref[:, at : at + STRIP] = x
        encode(sum_ref, (0, width), out_ref, spent)


def meet_kernel(
    rt_ref, lt_ref, pt_ref, rs_ref, ls_ref, ps_ref, target_ref, t_ref, s_ref, stats_ref
):
    rows, width = t_ref.shape
    tops, spents = [], []
    for r_ref, l_ref, part_ref, out_ref in (
        (rt_ref, lt_ref, pt_ref, t_ref),
        (rs_ref, ls_ref, ps_ref, s_ref),
    ):
        r_middle, r_scale, r_spent = row_codes(r_ref)
        l_middle, l_scale, l_spent = row_codes(l_ref)
        top = None
        for at in range(0, width, STRIP):
            strip = slice(at, at + STRIP)
            x = (
                part_ref[0, :, strip]
                + (r_middle + r_ref[:, strip].astype(jnp.int32).astype(f32) * r_scale)
                + (l_middle + l_ref[:, strip].astype(jnp.int32).astype(f32) * l_scale)
            )
            out_ref[:, strip] = x
            top = x if top is None else jnp.maximum(top, x)
        tops.append(jnp.max(top, axis=1, keepdims=True))
        spents.append((r_spent + l_spent) * 0.5)
    t_max, s_max = tops
    target = target_ref[:, 0:1]
    sums = None
    for at in range(0, width, 128):
        t, s = t_ref[:, at : at + 128], s_ref[:, at : at + 128]
        p = jnp.exp((t - t_max) * (1.0 / tau))
        q = jnp.exp((s - s_max) * (1.0 / tau))
        ids = at + lax.broadcasted_iota(jnp.int32, t.shape, 1)
        terms = (p, q, q * q, p * (t - s), jnp.where(ids == target, s, 0.0))
        sums = terms if sums is None else [a + b for a, b in zip(sums, terms)]
    lane = lax.broadcasted_iota(jnp.int32, (rows, 128), 1)
    kinds = [t_max, s_max] + [jnp.sum(a, axis=1, keepdims=True) for a in sums]
    kinds.append(jnp.maximum(spents[0], spents[1]))
    table = jnp.zeros((rows, 128), f32)
    for k, value in enumerate(kinds):
        table = jnp.where(lane == k, value, table)
    table = jnp.concatenate([table, jnp.zeros((128 - rows, 128), f32)], axis=0)
    stats_ref[...] = table.T[0:8, :]


def grad_kernel(t_ref, s_ref, every_ref, target_ref, a_ref, b_ref):
    rows, width = t_ref.shape
    t_tops, s_tops = every_ref[:, 0, :], every_ref[:, 1, :]
    t_max = jnp.max(t_tops, axis=0, keepdims=True)
    s_max = jnp.max(s_tops, axis=0, keepdims=True)
    t_weight = jnp.exp((t_tops - t_max) * (1.0 / tau))
    q_weight = jnp.exp((s_tops - s_max) * (1.0 / tau))
    s_weight = jnp.exp(s_tops - s_max)

    def total(k, weight):
        return jnp.sum(every_ref[:, k, :] * weight, axis=0, keepdims=True)

    p_total, q_total = total(2, t_weight), total(3, q_weight)
    s_total, cross = total(4, s_weight), total(5, t_weight)
    picked = jnp.sum(every_ref[:, 6, :], axis=0, keepdims=True)
    spent = jnp.max(every_ref[:, 7, :], axis=0, keepdims=True)
    kl_rows = (
        cross / (tau * p_total)
        - (t_max - s_max) / tau
        - jnp.log(p_total)
        + jnp.log(q_total)
    )
    row_loss = tau * tau * kl_rows + s_max + jnp.log(s_total) - picked
    flag = jnp.where(spent > LIMIT, 1.0, 0.0)
    lines = [t_max, s_max, tau / p_total, tau / q_total, 1.0 / s_total, row_loss, flag]
    lines.append(jnp.zeros((128 - len(lines), 128), f32))
    table = jnp.concatenate(lines, axis=0).T[:rows]
    t_max, s_max, p_scale, q_scale, s_scale, row_loss, flag = (
        table[:, k : k + 1] for k in range(7)
    )
    target = target_ref[:, 0:1]
    for at in range(0, width, STRIP):
        t, s = t_ref[:, at : at + STRIP], s_ref[:, at : at + STRIP]
        p = jnp.exp((t - t_max) * (1.0 / tau))
        q = jnp.exp((s - s_max) * (1.0 / tau))
        ids = at + lax.broadcasted_iota(jnp.int32, t.shape, 1)
        grad = q * q_scale - p * p_scale + (q * q) * s_scale
        grad = grad - jnp.where(ids == target, 1.0, 0.0)
        o_ref, to = (a_ref, at) if at < width // 2 else (b_ref, at - width // 2)
        o_ref[:, to : to + STRIP] = grad.astype(bf16)
    high = row_loss.astype(bf16).astype(f32)
    mid = (row_loss - high).astype(bf16).astype(f32)
    low = row_loss - high - mid
    lane = lax.broadcasted_iota(jnp.int32, (rows, CODES), 1)
    extra = jnp.where(
        lane == 0,
        high,
        jnp.where(lane == 1, mid, jnp.where(lane == 2, low, jnp.where(lane == 3, flag, 0.0))),
    )
    b_ref[:, width // 2 :] = extra.astype(bf16)


VMEM = pl.BlockSpec(memory_space=pltpu.VMEM)


def call(kernel, name, out, *operands, flops=0, **more):
    leaves = jax.tree.leaves((out, operands))
    return pl.pallas_call(
        kernel,
        out_shape=out,
        in_specs=[VMEM] * len(operands),
        out_specs=jax.tree.map(lambda _: VMEM, out),
        compiler_params=PARAMS,
        cost_estimate=pl.CostEstimate(
            flops=flops,
            bytes_accessed=sum(x.size * x.dtype.itemsize for x in leaves),
            transcendentals=0,
        ),
        name=name,
        **more,
    )(*operands)


def first(part, j):
    rows, width = part.shape[1:]
    out = jax.ShapeDtypeStruct((rows, width // 2 + CODES), i16)
    return call(functools.partial(first_kernel, j), "first", (out, out), part)


def hop(right, left, part, jr, jl):
    rows, width = part.shape[1:]
    out = jax.ShapeDtypeStruct((rows, width + CODES), i16)
    return call(
        functools.partial(hop_kernel, jr, jl),
        "hop",
        (out, out),
        right,
        left,
        part,
        scratch_shapes=[pltpu.VMEM((rows, width), f32)],
    )


def meet(teacher, student, target):
    rows, width = teacher[2].shape[1:]
    logits = jax.ShapeDtypeStruct((rows, width), f32)
    stats = jax.ShapeDtypeStruct((8, 128), f32)
    return call(meet_kernel, "meet", (logits, logits, stats), *teacher, *student, target)


def payload(teacher_logits, student_logits, every, target):
    rows, width = teacher_logits.shape
    out = (
        jax.ShapeDtypeStruct((rows, width // 2), bf16),
        jax.ShapeDtypeStruct((rows, width // 2 + CODES), bf16),
    )
    return call(
        grad_kernel, "payload", out, teacher_logits, student_logits, every, target
    )


def product_kernel(own_ref, sib_ref, head_ref, head_sib_ref, o_ref):
    width = o_ref.shape[2]
    step = min(width, 2 * STRIP)
    for at in range(0, width, step):
        strip = slice(at, at + step)
        x = jnp.dot(own_ref[...], head_ref[:, strip], preferred_element_type=f32)
        x = x + jnp.dot(sib_ref[...], head_sib_ref[:, strip], preferred_element_type=f32)
        o_ref[:, :, strip] = x.reshape(o_ref.shape[:2] + (step,))


def product(own, sib, head, head_sib, blocks):
    tokens, depth = own.shape
    width = head.shape[1]
    out = jax.ShapeDtypeStruct((blocks, tokens // blocks, width), f32)
    return call(
        product_kernel, "product", out, own, sib, head, head_sib,
        flops=4 * tokens * depth * width,
    )


def back_kernel(order, place_ref, head_ref, *refs):
    *groups, o_ref = refs
    z, core = place_ref[0], place_ref[1]
    chips, rows = o_ref.shape[0] // 2, o_ref.shape[1]
    depth = head_ref.shape[0] // 2
    for k, (a_ref, b_ref) in enumerate(zip(groups[0::2], groups[1::2])):
        x = jnp.dot(a_ref[...], head_ref[:depth], preferred_element_type=f32)
        x = x + jnp.dot(b_ref[:, :depth], head_ref[depth:], preferred_element_type=f32)
        which = core if k % 2 == 0 else 1 - core
        for i, j in enumerate(order[k // 2]):
            at = 2 * lax.rem(z + j, chips) + which
            o_ref[pl.ds(at, 1)] = x[i * rows : (i + 1) * rows][None]


def back(order, place, head_t, groups, rows):
    out = jax.ShapeDtypeStruct(
        (2 * sum(len(x) for x in order), rows, head_t.shape[1]), f32
    )
    arrays = [x for group in groups for x in group]
    return pl.pallas_call(
        functools.partial(back_kernel, order),
        out_shape=out,
        in_specs=[pl.BlockSpec(memory_space=pltpu.SMEM)] + [VMEM] * (1 + len(arrays)),
        out_specs=VMEM,
        compiler_params=PARAMS,
        name="back",
    )(place, head_t, *arrays)


def outer_kernel(n, *refs):
    hidden, arrays, o_ref = refs[:n], refs[n:-1], refs[-1]
    half = o_ref.shape[1] // 2
    for side in range(2):
        for at in range(0, half, STRIP):
            total = sum(
                jnp.dot(
                    hidden[k][...],
                    arrays[2 * k + side][:, at : at + STRIP],
                    preferred_element_type=f32,
                )
                for k in range(n)
            )
            to = side * half + at
            o_ref[:, to : to + STRIP] = total.astype(bf16)


def outer(hidden, groups):
    out = jax.ShapeDtypeStruct((hidden[0].shape[0], 2 * groups[0][0].shape[1]), bf16)
    arrays = [x for group in groups for x in group]
    return call(
        functools.partial(outer_kernel, len(hidden)), "outer", out, *hidden, *arrays,
        flops=2 * out.size * sum(x.shape[1] for x in hidden),
    )


def steps(wide, teacher_hidden, student_hidden, teacher_head, student_head, targets):
    tensor_size = lax.axis_size("tensor")
    section_size = lax.axis_size("section")
    chips = section_size // 2
    half_way = chips // 2
    me = lax.axis_index("section")
    z, core = me // 2, me % 2
    tok_block, dt = teacher_hidden.shape
    ds = student_hidden.shape[1]
    voc_local = teacher_head.shape[1]
    half = voc_local // 2

    def along(x, step):
        perm = [
            (s, ((s // 2 + step) % chips) * 2 + s % 2) for s in range(section_size)
        ]
        return lax.ppermute(x, "section", perm)

    def swap(x):
        return lax.ppermute(x, "section", [(s, s ^ 1) for s in range(section_size)])

    def spread(x, axis):
        n = lax.axis_size(axis)
        return lax.all_to_all(
            jnp.broadcast_to(x[None], (n,) + x.shape), axis, 0, 0
        )

    student_head_sib = swap(student_head)
    teacher_head_sib = swap(teacher_head)
    hidden = spread(jnp.concatenate([teacher_hidden, student_hidden], axis=1), "tensor")

    def rolled(x, which):
        pair = x.reshape((chips, 2) + x.shape[1:])
        twice = jnp.concatenate([pair, pair], axis=0)
        out = lax.dynamic_slice(
            twice, (z, which, 0, 0), (chips, 1) + x.shape[1:]
        )
        return out.reshape((chips * x.shape[1],) + x.shape[2:])

    mine, others = rolled(hidden, core), rolled(hidden, 1 - core)
    mine_sib = swap(others)
    student_part = product(
        mine[:, dt:], mine_sib[:, dt:], student_head, student_head_sib, chips
    )
    teacher_part = product(
        mine[:, :dt], mine_sib[:, :dt], teacher_head, teacher_head_sib, chips
    )

    near = [0] + [j for k in range(1, half_way - 1) for j in (chips - k, k)]
    far = [chips - half_way + 1, half_way - 1, half_way]
    place = jnp.stack([z, core]).astype(jnp.int32)
    head_t = student_head.T
    hidden_t = [
        jnp.concatenate(
            [x[j * tok_block : (j + 1) * tok_block, dt:] for j in order], axis=0
        ).T
        for order in (near, far)
        for x in (mine, others)
    ]

    def ring(part, meanwhile):
        right, left = first(part, half_way)
        right, left = along(right, 1), along(left, -1)
        for step in range(1, half_way):
            right, left = hop(right, left, part, half_way - step, half_way + step)
            if step == 2:
                right, left, meanwhile = lax.optimization_barrier((right, left, meanwhile))
            right, left = along(right, 1), along(left, -1)
        return (right, left, part), meanwhile

    def ring_wide(part):
        right = along(part[half_way][:, :half], 1)
        left = along(part[half_way][:, half:], -1)
        for step in range(1, half_way):
            mine_r, mine_l = part[half_way - step], part[half_way + step]
            if step == 1:
                right = jnp.concatenate([right + mine_r[:, :half], mine_r[:, half:]], 1)
                left = jnp.concatenate([mine_l[:, :half], left + mine_l[:, half:]], 1)
            else:
                right = right + mine_r
                left = left + mine_l
            right, left = along(right, 1), along(left, -1)
        return part[0] + right + left

    offset = lax.axis_index("tensor") * voc_local
    target_here = jnp.broadcast_to((targets - offset)[:, None], (tok_block, 128))

    def statistics(teacher_logits, student_logits):
        column_ids = lax.broadcasted_iota(jnp.int32, (tok_block, voc_local), 1)
        onehot = (column_ids == target_here[:, :1]).astype(f32)
        t_max = jnp.max(teacher_logits, axis=1)
        s_max = jnp.max(student_logits, axis=1)
        p_terms = jnp.exp((teacher_logits - t_max[:, None]) / tau)
        q_terms = jnp.exp((student_logits - s_max[:, None]) / tau)
        s_terms = jnp.exp(student_logits - s_max[:, None])
        stats = jnp.stack(
            [
                t_max,
                s_max,
                jnp.sum(p_terms, axis=1),
                jnp.sum(q_terms, axis=1),
                jnp.sum(s_terms, axis=1),
                jnp.sum(p_terms * (teacher_logits - student_logits), axis=1),
                jnp.sum(onehot * student_logits, axis=1),
                jnp.zeros_like(t_max),
            ]
        )
        return jnp.pad(stats, ((0, 0), (0, 128 - tok_block)))

    def gradients(teacher_logits, student_logits, stats):
        own = payload(teacher_logits, student_logits, spread(stats, "tensor"), target_here)

        pieces = [[None] * chips, [None] * chips]
        right, left = list(own), list(own)
        pieces[0][0], pieces[1][0] = own
        for step in range(1, half_way):
            for side in range(2):
                right[side] = along(right[side], 1)
                left[side] = along(left[side], -1)
                pieces[side][chips - step], pieces[side][step] = right[side], left[side]
        pieces[0][half_way] = along(right[0], 1)
        pieces[1][half_way] = along(left[1], -1)

        groups = []
        for order in (near, far):
            group = [jnp.concatenate([x[j] for j in order], axis=0) for x in pieces]
            groups += [group, [swap(x) for x in group]]

        rows = back((near, far), place, head_t, groups, tok_block)
        extra = sum(
            jnp.sum(g[1][:, half:].astype(f32), axis=0) for g in groups
        )
        loss = (extra[0] + extra[1] + extra[2]) / (tok_block * section_size)
        grad_hidden = jnp.sum(lax.all_to_all(rows, "tensor", 0, 0), axis=0).astype(bf16)
        grad_head = outer(hidden_t, groups)
        return (loss, grad_hidden, grad_head), extra[3]

    if wide:
        teacher_logits, student_logits = ring_wide(teacher_part), ring_wide(student_part)
        stats = statistics(teacher_logits, student_logits)
    else:
        student, hidden_t = ring(student_part, hidden_t)
        teacher, head_t = ring(teacher_part, head_t)
        teacher_logits, student_logits, stats = meet(teacher, student, target_here)
    return gradients(teacher_logits, student_logits, stats)


def shards(*arrays):
    fine, too_coarse = steps(False, *arrays)
    return lax.cond(too_coarse > 0.0, lambda: steps(True, *arrays)[0], lambda: fine)


def solution(mesh):
    placed = (
        P("tensor", "section"),
        P("tensor", "section"),
        P("section", "tensor"),
        P("section", "tensor"),
        P("section"),
    )
    return jax.shard_map(
        shards,
        mesh=mesh,
        in_specs=placed,
        out_specs=(P(), P("tensor", "section"), P("section", "tensor")),
        check_vma=False,
    )
```

```python
import functools

import jax
import jax.numpy as jnp
from jax import lax
from jax.experimental import pallas as pl
from jax.experimental.pallas import tpu as pltpu
from jax.sharding import PartitionSpec as P

tau = 2.0
f32 = jnp.float32
bf16 = jnp.bfloat16
i16 = jnp.int16

LEVELS = 32767.0
CODES = 128
LIMIT = 1000.0
STRIP = 512
PARAMS = pltpu.CompilerParams(vmem_limit_bytes=20 * 1024 * 1024)


def row_codes(ref):
    w = ref.shape[1] - CODES
    codes = ref[:, w:].astype(jnp.int32).astype(f32)
    middle = codes[:, 0:1] * 0.25
    scale = codes[:, 32:33] * (0.5 / LEVELS)
    return middle, scale, codes[:, 64:65]


def encode(x_ref, columns, o_ref, spent):
    lo, hi = columns
    top = bottom = None
    for at in range(lo, hi, STRIP):
        x = x_ref[:, at : at + STRIP]
        top = x if top is None else jnp.maximum(top, x)
        bottom = x if bottom is None else jnp.minimum(bottom, x)
    top = jnp.max(top, axis=1, keepdims=True)
    bottom = jnp.min(bottom, axis=1, keepdims=True)
    middle_code = jnp.round((top + bottom) * 2.0)
    middle = middle_code * 0.25
    reach = jnp.maximum(top - middle, middle - bottom)
    reach_code = jnp.floor(reach * 2.0) + 1.0
    spent_code = jnp.minimum(spent + reach_code, LEVELS)
    inverse = (2.0 * LEVELS) / reach_code
    for at in range(lo, hi, STRIP):
        code = jnp.round((x_ref[:, at : at + STRIP] - middle) * inverse)
        o_ref[:, at - lo : at - lo + STRIP] = code.astype(jnp.int32).astype(i16)
    lane = lax.broadcasted_iota(jnp.int32, (x_ref.shape[0], CODES), 1)
    codes = jnp.where(lane < 32, middle_code, jnp.where(lane < 64, reach_code, spent_code))
    o_ref[:, hi - lo :] = codes.astype(jnp.int32).astype(i16)


def first_kernel(part_ref, right_ref, left_ref):
    rows, width = part_ref.shape
    none = jnp.zeros((rows, 1), f32)
    encode(part_ref, (0, width // 2), right_ref, none)
    encode(part_ref, (width // 2, width), left_ref, none)


def hop_kernel(r_ref, l_ref, pr_ref, pl_ref, ro_ref, lo_ref, sum_ref):
    width = pr_ref.shape[1]
    for in_ref, part_ref, out_ref, at_end in (
        (r_ref, pr_ref, ro_ref, False),
        (l_ref, pl_ref, lo_ref, True),
    ):
        carried = in_ref.shape[1] - CODES
        start = width - carried if at_end else 0
        middle, scale, spent = row_codes(in_ref)
        for at in range(0, width, STRIP):
            x = part_ref[:, at : at + STRIP]
            if start <= at < start + carried:
                code = in_ref[:, at - start : at - start + STRIP]
                x = x + (middle + code.astype(jnp.int32).astype(f32) * scale)
            sum_ref[:, at : at + STRIP] = x
        encode(sum_ref, (0, width), out_ref, spent)


def meet_kernel(
    rt_ref, lt_ref, pt_ref, rs_ref, ls_ref, ps_ref, target_ref, t_ref, s_ref, stats_ref
):
    rows, width = t_ref.shape
    tops, spents = [], []
    for r_ref, l_ref, part_ref, out_ref in (
        (rt_ref, lt_ref, pt_ref, t_ref),
        (rs_ref, ls_ref, ps_ref, s_ref),
    ):
        r_middle, r_scale, r_spent = row_codes(r_ref)
        l_middle, l_scale, l_spent = row_codes(l_ref)
        top = None
        for at in range(0, width, STRIP):
            strip = slice(at, at + STRIP)
            x = (
                part_ref[:, strip]
                + (r_middle + r_ref[:, strip].astype(jnp.int32).astype(f32) * r_scale)
                + (l_middle + l_ref[:, strip].astype(jnp.int32).astype(f32) * l_scale)
            )
            out_ref[:, strip] = x
            top = x if top is None else jnp.maximum(top, x)
        tops.append(jnp.max(top, axis=1, keepdims=True))
        spents.append((r_spent + l_spent) * 0.5)
    t_max, s_max = tops
    target = target_ref[:, 0:1]
    sums = None
    for at in range(0, width, 128):
        t, s = t_ref[:, at : at + 128], s_ref[:, at : at + 128]
        p = jnp.exp((t - t_max) * (1.0 / tau))
        q = jnp.exp((s - s_max) * (1.0 / tau))
        ids = at + lax.broadcasted_iota(jnp.int32, t.shape, 1)
        terms = (p, q, q * q, p * (t - s), jnp.where(ids == target, s, 0.0))
        sums = terms if sums is None else [a + b for a, b in zip(sums, terms)]
    lane = lax.broadcasted_iota(jnp.int32, (rows, 128), 1)
    kinds = [t_max, s_max] + [jnp.sum(a, axis=1, keepdims=True) for a in sums]
    kinds.append(jnp.maximum(spents[0], spents[1]))
    table = jnp.zeros((rows, 128), f32)
    for k, value in enumerate(kinds):
        table = jnp.where(lane == k, value, table)
    table = jnp.concatenate([table, jnp.zeros((128 - rows, 128), f32)], axis=0)
    stats_ref[...] = table.T[0:8, :]


def grad_kernel(t_ref, s_ref, every_ref, target_ref, a_ref, b_ref):
    rows, width = t_ref.shape
    t_tops, s_tops = every_ref[:, 0, :], every_ref[:, 1, :]
    t_max = jnp.max(t_tops, axis=0, keepdims=True)
    s_max = jnp.max(s_tops, axis=0, keepdims=True)
    t_weight = jnp.exp((t_tops - t_max) * (1.0 / tau))
    q_weight = jnp.exp((s_tops - s_max) * (1.0 / tau))
    s_weight = jnp.exp(s_tops - s_max)

    def total(k, weight):
        return jnp.sum(every_ref[:, k, :] * weight, axis=0, keepdims=True)

    p_total, q_total = total(2, t_weight), total(3, q_weight)
    s_total, cross = total(4, s_weight), total(5, t_weight)
    picked = jnp.sum(every_ref[:, 6, :], axis=0, keepdims=True)
    spent = jnp.max(every_ref[:, 7, :], axis=0, keepdims=True)
    kl_rows = (
        cross / (tau * p_total)
        - (t_max - s_max) / tau
        - jnp.log(p_total)
        + jnp.log(q_total)
    )
    row_loss = tau * tau * kl_rows + s_max + jnp.log(s_total) - picked
    flag = jnp.where(spent > LIMIT, 1.0, 0.0)
    lines = [t_max, s_max, tau / p_total, tau / q_total, 1.0 / s_total, row_loss, flag]
    lines.append(jnp.zeros((128 - len(lines), 128), f32))
    table = jnp.concatenate(lines, axis=0).T[:rows]
    t_max, s_max, p_scale, q_scale, s_scale, row_loss, flag = (
        table[:, k : k + 1] for k in range(7)
    )
    target = target_ref[:, 0:1]
    for at in range(0, width, STRIP):
        t, s = t_ref[:, at : at + STRIP], s_ref[:, at : at + STRIP]
        p = jnp.exp((t - t_max) * (1.0 / tau))
        q = jnp.exp((s - s_max) * (1.0 / tau))
        ids = at + lax.broadcasted_iota(jnp.int32, t.shape, 1)
        grad = q * q_scale - p * p_scale + (q * q) * s_scale
        grad = grad - jnp.where(ids == target, 1.0, 0.0)
        o_ref, to = (a_ref, at) if at < width // 2 else (b_ref, at - width // 2)
        o_ref[:, to : to + STRIP] = grad.astype(bf16)
    high = row_loss.astype(bf16).astype(f32)
    mid = (row_loss - high).astype(bf16).astype(f32)
    low = row_loss - high - mid
    lane = lax.broadcasted_iota(jnp.int32, (rows, CODES), 1)
    extra = jnp.where(
        lane == 0,
        high,
        jnp.where(lane == 1, mid, jnp.where(lane == 2, low, jnp.where(lane == 3, flag, 0.0))),
    )
    b_ref[:, width // 2 :] = extra.astype(bf16)


VMEM = pl.BlockSpec(memory_space=pltpu.VMEM)


def call(kernel, name, out, *operands, flops=0, **more):
    leaves = jax.tree.leaves((out, operands))
    return pl.pallas_call(
        kernel,
        out_shape=out,
        in_specs=[VMEM] * len(operands),
        out_specs=jax.tree.map(lambda _: VMEM, out),
        compiler_params=PARAMS,
        cost_estimate=pl.CostEstimate(
            flops=flops,
            bytes_accessed=sum(x.size * x.dtype.itemsize for x in leaves),
            transcendentals=0,
        ),
        name=name,
        **more,
    )(*operands)


def first(part):
    rows, width = part.shape
    out = jax.ShapeDtypeStruct((rows, width // 2 + CODES), i16)
    return call(first_kernel, "first", (out, out), part)


def hop(right, left, part_right, part_left):
    rows, width = part_right.shape
    out = jax.ShapeDtypeStruct((rows, width + CODES), i16)
    return call(
        hop_kernel, "hop", (out, out), right, left, part_right, part_left,
        scratch_shapes=[pltpu.VMEM((rows, width), f32)],
    )


def meet(teacher, student, target):
    rows, width = teacher[2].shape
    logits = jax.ShapeDtypeStruct((rows, width), f32)
    stats = jax.ShapeDtypeStruct((8, 128), f32)
    return call(meet_kernel, "meet", (logits, logits, stats), *teacher, *student, target)


def payload(teacher_logits, student_logits, every, target):
    rows, width = teacher_logits.shape
    out = (
        jax.ShapeDtypeStruct((rows, width // 2), bf16),
        jax.ShapeDtypeStruct((rows, width // 2 + CODES), bf16),
    )
    return call(
        grad_kernel, "payload", out, teacher_logits, student_logits, every, target
    )


def product_kernel(own_ref, sib_ref, head_ref, head_sib_ref, *o_refs):
    rows, width = o_refs[0].shape
    step = min(width, 2 * STRIP)
    for at in range(0, width, step):
        strip = slice(at, at + step)
        x = jnp.dot(own_ref[...], head_ref[:, strip], preferred_element_type=f32)
        x = x + jnp.dot(sib_ref[...], head_sib_ref[:, strip], preferred_element_type=f32)
        for k, o_ref in enumerate(o_refs):
            o_ref[:, strip] = x[k * rows : (k + 1) * rows]


def product(own, sib, head, head_sib, blocks):
    tokens, depth = own.shape
    width = head.shape[1]
    out = jax.ShapeDtypeStruct((tokens // blocks, width), f32)
    return call(
        product_kernel, "product", (out,) * blocks, own, sib, head, head_sib,
        flops=4 * tokens * depth * width,
    )


def back(group, head_ref):
    depth = head_ref.shape[1] // 2
    turned = (((1,), (1,)), ((), ()))
    return lax.dot_general(
        group[0][...], head_ref[:, :depth], turned, preferred_element_type=f32
    ) + lax.dot_general(
        group[1][:, :depth], head_ref[:, depth:], turned, preferred_element_type=f32
    )


def outer(hidden, groups, store):
    half = groups[0][0].shape[1]
    for side in range(2):
        for at in range(0, half, STRIP):
            total = sum(
                lax.dot_general(
                    x[...],
                    group[side][:, at : at + STRIP],
                    (((0,), (0,)), ((), ())),
                    preferred_element_type=f32,
                )
                for x, group in zip(hidden, groups)
            )
            store(side * half + at, total)


def near_kernel(head_ref, h0, h1, a0, b0, a1, b1, rows0_ref, rows1_ref, acc_ref):
    rows0_ref[...] = back((a0, b0), head_ref)
    rows1_ref[...] = back((a1, b1), head_ref)

    def store(at, total):
        acc_ref[:, at : at + STRIP] = total

    outer((h0, h1), ((a0, b0), (a1, b1)), store)


def far_kernel(
    order, place_ref, head_ref, near0, near1, acc_ref, h0, h1, a0, b0, a1, b1,
    rows_ref, o_ref,
):
    z, core = place_ref[0], place_ref[1]
    blocks, rows = rows_ref.shape[:2]
    chips = blocks // 2
    for near, group, which in (
        (near0, (a0, b0), core), (near1, (a1, b1), 1 - core)
    ):
        far = back(group, head_ref)
        count = near.shape[0] // rows
        for i, j in enumerate(order):
            x = near[i * rows : (i + 1) * rows] if i < count else (
                far[(i - count) * rows : (i - count + 1) * rows]
            )
            at = 2 * lax.rem(z + j, chips) + which
            rows_ref[pl.ds(at, 1)] = x[None]

    def store(at, total):
        o_ref[:, at : at + STRIP] = (acc_ref[:, at : at + STRIP] + total).astype(bf16)

    outer((h0, h1), ((a0, b0), (a1, b1)), store)


def near_products(head, hidden, groups):
    depth, width = head.shape
    rows = jax.ShapeDtypeStruct((hidden[0].shape[0], depth), f32)
    acc = jax.ShapeDtypeStruct((depth, width), f32)
    return call(
        near_kernel, "near", (rows, rows, acc), head, *hidden, *groups[0], *groups[1],
        flops=8 * rows.size * width,
    )


def far_products(order, place, head, near, hidden, groups, rows):
    depth, width = head.shape
    blocks = 2 * len(order)
    return pl.pallas_call(
        functools.partial(far_kernel, order),
        out_shape=(
            jax.ShapeDtypeStruct((blocks, rows, depth), f32),
            jax.ShapeDtypeStruct((depth, width), bf16),
        ),
        in_specs=[pl.BlockSpec(memory_space=pltpu.SMEM)] + [VMEM] * 10,
        out_specs=(VMEM, VMEM),
        compiler_params=PARAMS,
        name="far",
    )(place, head, *near, *hidden, *groups[0], *groups[1])


def plain(teacher_hidden, student_hidden, teacher_head, student_head, targets):
    teacher_all, student_all = (
        lax.all_gather(teacher_hidden, "tensor", axis=0, tiled=True),
        lax.all_gather(student_hidden, "tensor", axis=0, tiled=True),
    )
    tok_block = targets.shape[0]
    voc_local = teacher_head.shape[1]
    rows = teacher_all
    teacher_logits = lax.psum_scatter(
        jnp.dot(rows, teacher_head, preferred_element_type=jnp.float32),
        "section",
        scatter_dimension=0,
        tiled=True,
    )
    rows = student_all
    student_logits = lax.psum_scatter(
        jnp.dot(rows, student_head, preferred_element_type=jnp.float32),
        "section",
        scatter_dimension=0,
        tiled=True,
    )
    teacher_max, student_max = lax.pmax(
        (jnp.max(teacher_logits, axis=1), jnp.max(student_logits, axis=1)), "tensor"
    )
    offset = lax.axis_index("tensor") * voc_local
    column_ids = offset + lax.broadcasted_iota(jnp.int32, (tok_block, voc_local), 1)
    onehot = (column_ids == targets[:, None]).astype(jnp.float32)
    p_terms = jnp.exp((teacher_logits - teacher_max[:, None]) / tau)
    q_terms = jnp.exp((student_logits - student_max[:, None]) / tau)
    s_terms = jnp.exp(student_logits - student_max[:, None])
    p_total, q_total, s_total, cross, picked = lax.psum(
        (
            jnp.sum(p_terms, axis=1),
            jnp.sum(q_terms, axis=1),
            jnp.sum(s_terms, axis=1),
            jnp.sum(p_terms * (teacher_logits - student_logits), axis=1),
            jnp.sum(onehot * student_logits, axis=1),
        ),
        "tensor",
    )
    kl_rows = (
        cross / (tau * p_total)
        - (teacher_max - student_max) / tau
        - jnp.log(p_total)
        + jnp.log(q_total)
    )
    row_loss = tau * tau * kl_rows + student_max + jnp.log(s_total) - picked
    loss = lax.psum(jnp.sum(row_loss), "section") / (tok_block * lax.axis_size("section"))
    p_prob = p_terms / p_total[:, None]
    q_prob = q_terms / q_total[:, None]
    s_prob = s_terms / s_total[:, None]
    logit_grad = (tau * (q_prob - p_prob) + s_prob - onehot).astype(jnp.bfloat16)
    piece = lax.all_gather(logit_grad, "section", axis=0, tiled=True)
    rows = student_all
    head_acc = lax.dot_general(
        rows, piece, (((0,), (0,)), ((), ())), preferred_element_type=jnp.float32
    )
    partial_rows = lax.dot_general(
        piece, student_head, (((1,), (1,)), ((), ())), preferred_element_type=jnp.float32
    )
    grad_hidden = lax.psum_scatter(partial_rows, "tensor", scatter_dimension=0, tiled=True).astype(
        jnp.bfloat16
    )
    return (loss, grad_hidden, head_acc.astype(jnp.bfloat16))


def steps(teacher_hidden, student_hidden, teacher_head, student_head, targets):
    section_size = lax.axis_size("section")
    chips = section_size // 2
    half_way = chips // 2
    me = lax.axis_index("section")
    z, core = me // 2, me % 2
    tok_block, dt = teacher_hidden.shape
    ds = student_hidden.shape[1]
    voc_local = teacher_head.shape[1]
    half = voc_local // 2

    def along(x, step):
        perm = [
            (s, ((s // 2 + step) % chips) * 2 + s % 2) for s in range(section_size)
        ]
        return lax.ppermute(x, "section", perm)

    def swap(x):
        return lax.ppermute(x, "section", [(s, s ^ 1) for s in range(section_size)])

    def spread(x, axis):
        n = lax.axis_size(axis)
        return lax.all_to_all(
            jnp.broadcast_to(x[None], (n,) + x.shape), axis, 0, 0
        )

    student_head_sib = swap(student_head)
    teacher_head_sib = swap(teacher_head)
    hidden = spread(jnp.concatenate([teacher_hidden, student_hidden], axis=1), "tensor")

    start = chips - half_way + 2
    order = [(start + i) % chips for i in range(chips)]
    count = chips - 3

    def rolled(x, which):
        pair = x.reshape((chips, 2) + x.shape[1:])
        twice = jnp.concatenate([pair, pair], axis=0)
        out = lax.dynamic_slice(
            twice, ((z + start) % chips, which, 0, 0), (chips, 1) + x.shape[1:]
        )
        return out.reshape((chips * x.shape[1],) + x.shape[2:])

    mine, others = rolled(hidden, core), rolled(hidden, 1 - core)
    mine_sib = swap(others)
    student_part = product(
        mine[:, dt:], mine_sib[:, dt:], student_head, student_head_sib, chips
    )
    teacher_part = product(
        mine[:, :dt], mine_sib[:, :dt], teacher_head, teacher_head_sib, chips
    )

    place = jnp.stack([z, core]).astype(jnp.int32)
    split = count * tok_block
    hidden_near = (mine[:split, dt:], others[:split, dt:])
    hidden_far = (mine[split:, dt:], others[split:, dt:])

    def ring(parts):
        parts = dict(zip(order, parts))
        right, left = first(parts[half_way])
        right, left = along(right, 1), along(left, -1)
        for step in range(1, half_way):
            right, left = hop(
                right, left, parts[half_way - step], parts[half_way + step]
            )
            right, left = along(right, 1), along(left, -1)
        return right, left, parts[0]

    offset = lax.axis_index("tensor") * voc_local
    target_here = jnp.broadcast_to((targets - offset)[:, None], (tok_block, 128))

    teacher_logits, student_logits, stats = meet(
        ring(teacher_part), ring(student_part), target_here
    )
    own = payload(teacher_logits, student_logits, spread(stats, "tensor"), target_here)

    pieces = [[None] * chips, [None] * chips]
    right, left = list(own), list(own)
    pieces[0][0], pieces[1][0] = own
    for step in range(1, half_way):
        for side in range(2):
            right[side] = along(right[side], 1)
            left[side] = along(left[side], -1)
            pieces[side][chips - step], pieces[side][step] = right[side], left[side]

    def gathered(js):
        group = [jnp.concatenate([x[j] for j in js], axis=0) for x in pieces]
        return group, [swap(x) for x in group]

    near = gathered(order[:count])
    right[0], left[1], near = lax.optimization_barrier((right[0], left[1], near))
    last = along(right[0], 1), along(left[1], -1)
    sums = near_products(student_head, hidden_near, near)
    pieces[0][half_way], pieces[1][half_way], sums = lax.optimization_barrier(
        (*last, sums)
    )
    far = gathered(order[count:])
    rows, grad_head = far_products(
        order, place, student_head, sums, hidden_far, far, tok_block
    )
    rows, grad_head = lax.optimization_barrier((rows, grad_head))
    extra = sum(
        jnp.sum(g[1][:, half:].astype(f32), axis=0) for group in (near, far) for g in group
    )
    loss = (extra[0] + extra[1] + extra[2]) / (tok_block * section_size)
    grad_hidden = jnp.sum(lax.all_to_all(rows, "tensor", 0, 0), axis=0).astype(bf16)
    return (loss, grad_hidden, grad_head), extra[3]


def shards(*arrays):
    fine, too_coarse = steps(*arrays)
    return lax.cond(too_coarse > 0.0, lambda: plain(*arrays), lambda: fine)


def solution(mesh):
    placed = (
        P("tensor", "section"),
        P("tensor", "section"),
        P("section", "tensor"),
        P("section", "tensor"),
        P("section"),
    )
    return jax.shard_map(
        shards,
        mesh=mesh,
        in_specs=placed,
        out_specs=(P(), P("tensor", "section"), P("section", "tensor")),
        check_vma=False,
    )
```

```python
import functools

import jax
import jax.numpy as jnp
from jax import lax
from jax.experimental import pallas as pl
from jax.experimental.pallas import tpu as pltpu
from jax.sharding import PartitionSpec as P

tau = 2.0
f32 = jnp.float32
bf16 = jnp.bfloat16
i16 = jnp.int16

LEVELS = 32767.0
CODES = 128
LIMIT = 1000.0
STRIP = 512
PARAMS = pltpu.CompilerParams(vmem_limit_bytes=20 * 1024 * 1024)


def row_codes(ref):
    w = ref.shape[1] - CODES
    codes = ref[:, w:].astype(jnp.int32).astype(f32)
    middle = codes[:, 0:1] * 0.25
    scale = codes[:, 32:33] * (0.5 / LEVELS)
    return middle, scale, codes[:, 64:65]


def encode(x_ref, columns, o_ref, spent):
    lo, hi = columns
    top = bottom = None
    for at in range(lo, hi, STRIP):
        x = x_ref[:, at : at + STRIP]
        top = x if top is None else jnp.maximum(top, x)
        bottom = x if bottom is None else jnp.minimum(bottom, x)
    top = jnp.max(top, axis=1, keepdims=True)
    bottom = jnp.min(bottom, axis=1, keepdims=True)
    middle_code = jnp.round((top + bottom) * 2.0)
    middle = middle_code * 0.25
    reach = jnp.maximum(top - middle, middle - bottom)
    reach_code = jnp.floor(reach * 2.0) + 1.0
    spent_code = jnp.minimum(spent + reach_code, LEVELS)
    inverse = (2.0 * LEVELS) / reach_code
    for at in range(lo, hi, STRIP):
        code = jnp.round((x_ref[:, at : at + STRIP] - middle) * inverse)
        o_ref[:, at - lo : at - lo + STRIP] = code.astype(jnp.int32).astype(i16)
    lane = lax.broadcasted_iota(jnp.int32, (x_ref.shape[0], CODES), 1)
    codes = jnp.where(lane < 32, middle_code, jnp.where(lane < 64, reach_code, spent_code))
    o_ref[:, hi - lo :] = codes.astype(jnp.int32).astype(i16)


def first_kernel(part_ref, right_ref, left_ref):
    rows, width = part_ref.shape
    none = jnp.zeros((rows, 1), f32)
    encode(part_ref, (0, width // 2), right_ref, none)
    encode(part_ref, (width // 2, width), left_ref, none)


def hop_kernel(r_ref, l_ref, pr_ref, pl_ref, ro_ref, lo_ref, sum_ref):
    width = pr_ref.shape[1]
    for in_ref, part_ref, out_ref, at_end in (
        (r_ref, pr_ref, ro_ref, False),
        (l_ref, pl_ref, lo_ref, True),
    ):
        carried = in_ref.shape[1] - CODES
        start = width - carried if at_end else 0
        middle, scale, spent = row_codes(in_ref)
        for at in range(0, width, STRIP):
            x = part_ref[:, at : at + STRIP]
            if start <= at < start + carried:
                code = in_ref[:, at - start : at - start + STRIP]
                x = x + (middle + code.astype(jnp.int32).astype(f32) * scale)
            sum_ref[:, at : at + STRIP] = x
        encode(sum_ref, (0, width), out_ref, spent)


def meet_kernel(
    rt_ref, lt_ref, pt_ref, rs_ref, ls_ref, ps_ref, target_ref, t_ref, s_ref, stats_ref
):
    rows, width = t_ref.shape
    tops, spents = [], []
    for r_ref, l_ref, part_ref, out_ref in (
        (rt_ref, lt_ref, pt_ref, t_ref),
        (rs_ref, ls_ref, ps_ref, s_ref),
    ):
        r_middle, r_scale, r_spent = row_codes(r_ref)
        l_middle, l_scale, l_spent = row_codes(l_ref)
        top = None
        for at in range(0, width, STRIP):
            strip = slice(at, at + STRIP)
            x = (
                part_ref[:, strip]
                + (r_middle + r_ref[:, strip].astype(jnp.int32).astype(f32) * r_scale)
                + (l_middle + l_ref[:, strip].astype(jnp.int32).astype(f32) * l_scale)
            )
            out_ref[:, strip] = x
            top = x if top is None else jnp.maximum(top, x)
        tops.append(jnp.max(top, axis=1, keepdims=True))
        spents.append((r_spent + l_spent) * 0.5)
    t_max, s_max = tops
    target = target_ref[:, 0:1]
    sums = None
    for at in range(0, width, 128):
        t, s = t_ref[:, at : at + 128], s_ref[:, at : at + 128]
        p = jnp.exp((t - t_max) * (1.0 / tau))
        q = jnp.exp((s - s_max) * (1.0 / tau))
        ids = at + lax.broadcasted_iota(jnp.int32, t.shape, 1)
        terms = (p, q, q * q, p * (t - s), jnp.where(ids == target, s, 0.0))
        sums = terms if sums is None else [a + b for a, b in zip(sums, terms)]
    lane = lax.broadcasted_iota(jnp.int32, (rows, 128), 1)
    kinds = [t_max, s_max] + [jnp.sum(a, axis=1, keepdims=True) for a in sums]
    kinds.append(jnp.maximum(spents[0], spents[1]))
    table = jnp.zeros((rows, 128), f32)
    for k, value in enumerate(kinds):
        table = jnp.where(lane == k, value, table)
    table = jnp.concatenate([table, jnp.zeros((128 - rows, 128), f32)], axis=0)
    stats_ref[...] = table.T[0:8, :]


def grad_kernel(t_ref, s_ref, every_ref, target_ref, a_ref, b_ref):
    rows, width = t_ref.shape
    t_tops, s_tops = every_ref[:, 0, :], every_ref[:, 1, :]
    t_max = jnp.max(t_tops, axis=0, keepdims=True)
    s_max = jnp.max(s_tops, axis=0, keepdims=True)
    t_weight = jnp.exp((t_tops - t_max) * (1.0 / tau))
    q_weight = jnp.exp((s_tops - s_max) * (1.0 / tau))
    s_weight = jnp.exp(s_tops - s_max)

    def total(k, weight):
        return jnp.sum(every_ref[:, k, :] * weight, axis=0, keepdims=True)

    p_total, q_total = total(2, t_weight), total(3, q_weight)
    s_total, cross = total(4, s_weight), total(5, t_weight)
    picked = jnp.sum(every_ref[:, 6, :], axis=0, keepdims=True)
    spent = jnp.max(every_ref[:, 7, :], axis=0, keepdims=True)
    kl_rows = (
        cross / (tau * p_total)
        - (t_max - s_max) / tau
        - jnp.log(p_total)
        + jnp.log(q_total)
    )
    row_loss = tau * tau * kl_rows + s_max + jnp.log(s_total) - picked
    flag = jnp.where(spent > LIMIT, 1.0, 0.0)
    lines = [t_max, s_max, tau / p_total, tau / q_total, 1.0 / s_total, row_loss, flag]
    lines.append(jnp.zeros((128 - len(lines), 128), f32))
    table = jnp.concatenate(lines, axis=0).T[:rows]
    t_max, s_max, p_scale, q_scale, s_scale, row_loss, flag = (
        table[:, k : k + 1] for k in range(7)
    )
    target = target_ref[:, 0:1]
    for at in range(0, width, STRIP):
        t, s = t_ref[:, at : at + STRIP], s_ref[:, at : at + STRIP]
        p = jnp.exp((t - t_max) * (1.0 / tau))
        q = jnp.exp((s - s_max) * (1.0 / tau))
        ids = at + lax.broadcasted_iota(jnp.int32, t.shape, 1)
        grad = q * q_scale - p * p_scale + (q * q) * s_scale
        grad = grad - jnp.where(ids == target, 1.0, 0.0)
        o_ref, to = (a_ref, at) if at < width // 2 else (b_ref, at - width // 2)
        o_ref[:, to : to + STRIP] = grad.astype(bf16)
    high = row_loss.astype(bf16).astype(f32)
    mid = (row_loss - high).astype(bf16).astype(f32)
    low = row_loss - high - mid
    lane = lax.broadcasted_iota(jnp.int32, (rows, CODES), 1)
    extra = jnp.where(
        lane == 0,
        high,
        jnp.where(lane == 1, mid, jnp.where(lane == 2, low, jnp.where(lane == 3, flag, 0.0))),
    )
    b_ref[:, width // 2 :] = extra.astype(bf16)


VMEM = pl.BlockSpec(memory_space=pltpu.VMEM)


def call(kernel, name, out, *operands, flops=0, **more):
    leaves = jax.tree.leaves((out, operands))
    return pl.pallas_call(
        kernel,
        out_shape=out,
        in_specs=[VMEM] * len(operands),
        out_specs=jax.tree.map(lambda _: VMEM, out),
        compiler_params=PARAMS,
        cost_estimate=pl.CostEstimate(
            flops=flops,
            bytes_accessed=sum(x.size * x.dtype.itemsize for x in leaves),
            transcendentals=0,
        ),
        name=name,
        **more,
    )(*operands)


def first(part):
    rows, width = part.shape
    out = jax.ShapeDtypeStruct((rows, width // 2 + CODES), i16)
    return call(first_kernel, "first", (out, out), part)


def hop(right, left, part_right, part_left):
    rows, width = part_right.shape
    out = jax.ShapeDtypeStruct((rows, width + CODES), i16)
    return call(
        hop_kernel, "hop", (out, out), right, left, part_right, part_left,
        scratch_shapes=[pltpu.VMEM((rows, width), f32)],
    )


def meet(teacher, student, target):
    rows, width = teacher[2].shape
    logits = jax.ShapeDtypeStruct((rows, width), f32)
    stats = jax.ShapeDtypeStruct((8, 128), f32)
    return call(meet_kernel, "meet", (logits, logits, stats), *teacher, *student, target)


def payload(teacher_logits, student_logits, every, target):
    rows, width = teacher_logits.shape
    out = (
        jax.ShapeDtypeStruct((rows, width // 2), bf16),
        jax.ShapeDtypeStruct((rows, width // 2 + CODES), bf16),
    )
    return call(
        grad_kernel, "payload", out, teacher_logits, student_logits, every, target
    )


def product_kernel(own_ref, sib_ref, head_ref, head_sib_ref, *o_refs):
    rows, width = o_refs[0].shape
    step = min(width, 2 * STRIP)
    for at in range(0, width, step):
        strip = slice(at, at + step)
        x = jnp.dot(own_ref[...], head_ref[:, strip], preferred_element_type=f32)
        x = x + jnp.dot(sib_ref[...], head_sib_ref[:, strip], preferred_element_type=f32)
        for k, o_ref in enumerate(o_refs):
            o_ref[:, strip] = x[k * rows : (k + 1) * rows]


def product(own, sib, head, head_sib, blocks):
    tokens, depth = own.shape
    width = head.shape[1]
    out = jax.ShapeDtypeStruct((tokens // blocks, width), f32)
    return call(
        product_kernel, "product", (out,) * blocks, own, sib, head, head_sib,
        flops=4 * tokens * depth * width,
    )


def back(group, head_ref):
    depth = head_ref.shape[1] // 2
    turned = (((1,), (1,)), ((), ()))
    return lax.dot_general(
        group[0][...], head_ref[:, :depth], turned, preferred_element_type=f32
    ) + lax.dot_general(
        group[1][:, :depth], head_ref[:, depth:], turned, preferred_element_type=f32
    )


def outer(hidden, groups, store):
    half = groups[0][0].shape[1]
    for side in range(2):
        for at in range(0, half, STRIP):
            total = sum(
                lax.dot_general(
                    x[...],
                    group[side][:, at : at + STRIP],
                    (((0,), (0,)), ((), ())),
                    preferred_element_type=f32,
                )
                for x, group in zip(hidden, groups)
            )
            store(side * half + at, total)


def near_kernel(head_ref, h0, h1, a0, b0, a1, b1, rows0_ref, rows1_ref, acc_ref):
    rows0_ref[...] = back((a0, b0), head_ref)
    rows1_ref[...] = back((a1, b1), head_ref)

    def store(at, total):
        acc_ref[:, at : at + STRIP] = total

    outer((h0, h1), ((a0, b0), (a1, b1)), store)


def far_kernel(
    order, place_ref, head_ref, near0, near1, acc_ref, h0, h1, a0, b0, a1, b1,
    rows_ref, o_ref,
):
    z, core = place_ref[0], place_ref[1]
    blocks, rows = rows_ref.shape[:2]
    chips = blocks // 2
    for near, group, which in (
        (near0, (a0, b0), core), (near1, (a1, b1), 1 - core)
    ):
        far = back(group, head_ref)
        count = near.shape[0] // rows
        for i, j in enumerate(order):
            x = near[i * rows : (i + 1) * rows] if i < count else (
                far[(i - count) * rows : (i - count + 1) * rows]
            )
            at = 2 * lax.rem(z + j, chips) + which
            rows_ref[pl.ds(at, 1)] = x[None].astype(bf16)

    def store(at, total):
        o_ref[:, at : at + STRIP] = (acc_ref[:, at : at + STRIP] + total).astype(bf16)

    outer((h0, h1), ((a0, b0), (a1, b1)), store)


def near_products(head, hidden, groups):
    depth, width = head.shape
    rows = jax.ShapeDtypeStruct((hidden[0].shape[0], depth), f32)
    acc = jax.ShapeDtypeStruct((depth, width), f32)
    return call(
        near_kernel, "near", (rows, rows, acc), head, *hidden, *groups[0], *groups[1],
        flops=8 * rows.size * width,
    )


def far_products(order, place, head, near, hidden, groups, rows):
    depth, width = head.shape
    blocks = 2 * len(order)
    return pl.pallas_call(
        functools.partial(far_kernel, order),
        out_shape=(
            jax.ShapeDtypeStruct((blocks, rows, depth), bf16),
            jax.ShapeDtypeStruct((depth, width), bf16),
        ),
        in_specs=[pl.BlockSpec(memory_space=pltpu.SMEM)] + [VMEM] * 10,
        out_specs=(VMEM, VMEM),
        compiler_params=PARAMS,
        name="far",
    )(place, head, *near, *hidden, *groups[0], *groups[1])


def spread(x, axis):
    n = lax.axis_size(axis)
    return lax.all_to_all(jnp.broadcast_to(x[None], (n,) + x.shape), axis, 0, 0)


def summed(x, axis):
    n = lax.axis_size(axis)
    blocks = x.reshape((n, x.shape[0] // n) + x.shape[1:])
    return jnp.sum(lax.all_to_all(blocks, axis, 0, 0), axis=0)


def plain(teacher_hidden, student_hidden, teacher_head, student_head, targets):
    tok_block, voc_local = targets.shape[0], teacher_head.shape[1]
    teacher_all = spread(teacher_hidden, "tensor").reshape(-1, teacher_hidden.shape[1])
    student_all = spread(student_hidden, "tensor").reshape(-1, student_hidden.shape[1])
    teacher_logits = summed(
        jnp.dot(teacher_all, teacher_head, preferred_element_type=f32), "section"
    )
    student_logits = summed(
        jnp.dot(student_all, student_head, preferred_element_type=f32), "section"
    )
    tops = jnp.stack([jnp.max(teacher_logits, axis=1), jnp.max(student_logits, axis=1)])
    teacher_max, student_max = jnp.max(spread(tops, "tensor"), axis=0)
    offset = lax.axis_index("tensor") * voc_local
    column_ids = offset + lax.broadcasted_iota(jnp.int32, (tok_block, voc_local), 1)
    onehot = (column_ids == targets[:, None]).astype(f32)
    p_terms = jnp.exp((teacher_logits - teacher_max[:, None]) / tau)
    q_terms = jnp.exp((student_logits - student_max[:, None]) / tau)
    s_terms = jnp.exp(student_logits - student_max[:, None])
    sums = jnp.stack(
        [
            jnp.sum(p_terms, axis=1),
            jnp.sum(q_terms, axis=1),
            jnp.sum(s_terms, axis=1),
            jnp.sum(p_terms * (teacher_logits - student_logits), axis=1),
            jnp.sum(onehot * student_logits, axis=1),
        ]
    )
    p_total, q_total, s_total, cross, picked = jnp.sum(spread(sums, "tensor"), axis=0)
    kl_rows = (
        cross / (tau * p_total)
        - (teacher_max - student_max) / tau
        - jnp.log(p_total)
        + jnp.log(q_total)
    )
    row_loss = tau * tau * kl_rows + student_max + jnp.log(s_total) - picked
    loss = jnp.mean(spread(row_loss, "section"))
    p_prob = p_terms / p_total[:, None]
    q_prob = q_terms / q_total[:, None]
    s_prob = s_terms / s_total[:, None]
    grad = (tau * (q_prob - p_prob) + s_prob - onehot).astype(bf16)
    grad = spread(grad, "section").reshape(-1, voc_local)
    grad_head = lax.dot_general(
        student_all, grad, (((0,), (0,)), ((), ())), preferred_element_type=f32
    )
    rows = lax.dot_general(
        grad, student_head, (((1,), (1,)), ((), ())), preferred_element_type=f32
    )
    return loss, summed(rows, "tensor").astype(bf16), grad_head.astype(bf16)


def steps(teacher_hidden, student_hidden, teacher_head, student_head, targets):
    section_size = lax.axis_size("section")
    chips = section_size // 2
    half_way = chips // 2
    me = lax.axis_index("section")
    z, core = me // 2, me % 2
    tok_block, dt = teacher_hidden.shape
    ds = student_hidden.shape[1]
    voc_local = teacher_head.shape[1]
    half = voc_local // 2

    def along(x, step):
        perm = [
            (s, ((s // 2 + step) % chips) * 2 + s % 2) for s in range(section_size)
        ]
        return lax.ppermute(x, "section", perm)

    def swap(x):
        return lax.ppermute(x, "section", [(s, s ^ 1) for s in range(section_size)])

    student_head_sib = swap(student_head)
    teacher_head_sib = swap(teacher_head)
    hidden = spread(jnp.concatenate([teacher_hidden, student_hidden], axis=1), "tensor")

    start = chips - half_way + 2
    order = [(start + i) % chips for i in range(chips)]
    count = chips - 3

    def rolled(x, which):
        pair = x.reshape((chips, 2) + x.shape[1:])
        twice = jnp.concatenate([pair, pair], axis=0)
        out = lax.dynamic_slice(
            twice, ((z + start) % chips, which, 0, 0), (chips, 1) + x.shape[1:]
        )
        return out.reshape((chips * x.shape[1],) + x.shape[2:])

    mine, others = rolled(hidden, core), rolled(hidden, 1 - core)
    mine_sib = swap(others)
    student_part = product(
        mine[:, dt:], mine_sib[:, dt:], student_head, student_head_sib, chips
    )
    teacher_part = product(
        mine[:, :dt], mine_sib[:, :dt], teacher_head, teacher_head_sib, chips
    )

    place = jnp.stack([z, core]).astype(jnp.int32)
    split = count * tok_block
    hidden_near = (mine[:split, dt:], others[:split, dt:])
    hidden_far = (mine[split:, dt:], others[split:, dt:])

    def ring(parts):
        parts = dict(zip(order, parts))
        right, left = first(parts[half_way])
        right, left = along(right, 1), along(left, -1)
        for step in range(1, half_way):
            right, left = hop(
                right, left, parts[half_way - step], parts[half_way + step]
            )
            right, left = along(right, 1), along(left, -1)
        return right, left, parts[0]

    offset = lax.axis_index("tensor") * voc_local
    target_here = jnp.broadcast_to((targets - offset)[:, None], (tok_block, 128))

    teacher_logits, student_logits, stats = meet(
        ring(teacher_part), ring(student_part), target_here
    )
    own = payload(teacher_logits, student_logits, spread(stats, "tensor"), target_here)

    pieces = [[None] * chips, [None] * chips]
    right, left = list(own), list(own)
    pieces[0][0], pieces[1][0] = own
    for step in range(1, half_way):
        for side in range(2):
            right[side] = along(right[side], 1)
            left[side] = along(left[side], -1)
            pieces[side][chips - step], pieces[side][step] = right[side], left[side]

    def gathered(js):
        group = [jnp.concatenate([x[j] for j in js], axis=0) for x in pieces]
        return group, [swap(x) for x in group]

    near = gathered(order[:count])
    right[0], left[1], near = lax.optimization_barrier((right[0], left[1], near))
    last = along(right[0], 1), along(left[1], -1)
    sums = near_products(student_head, hidden_near, near)
    pieces[0][half_way], pieces[1][half_way], sums = lax.optimization_barrier(
        (*last, sums)
    )
    far = gathered(order[count:])
    rows, grad_head = far_products(
        order, place, student_head, sums, hidden_far, far, tok_block
    )
    rows, grad_head = lax.optimization_barrier((rows, grad_head))
    extra = sum(
        jnp.sum(g[1][:, half:].astype(f32), axis=0) for group in (near, far) for g in group
    )
    loss = (extra[0] + extra[1] + extra[2]) / (tok_block * section_size)
    rows = lax.all_to_all(rows, "tensor", 0, 0).astype(f32)
    grad_hidden = jnp.sum(rows, axis=0).astype(bf16)
    return (loss, grad_hidden, grad_head), extra[3]


def shards(*arrays):
    fine, too_coarse = steps(*arrays)
    return lax.while_loop(
        lambda state: state[0] > 0.0,
        lambda state: (jnp.zeros_like(too_coarse), plain(*arrays)),
        (too_coarse, fine),
    )[1]


def solution(mesh):
    placed = (
        P("tensor", "section"),
        P("tensor", "section"),
        P("section", "tensor"),
        P("section", "tensor"),
        P("section"),
    )
    return jax.shard_map(
        shards,
        mesh=mesh,
        in_specs=placed,
        out_specs=(P(), P("tensor", "section"), P("section", "tensor")),
        check_vma=False,
    )
```

```python
import functools

import jax
import jax.numpy as jnp
from jax import lax
from jax.experimental import pallas as pl
from jax.experimental.pallas import tpu as pltpu
from jax.sharding import PartitionSpec as P

tau = 2.0
f32 = jnp.float32
bf16 = jnp.bfloat16
i16 = jnp.int16

LEVELS = 32767.0
CODES = 128
LIMIT = 1000.0
STRIP = 512
PARAMS = pltpu.CompilerParams(vmem_limit_bytes=20 * 1024 * 1024)


def row_codes(ref):
    w = ref.shape[1] - CODES
    codes = ref[:, w:].astype(jnp.int32).astype(f32)
    middle = codes[:, 0:1] * 0.25
    scale = codes[:, 32:33] * (0.5 / LEVELS)
    return middle, scale, codes[:, 64:65]


def encode(x_ref, columns, o_ref, spent):
    lo, hi = columns
    top = bottom = None
    for at in range(lo, hi, STRIP):
        x = x_ref[:, at : at + STRIP]
        top = x if top is None else jnp.maximum(top, x)
        bottom = x if bottom is None else jnp.minimum(bottom, x)
    top = jnp.max(top, axis=1, keepdims=True)
    bottom = jnp.min(bottom, axis=1, keepdims=True)
    middle_code = jnp.round((top + bottom) * 2.0)
    middle = middle_code * 0.25
    reach = jnp.maximum(top - middle, middle - bottom)
    reach_code = jnp.floor(reach * 2.0) + 1.0
    spent_code = jnp.minimum(spent + reach_code, LEVELS)
    inverse = (2.0 * LEVELS) / reach_code
    for at in range(lo, hi, STRIP):
        code = jnp.round((x_ref[:, at : at + STRIP] - middle) * inverse)
        o_ref[:, at - lo : at - lo + STRIP] = code.astype(jnp.int32).astype(i16)
    lane = lax.broadcasted_iota(jnp.int32, (x_ref.shape[0], CODES), 1)
    codes = jnp.where(lane < 32, middle_code, jnp.where(lane < 64, reach_code, spent_code))
    o_ref[:, hi - lo :] = codes.astype(jnp.int32).astype(i16)


def first_kernel(part_ref, right_ref, left_ref):
    rows, width = part_ref.shape
    none = jnp.zeros((rows, 1), f32)
    encode(part_ref, (0, width // 2), right_ref, none)
    encode(part_ref, (width // 2, width), left_ref, none)


def hop_kernel(r_ref, l_ref, pr_ref, pl_ref, ro_ref, lo_ref, sum_ref):
    width = pr_ref.shape[1]
    for in_ref, part_ref, out_ref, at_end in (
        (r_ref, pr_ref, ro_ref, False),
        (l_ref, pl_ref, lo_ref, True),
    ):
        carried = in_ref.shape[1] - CODES
        start = width - carried if at_end else 0
        middle, scale, spent = row_codes(in_ref)
        for at in range(0, width, STRIP):
            x = part_ref[:, at : at + STRIP]
            if start <= at < start + carried:
                code = in_ref[:, at - start : at - start + STRIP]
                x = x + (middle + code.astype(jnp.int32).astype(f32) * scale)
            sum_ref[:, at : at + STRIP] = x
        encode(sum_ref, (0, width), out_ref, spent)


def meet_kernel(
    rt_ref, lt_ref, pt_ref, rs_ref, ls_ref, ps_ref, target_ref, t_ref, s_ref, stats_ref
):
    rows, width = t_ref.shape
    tops, spents = [], []
    for r_ref, l_ref, part_ref, out_ref in (
        (rt_ref, lt_ref, pt_ref, t_ref),
        (rs_ref, ls_ref, ps_ref, s_ref),
    ):
        r_middle, r_scale, r_spent = row_codes(r_ref)
        l_middle, l_scale, l_spent = row_codes(l_ref)
        top = None
        for at in range(0, width, STRIP):
            strip = slice(at, at + STRIP)
            x = (
                part_ref[:, strip]
                + (r_middle + r_ref[:, strip].astype(jnp.int32).astype(f32) * r_scale)
                + (l_middle + l_ref[:, strip].astype(jnp.int32).astype(f32) * l_scale)
            )
            out_ref[:, strip] = x
            top = x if top is None else jnp.maximum(top, x)
        tops.append(jnp.max(top, axis=1, keepdims=True))
        spents.append((r_spent + l_spent) * 0.5)
    t_max, s_max = tops
    target = target_ref[:, 0:1]
    sums = None
    for at in range(0, width, 128):
        t, s = t_ref[:, at : at + 128], s_ref[:, at : at + 128]
        p = jnp.exp((t - t_max) * (1.0 / tau))
        q = jnp.exp((s - s_max) * (1.0 / tau))
        ids = at + lax.broadcasted_iota(jnp.int32, t.shape, 1)
        terms = (p, q, q * q, p * (t - s), jnp.where(ids == target, s, 0.0))
        sums = terms if sums is None else [a + b for a, b in zip(sums, terms)]
    lane = lax.broadcasted_iota(jnp.int32, (rows, 128), 1)
    kinds = [t_max, s_max] + [jnp.sum(a, axis=1, keepdims=True) for a in sums]
    kinds.append(jnp.maximum(spents[0], spents[1]))
    table = jnp.zeros((rows, 128), f32)
    for k, value in enumerate(kinds):
        table = jnp.where(lane == k, value, table)
    table = jnp.concatenate([table, jnp.zeros((128 - rows, 128), f32)], axis=0)
    stats_ref[...] = table.T[0:8, :]


def grad_kernel(t_ref, s_ref, every_ref, target_ref, a_ref, b_ref):
    rows, width = t_ref.shape
    t_tops, s_tops = every_ref[:, 0, :], every_ref[:, 1, :]
    t_max = jnp.max(t_tops, axis=0, keepdims=True)
    s_max = jnp.max(s_tops, axis=0, keepdims=True)
    t_weight = jnp.exp((t_tops - t_max) * (1.0 / tau))
    q_weight = jnp.exp((s_tops - s_max) * (1.0 / tau))
    s_weight = jnp.exp(s_tops - s_max)

    def total(k, weight):
        return jnp.sum(every_ref[:, k, :] * weight, axis=0, keepdims=True)

    p_total, q_total = total(2, t_weight), total(3, q_weight)
    s_total, cross = total(4, s_weight), total(5, t_weight)
    picked = jnp.sum(every_ref[:, 6, :], axis=0, keepdims=True)
    spent = jnp.max(every_ref[:, 7, :], axis=0, keepdims=True)
    kl_rows = (
        cross / (tau * p_total)
        - (t_max - s_max) / tau
        - jnp.log(p_total)
        + jnp.log(q_total)
    )
    row_loss = tau * tau * kl_rows + s_max + jnp.log(s_total) - picked
    flag = jnp.where(spent > LIMIT, 1.0, 0.0)
    lines = [t_max, s_max, tau / p_total, tau / q_total, 1.0 / s_total, row_loss, flag]
    lines.append(jnp.zeros((128 - len(lines), 128), f32))
    table = jnp.concatenate(lines, axis=0).T[:rows]
    t_max, s_max, p_scale, q_scale, s_scale, row_loss, flag = (
        table[:, k : k + 1] for k in range(7)
    )
    target = target_ref[:, 0:1]
    for at in range(0, width, STRIP):
        t, s = t_ref[:, at : at + STRIP], s_ref[:, at : at + STRIP]
        p = jnp.exp((t - t_max) * (1.0 / tau))
        q = jnp.exp((s - s_max) * (1.0 / tau))
        ids = at + lax.broadcasted_iota(jnp.int32, t.shape, 1)
        grad = q * q_scale - p * p_scale + (q * q) * s_scale
        grad = grad - jnp.where(ids == target, 1.0, 0.0)
        o_ref, to = (a_ref, at) if at < width // 2 else (b_ref, at - width // 2)
        o_ref[:, to : to + STRIP] = grad.astype(bf16)
    high = row_loss.astype(bf16).astype(f32)
    mid = (row_loss - high).astype(bf16).astype(f32)
    low = row_loss - high - mid
    lane = lax.broadcasted_iota(jnp.int32, (rows, CODES), 1)
    extra = jnp.where(
        lane == 0,
        high,
        jnp.where(lane == 1, mid, jnp.where(lane == 2, low, jnp.where(lane == 3, flag, 0.0))),
    )
    b_ref[:, width // 2 :] = extra.astype(bf16)


VMEM = pl.BlockSpec(memory_space=pltpu.VMEM)


def call(kernel, name, out, *operands, flops=0, **more):
    leaves = jax.tree.leaves((out, operands))
    return pl.pallas_call(
        kernel,
        out_shape=out,
        in_specs=[VMEM] * len(operands),
        out_specs=jax.tree.map(lambda _: VMEM, out),
        compiler_params=PARAMS,
        cost_estimate=pl.CostEstimate(
            flops=flops,
            bytes_accessed=sum(x.size * x.dtype.itemsize for x in leaves),
            transcendentals=0,
        ),
        name=name,
        **more,
    )(*operands)


def first(part):
    rows, width = part.shape
    out = jax.ShapeDtypeStruct((rows, width // 2 + CODES), i16)
    return call(first_kernel, "first", (out, out), part)


def hop(right, left, part_right, part_left):
    rows, width = part_right.shape
    out = jax.ShapeDtypeStruct((rows, width + CODES), i16)
    return call(
        hop_kernel, "hop", (out, out), right, left, part_right, part_left,
        scratch_shapes=[pltpu.VMEM((rows, width), f32)],
    )


def meet(teacher, student, target):
    rows, width = teacher[2].shape
    logits = jax.ShapeDtypeStruct((rows, width), f32)
    stats = jax.ShapeDtypeStruct((8, 128), f32)
    return call(meet_kernel, "meet", (logits, logits, stats), *teacher, *student, target)


def payload(teacher_logits, student_logits, every, target):
    rows, width = teacher_logits.shape
    out = (
        jax.ShapeDtypeStruct((rows, width // 2), bf16),
        jax.ShapeDtypeStruct((rows, width // 2 + CODES), bf16),
    )
    return call(
        grad_kernel, "payload", out, teacher_logits, student_logits, every, target
    )


def product_kernel(own_ref, sib_ref, head_ref, head_sib_ref, *o_refs):
    rows, width = o_refs[0].shape
    step = min(width, 2 * STRIP)
    for at in range(0, width, step):
        strip = slice(at, at + step)
        x = jnp.dot(own_ref[...], head_ref[:, strip], preferred_element_type=f32)
        x = x + jnp.dot(sib_ref[...], head_sib_ref[:, strip], preferred_element_type=f32)
        for k, o_ref in enumerate(o_refs):
            o_ref[:, strip] = x[k * rows : (k + 1) * rows]


def product(own, sib, head, head_sib, blocks):
    tokens, depth = own.shape
    width = head.shape[1]
    out = jax.ShapeDtypeStruct((tokens // blocks, width), f32)
    return call(
        product_kernel, "product", (out,) * blocks, own, sib, head, head_sib,
        flops=4 * tokens * depth * width,
    )


def back(group, head_ref):
    depth = head_ref.shape[1] // 2
    turned = (((1,), (1,)), ((), ()))
    return lax.dot_general(
        group[0][...], head_ref[:, :depth], turned, preferred_element_type=f32
    ) + lax.dot_general(
        group[1][:, :depth], head_ref[:, depth:], turned, preferred_element_type=f32
    )


def outer(hidden, groups, store):
    half = groups[0][0].shape[1]
    for side in range(2):
        for at in range(0, half, STRIP):
            total = sum(
                lax.dot_general(
                    x[...],
                    group[side][:, at : at + STRIP],
                    (((0,), (0,)), ((), ())),
                    preferred_element_type=f32,
                )
                for x, group in zip(hidden, groups)
            )
            store(side * half + at, total)


def near_kernel(head_ref, h0, h1, a0, b0, a1, b1, rows0_ref, rows1_ref, acc_ref):
    rows0_ref[...] = back((a0, b0), head_ref)
    rows1_ref[...] = back((a1, b1), head_ref)

    def store(at, total):
        acc_ref[:, at : at + STRIP] = total

    outer((h0, h1), ((a0, b0), (a1, b1)), store)


def far_kernel(
    order, place_ref, head_ref, near0, near1, acc_ref, h0, h1, a0, b0, a1, b1,
    rows_ref, o_ref,
):
    z, core = place_ref[0], place_ref[1]
    blocks, rows = rows_ref.shape[:2]
    chips = blocks // 2
    for near, group, which in (
        (near0, (a0, b0), core), (near1, (a1, b1), 1 - core)
    ):
        far = back(group, head_ref)
        count = near.shape[0] // rows
        for i, j in enumerate(order):
            x = near[i * rows : (i + 1) * rows] if i < count else (
                far[(i - count) * rows : (i - count + 1) * rows]
            )
            at = 2 * lax.rem(z + j, chips) + which
            rows_ref[pl.ds(at, 1)] = x[None]

    def store(at, total):
        o_ref[:, at : at + STRIP] = (acc_ref[:, at : at + STRIP] + total).astype(bf16)

    outer((h0, h1), ((a0, b0), (a1, b1)), store)


def near_products(head, hidden, groups):
    depth, width = head.shape
    rows = jax.ShapeDtypeStruct((hidden[0].shape[0], depth), f32)
    acc = jax.ShapeDtypeStruct((depth, width), f32)
    return call(
        near_kernel, "near", (rows, rows, acc), head, *hidden, *groups[0], *groups[1],
        flops=8 * rows.size * width,
    )


def far_products(order, place, head, near, hidden, groups, rows):
    depth, width = head.shape
    blocks = 2 * len(order)
    return pl.pallas_call(
        functools.partial(far_kernel, order),
        out_shape=(
            jax.ShapeDtypeStruct((blocks, rows, depth), f32),
            jax.ShapeDtypeStruct((depth, width), bf16),
        ),
        in_specs=[pl.BlockSpec(memory_space=pltpu.SMEM)] + [VMEM] * 10,
        out_specs=(VMEM, VMEM),
        compiler_params=PARAMS,
        name="far",
    )(place, head, *near, *hidden, *groups[0], *groups[1])


def spread(x, axis):
    n = lax.axis_size(axis)
    return lax.all_to_all(jnp.broadcast_to(x[None], (n,) + x.shape), axis, 0, 0)


def summed(x, axis):
    n = lax.axis_size(axis)
    blocks = x.reshape((n, x.shape[0] // n) + x.shape[1:])
    return jnp.sum(lax.all_to_all(blocks, axis, 0, 0), axis=0)


def plain(teacher_hidden, student_hidden, teacher_head, student_head, targets):
    tok_block, voc_local = targets.shape[0], teacher_head.shape[1]
    teacher_all = spread(teacher_hidden, "tensor").reshape(-1, teacher_hidden.shape[1])
    student_all = spread(student_hidden, "tensor").reshape(-1, student_hidden.shape[1])
    teacher_logits = summed(
        jnp.dot(teacher_all, teacher_head, preferred_element_type=f32), "section"
    )
    student_logits = summed(
        jnp.dot(student_all, student_head, preferred_element_type=f32), "section"
    )
    tops = jnp.stack([jnp.max(teacher_logits, axis=1), jnp.max(student_logits, axis=1)])
    teacher_max, student_max = jnp.max(spread(tops, "tensor"), axis=0)
    offset = lax.axis_index("tensor") * voc_local
    column_ids = offset + lax.broadcasted_iota(jnp.int32, (tok_block, voc_local), 1)
    onehot = (column_ids == targets[:, None]).astype(f32)
    p_terms = jnp.exp((teacher_logits - teacher_max[:, None]) / tau)
    q_terms = jnp.exp((student_logits - student_max[:, None]) / tau)
    s_terms = jnp.exp(student_logits - student_max[:, None])
    sums = jnp.stack(
        [
            jnp.sum(p_terms, axis=1),
            jnp.sum(q_terms, axis=1),
            jnp.sum(s_terms, axis=1),
            jnp.sum(p_terms * (teacher_logits - student_logits), axis=1),
            jnp.sum(onehot * student_logits, axis=1),
        ]
    )
    p_total, q_total, s_total, cross, picked = jnp.sum(spread(sums, "tensor"), axis=0)
    kl_rows = (
        cross / (tau * p_total)
        - (teacher_max - student_max) / tau
        - jnp.log(p_total)
        + jnp.log(q_total)
    )
    row_loss = tau * tau * kl_rows + student_max + jnp.log(s_total) - picked
    loss = jnp.mean(spread(row_loss, "section"))
    p_prob = p_terms / p_total[:, None]
    q_prob = q_terms / q_total[:, None]
    s_prob = s_terms / s_total[:, None]
    grad = (tau * (q_prob - p_prob) + s_prob - onehot).astype(bf16)
    grad = spread(grad, "section").reshape(-1, voc_local)
    grad_head = lax.dot_general(
        student_all, grad, (((0,), (0,)), ((), ())), preferred_element_type=f32
    )
    rows = lax.dot_general(
        grad, student_head, (((1,), (1,)), ((), ())), preferred_element_type=f32
    )
    return loss, summed(rows, "tensor").astype(bf16), grad_head.astype(bf16)


def steps(teacher_hidden, student_hidden, teacher_head, student_head, targets):
    section_size = lax.axis_size("section")
    chips = section_size // 2
    half_way = chips // 2
    me = lax.axis_index("section")
    z, core = me // 2, me % 2
    tok_block, dt = teacher_hidden.shape
    ds = student_hidden.shape[1]
    voc_local = teacher_head.shape[1]
    half = voc_local // 2

    def along(x, step):
        perm = [
            (s, ((s // 2 + step) % chips) * 2 + s % 2) for s in range(section_size)
        ]
        return lax.ppermute(x, "section", perm)

    def swap(x):
        return lax.ppermute(x, "section", [(s, s ^ 1) for s in range(section_size)])

    student_head_sib = swap(student_head)
    teacher_head_sib = swap(teacher_head)
    copies = [
        jnp.broadcast_to(x[None], (lax.axis_size("tensor"),) + x.shape)
        for x in (teacher_hidden, student_hidden)
    ]
    hidden = lax.all_to_all(jnp.concatenate(copies, axis=2), "tensor", 0, 0)

    start = chips - half_way + 2
    order = [(start + i) % chips for i in range(chips)]
    count = chips - 3

    def rolled(x, which):
        pair = x.reshape((chips, 2) + x.shape[1:])
        twice = jnp.concatenate([pair, pair], axis=0)
        out = lax.dynamic_slice(
            twice, ((z + start) % chips, which, 0, 0), (chips, 1) + x.shape[1:]
        )
        return out.reshape((chips * x.shape[1],) + x.shape[2:])

    mine, others = rolled(hidden, core), rolled(hidden, 1 - core)
    mine_sib = swap(others)
    student_part = product(
        mine[:, dt:], mine_sib[:, dt:], student_head, student_head_sib, chips
    )
    teacher_part = product(
        mine[:, :dt], mine_sib[:, :dt], teacher_head, teacher_head_sib, chips
    )

    place = jnp.stack([z, core]).astype(jnp.int32)
    split = count * tok_block
    hidden_near = (mine[:split, dt:], others[:split, dt:])
    hidden_far = (mine[split:, dt:], others[split:, dt:])

    def ring(parts, meanwhile=()):
        parts = dict(zip(order, parts))
        right, left = first(parts[half_way])
        right, left = along(right, 1), along(left, -1)
        for step in range(1, half_way):
            right, left = hop(
                right, left, parts[half_way - step], parts[half_way + step]
            )
            if step == half_way - 1:
                right, left, meanwhile = lax.optimization_barrier((right, left, meanwhile))
            right, left = along(right, 1), along(left, -1)
        return (right, left, parts[0]), meanwhile

    offset = lax.axis_index("tensor") * voc_local
    target_here = jnp.broadcast_to((targets - offset)[:, None], (tok_block, 128))

    student, _ = ring(student_part)
    teacher, (hidden_near, hidden_far) = ring(teacher_part, (hidden_near, hidden_far))
    teacher_logits, student_logits, stats = meet(teacher, student, target_here)
    own = payload(teacher_logits, student_logits, spread(stats, "tensor"), target_here)

    pieces = [[None] * chips, [None] * chips]
    right, left = list(own), list(own)
    pieces[0][0], pieces[1][0] = own
    for step in range(1, half_way):
        for side in range(2):
            right[side] = along(right[side], 1)
            left[side] = along(left[side], -1)
            pieces[side][chips - step], pieces[side][step] = right[side], left[side]

    def gathered(js):
        group = [jnp.concatenate([x[j] for j in js], axis=0) for x in pieces]
        return group, [swap(x) for x in group]

    pieces, right[0], left[1] = lax.optimization_barrier((pieces, right[0], left[1]))
    near = gathered(order[:count])
    last = along(right[0], 1), along(left[1], -1)
    sums = near_products(student_head, hidden_near, near)
    pieces[0][half_way], pieces[1][half_way], sums = lax.optimization_barrier(
        (*last, sums)
    )
    far = gathered(order[count:])
    rows, grad_head = far_products(
        order, place, student_head, sums, hidden_far, far, tok_block
    )
    rows, grad_head = lax.optimization_barrier((rows, grad_head))
    extra = sum(
        jnp.sum(g[1][:, half:].astype(f32), axis=0) for group in (near, far) for g in group
    )
    loss = (extra[0] + extra[1] + extra[2]) / (tok_block * section_size)
    grad_hidden = jnp.sum(lax.all_to_all(rows, "tensor", 0, 0), axis=0).astype(bf16)
    return (loss, grad_hidden, grad_head), extra[3]


def shards(*arrays):
    fine, too_coarse = steps(*arrays)
    return lax.cond(too_coarse > 0.0, lambda: plain(*arrays), lambda: fine)


def solution(mesh):
    placed = (
        P("tensor", "section"),
        P("tensor", "section"),
        P("section", "tensor"),
        P("section", "tensor"),
        P("section"),
    )
    return jax.shard_map(
        shards,
        mesh=mesh,
        in_specs=placed,
        out_specs=(P(), P("tensor", "section"), P("section", "tensor")),
        check_vma=False,
    )
```

```python
import functools

import jax
import jax.numpy as jnp
from jax import lax
from jax.experimental import pallas as pl
from jax.experimental.pallas import tpu as pltpu
from jax.sharding import PartitionSpec as P

tau = 2.0
f32 = jnp.float32
bf16 = jnp.bfloat16
i16 = jnp.int16

LEVELS = 32767.0
CODES = 128
LIMIT = 1000.0
STRIP = 512
PARAMS = pltpu.CompilerParams(vmem_limit_bytes=20 * 1024 * 1024)


def row_codes(ref):
    w = ref.shape[1] - CODES
    codes = ref[:, w:].astype(jnp.int32).astype(f32)
    middle = codes[:, 0:1] * 0.25
    scale = codes[:, 32:33] * (0.5 / LEVELS)
    return middle, scale, codes[:, 64:65]


def encode(x_ref, columns, o_ref, spent):
    lo, hi = columns
    top = bottom = None
    for at in range(lo, hi, STRIP):
        x = x_ref[:, at : at + STRIP]
        top = x if top is None else jnp.maximum(top, x)
        bottom = x if bottom is None else jnp.minimum(bottom, x)
    top = jnp.max(top, axis=1, keepdims=True)
    bottom = jnp.min(bottom, axis=1, keepdims=True)
    middle_code = jnp.round((top + bottom) * 2.0)
    middle = middle_code * 0.25
    reach = jnp.maximum(top - middle, middle - bottom)
    reach_code = jnp.floor(reach * 2.0) + 1.0
    spent_code = jnp.minimum(spent + reach_code, LEVELS)
    inverse = (2.0 * LEVELS) / reach_code
    for at in range(lo, hi, STRIP):
        code = jnp.round((x_ref[:, at : at + STRIP] - middle) * inverse)
        o_ref[:, at - lo : at - lo + STRIP] = code.astype(jnp.int32).astype(i16)
    lane = lax.broadcasted_iota(jnp.int32, (x_ref.shape[0], CODES), 1)
    codes = jnp.where(lane < 32, middle_code, jnp.where(lane < 64, reach_code, spent_code))
    o_ref[:, hi - lo :] = codes.astype(jnp.int32).astype(i16)


def first_kernel(part_ref, right_ref, left_ref):
    rows, width = part_ref.shape
    none = jnp.zeros((rows, 1), f32)
    encode(part_ref, (0, width // 2), right_ref, none)
    encode(part_ref, (width // 2, width), left_ref, none)


def hop_kernel(r_ref, l_ref, pr_ref, pl_ref, ro_ref, lo_ref, sum_ref):
    width = pr_ref.shape[1]
    for in_ref, part_ref, out_ref, at_end in (
        (r_ref, pr_ref, ro_ref, False),
        (l_ref, pl_ref, lo_ref, True),
    ):
        carried = in_ref.shape[1] - CODES
        start = width - carried if at_end else 0
        middle, scale, spent = row_codes(in_ref)
        for at in range(0, width, STRIP):
            x = part_ref[:, at : at + STRIP]
            if start <= at < start + carried:
                code = in_ref[:, at - start : at - start + STRIP]
                x = x + (middle + code.astype(jnp.int32).astype(f32) * scale)
            sum_ref[:, at : at + STRIP] = x
        encode(sum_ref, (0, width), out_ref, spent)


def meet_kernel(
    rt_ref, lt_ref, pt_ref, rs_ref, ls_ref, ps_ref, target_ref, t_ref, s_ref, stats_ref
):
    rows, width = t_ref.shape
    tops, spents = [], []
    for r_ref, l_ref, part_ref, out_ref in (
        (rt_ref, lt_ref, pt_ref, t_ref),
        (rs_ref, ls_ref, ps_ref, s_ref),
    ):
        r_middle, r_scale, r_spent = row_codes(r_ref)
        l_middle, l_scale, l_spent = row_codes(l_ref)
        top = None
        for at in range(0, width, STRIP):
            strip = slice(at, at + STRIP)
            x = (
                part_ref[:, strip]
                + (r_middle + r_ref[:, strip].astype(jnp.int32).astype(f32) * r_scale)
                + (l_middle + l_ref[:, strip].astype(jnp.int32).astype(f32) * l_scale)
            )
            out_ref[:, strip] = x
            top = x if top is None else jnp.maximum(top, x)
        tops.append(jnp.max(top, axis=1, keepdims=True))
        spents.append((r_spent + l_spent) * 0.5)
    t_max, s_max = tops
    target = target_ref[:, 0:1]
    sums = None
    for at in range(0, width, 128):
        t, s = t_ref[:, at : at + 128], s_ref[:, at : at + 128]
        p = jnp.exp((t - t_max) * (1.0 / tau))
        q = jnp.exp((s - s_max) * (1.0 / tau))
        ids = at + lax.broadcasted_iota(jnp.int32, t.shape, 1)
        terms = (p, q, q * q, p * (t - s), jnp.where(ids == target, s, 0.0))
        sums = terms if sums is None else [a + b for a, b in zip(sums, terms)]
    lane = lax.broadcasted_iota(jnp.int32, (rows, 128), 1)
    kinds = [t_max, s_max] + [jnp.sum(a, axis=1, keepdims=True) for a in sums]
    kinds.append(jnp.maximum(spents[0], spents[1]))
    table = jnp.zeros((rows, 128), f32)
    for k, value in enumerate(kinds):
        table = jnp.where(lane == k, value, table)
    table = jnp.concatenate([table, jnp.zeros((128 - rows, 128), f32)], axis=0)
    stats_ref[...] = table.T[0:8, :]


def grad_kernel(t_ref, s_ref, every_ref, target_ref, a_ref, b_ref):
    rows, width = t_ref.shape
    t_tops, s_tops = every_ref[:, 0, :], every_ref[:, 1, :]
    t_max = jnp.max(t_tops, axis=0, keepdims=True)
    s_max = jnp.max(s_tops, axis=0, keepdims=True)
    t_weight = jnp.exp((t_tops - t_max) * (1.0 / tau))
    q_weight = jnp.exp((s_tops - s_max) * (1.0 / tau))
    s_weight = jnp.exp(s_tops - s_max)

    def total(k, weight):
        return jnp.sum(every_ref[:, k, :] * weight, axis=0, keepdims=True)

    p_total, q_total = total(2, t_weight), total(3, q_weight)
    s_total, cross = total(4, s_weight), total(5, t_weight)
    picked = jnp.sum(every_ref[:, 6, :], axis=0, keepdims=True)
    spent = jnp.max(every_ref[:, 7, :], axis=0, keepdims=True)
    kl_rows = (
        cross / (tau * p_total)
        - (t_max - s_max) / tau
        - jnp.log(p_total)
        + jnp.log(q_total)
    )
    row_loss = tau * tau * kl_rows + s_max + jnp.log(s_total) - picked
    flag = jnp.where(spent > LIMIT, 1.0, 0.0)
    lines = [t_max, s_max, tau / p_total, tau / q_total, 1.0 / s_total, row_loss, flag]
    lines.append(jnp.zeros((128 - len(lines), 128), f32))
    table = jnp.concatenate(lines, axis=0).T[:rows]
    t_max, s_max, p_scale, q_scale, s_scale, row_loss, flag = (
        table[:, k : k + 1] for k in range(7)
    )
    target = target_ref[:, 0:1]
    for at in range(0, width, STRIP):
        t, s = t_ref[:, at : at + STRIP], s_ref[:, at : at + STRIP]
        p = jnp.exp((t - t_max) * (1.0 / tau))
        q = jnp.exp((s - s_max) * (1.0 / tau))
        ids = at + lax.broadcasted_iota(jnp.int32, t.shape, 1)
        grad = q * q_scale - p * p_scale + (q * q) * s_scale
        grad = grad - jnp.where(ids == target, 1.0, 0.0)
        o_ref, to = (a_ref, at) if at < width // 2 else (b_ref, at - width // 2)
        o_ref[:, to : to + STRIP] = grad.astype(bf16)
    high = row_loss.astype(bf16).astype(f32)
    mid = (row_loss - high).astype(bf16).astype(f32)
    low = row_loss - high - mid
    lane = lax.broadcasted_iota(jnp.int32, (rows, CODES), 1)
    extra = jnp.where(
        lane == 0,
        high,
        jnp.where(lane == 1, mid, jnp.where(lane == 2, low, jnp.where(lane == 3, flag, 0.0))),
    )
    b_ref[:, width // 2 :] = extra.astype(bf16)


VMEM = pl.BlockSpec(memory_space=pltpu.VMEM)


def call(kernel, name, out, *operands, flops=0, **more):
    leaves = jax.tree.leaves((out, operands))
    return pl.pallas_call(
        kernel,
        out_shape=out,
        in_specs=[VMEM] * len(operands),
        out_specs=jax.tree.map(lambda _: VMEM, out),
        compiler_params=PARAMS,
        cost_estimate=pl.CostEstimate(
            flops=flops,
            bytes_accessed=sum(x.size * x.dtype.itemsize for x in leaves),
            transcendentals=0,
        ),
        name=name,
        **more,
    )(*operands)


def first(part):
    rows, width = part.shape
    out = jax.ShapeDtypeStruct((rows, width // 2 + CODES), i16)
    return call(first_kernel, "first", (out, out), part)


def hop(right, left, part_right, part_left):
    rows, width = part_right.shape
    out = jax.ShapeDtypeStruct((rows, width + CODES), i16)
    return call(
        hop_kernel, "hop", (out, out), right, left, part_right, part_left,
        scratch_shapes=[pltpu.VMEM((rows, width), f32)],
    )


def meet(teacher, student, target):
    rows, width = teacher[2].shape
    logits = jax.ShapeDtypeStruct((rows, width), f32)
    stats = jax.ShapeDtypeStruct((8, 128), f32)
    return call(meet_kernel, "meet", (logits, logits, stats), *teacher, *student, target)


def payload(teacher_logits, student_logits, every, target):
    rows, width = teacher_logits.shape
    out = (
        jax.ShapeDtypeStruct((rows, width // 2), bf16),
        jax.ShapeDtypeStruct((rows, width // 2 + CODES), bf16),
    )
    return call(
        grad_kernel, "payload", out, teacher_logits, student_logits, every, target
    )


def product_kernel(own_ref, sib_ref, head_ref, head_sib_ref, *refs):
    *o_refs, held, sems = refs
    rows, width = o_refs[0].shape
    step = held.shape[3]
    strips = width // step

    def copies(i):
        strip = pl.ds(i * step, step)
        return [
            pltpu.make_async_copy(
                ref.at[:, strip], held.at[i % 2, k], sems.at[i % 2, k]
            )
            for k, ref in enumerate((head_ref, head_sib_ref))
        ]

    for copy in copies(0):
        copy.start()
    for i in range(strips):
        if i + 1 < strips:
            for copy in copies(i + 1):
                copy.start()
        for copy in copies(i):
            copy.wait()
        x = jnp.dot(own_ref[...], held[i % 2, 0], preferred_element_type=f32)
        x = x + jnp.dot(sib_ref[...], held[i % 2, 1], preferred_element_type=f32)
        for k, o_ref in enumerate(o_refs):
            o_ref[:, i * step : (i + 1) * step] = x[k * rows : (k + 1) * rows]


def product(own, sib, head, head_sib, blocks):
    tokens, depth = own.shape
    width = head.shape[1]
    out = jax.ShapeDtypeStruct((tokens // blocks, width), f32)
    anywhere = pl.BlockSpec(memory_space=pl.ANY)
    return pl.pallas_call(
        product_kernel,
        out_shape=(out,) * blocks,
        in_specs=[VMEM, VMEM, anywhere, anywhere],
        out_specs=(VMEM,) * blocks,
        scratch_shapes=[
            pltpu.VMEM((2, 2, depth, STRIP), head.dtype),
            pltpu.SemaphoreType.DMA((2, 2)),
        ],
        compiler_params=PARAMS,
        cost_estimate=pl.CostEstimate(
            flops=4 * tokens * depth * width,
            bytes_accessed=4 * depth * width + 4 * tokens * width,
            transcendentals=0,
        ),
        name="product",
    )(own, sib, head, head_sib)


def back(group, head_ref):
    depth = head_ref.shape[0] // 2
    return jnp.dot(
        group[0][...], head_ref[:depth], preferred_element_type=f32
    ) + jnp.dot(group[1][:, :depth], head_ref[depth:], preferred_element_type=f32)


def outer(hidden, groups, store):
    half = groups[0][0].shape[1]
    for side in range(2):
        for at in range(0, half, STRIP):
            total = sum(
                jnp.dot(
                    x[...],
                    group[side][:, at : at + STRIP],
                    preferred_element_type=f32,
                )
                for x, group in zip(hidden, groups)
            )
            store(side * half + at, total)


def near_kernel(head_ref, h0, h1, a0, b0, a1, b1, rows0_ref, rows1_ref, acc_ref):
    rows0_ref[...] = back((a0, b0), head_ref)
    rows1_ref[...] = back((a1, b1), head_ref)

    def store(at, total):
        acc_ref[:, at : at + STRIP] = total

    outer((h0, h1), ((a0, b0), (a1, b1)), store)


def far_kernel(
    order, place_ref, head_ref, near0, near1, acc_ref, h0, h1, a0, b0, a1, b1,
    rows_ref, o_ref,
):
    z, core = place_ref[0], place_ref[1]
    blocks, rows = rows_ref.shape[:2]
    chips = blocks // 2
    for near, group, which in (
        (near0, (a0, b0), core), (near1, (a1, b1), 1 - core)
    ):
        far = back(group, head_ref)
        count = near.shape[0] // rows
        for i, j in enumerate(order):
            x = near[i * rows : (i + 1) * rows] if i < count else (
                far[(i - count) * rows : (i - count + 1) * rows]
            )
            at = 2 * lax.rem(z + j, chips) + which
            rows_ref[pl.ds(at, 1)] = x[None]

    def store(at, total):
        o_ref[:, at : at + STRIP] = (acc_ref[:, at : at + STRIP] + total).astype(bf16)

    outer((h0, h1), ((a0, b0), (a1, b1)), store)


def near_products(head_t, hidden_t, groups):
    width, depth = head_t.shape
    rows = jax.ShapeDtypeStruct((hidden_t[0].shape[1], depth), f32)
    acc = jax.ShapeDtypeStruct((depth, width), f32)
    return call(
        near_kernel, "near", (rows, rows, acc), head_t, *hidden_t, *groups[0], *groups[1],
        flops=8 * rows.size * width,
    )


def far_products(order, place, head_t, near, hidden_t, groups, rows):
    width, depth = head_t.shape
    blocks = 2 * len(order)
    return pl.pallas_call(
        functools.partial(far_kernel, order),
        out_shape=(
            jax.ShapeDtypeStruct((blocks, rows, depth), f32),
            jax.ShapeDtypeStruct((depth, width), bf16),
        ),
        in_specs=[pl.BlockSpec(memory_space=pltpu.SMEM)] + [VMEM] * 10,
        out_specs=(VMEM, VMEM),
        compiler_params=PARAMS,
        name="far",
    )(place, head_t, *near, *hidden_t, *groups[0], *groups[1])


def spread(x, axis):
    n = lax.axis_size(axis)
    return lax.all_to_all(jnp.broadcast_to(x[None], (n,) + x.shape), axis, 0, 0)


def summed(x, axis):
    n = lax.axis_size(axis)
    blocks = x.reshape((n, x.shape[0] // n) + x.shape[1:])
    return jnp.sum(lax.all_to_all(blocks, axis, 0, 0), axis=0)


def plain(teacher_hidden, student_hidden, teacher_head, student_head, targets):
    tok_block, voc_local = targets.shape[0], teacher_head.shape[1]
    teacher_all = spread(teacher_hidden, "tensor").reshape(-1, teacher_hidden.shape[1])
    student_all = spread(student_hidden, "tensor").reshape(-1, student_hidden.shape[1])
    teacher_logits = summed(
        jnp.dot(teacher_all, teacher_head, preferred_element_type=f32), "section"
    )
    student_logits = summed(
        jnp.dot(student_all, student_head, preferred_element_type=f32), "section"
    )
    tops = jnp.stack([jnp.max(teacher_logits, axis=1), jnp.max(student_logits, axis=1)])
    teacher_max, student_max = jnp.max(spread(tops, "tensor"), axis=0)
    offset = lax.axis_index("tensor") * voc_local
    column_ids = offset + lax.broadcasted_iota(jnp.int32, (tok_block, voc_local), 1)
    onehot = (column_ids == targets[:, None]).astype(f32)
    p_terms = jnp.exp((teacher_logits - teacher_max[:, None]) / tau)
    q_terms = jnp.exp((student_logits - student_max[:, None]) / tau)
    s_terms = jnp.exp(student_logits - student_max[:, None])
    sums = jnp.stack(
        [
            jnp.sum(p_terms, axis=1),
            jnp.sum(q_terms, axis=1),
            jnp.sum(s_terms, axis=1),
            jnp.sum(p_terms * (teacher_logits - student_logits), axis=1),
            jnp.sum(onehot * student_logits, axis=1),
        ]
    )
    p_total, q_total, s_total, cross, picked = jnp.sum(spread(sums, "tensor"), axis=0)
    kl_rows = (
        cross / (tau * p_total)
        - (teacher_max - student_max) / tau
        - jnp.log(p_total)
        + jnp.log(q_total)
    )
    row_loss = tau * tau * kl_rows + student_max + jnp.log(s_total) - picked
    loss = jnp.mean(spread(row_loss, "section"))
    p_prob = p_terms / p_total[:, None]
    q_prob = q_terms / q_total[:, None]
    s_prob = s_terms / s_total[:, None]
    grad = (tau * (q_prob - p_prob) + s_prob - onehot).astype(bf16)
    grad = spread(grad, "section").reshape(-1, voc_local)
    grad_head = lax.dot_general(
        student_all, grad, (((0,), (0,)), ((), ())), preferred_element_type=f32
    )
    rows = lax.dot_general(
        grad, student_head, (((1,), (1,)), ((), ())), preferred_element_type=f32
    )
    return loss, summed(rows, "tensor").astype(bf16), grad_head.astype(bf16)


def steps(teacher_hidden, student_hidden, teacher_head, student_head, targets):
    section_size = lax.axis_size("section")
    chips = section_size // 2
    half_way = chips // 2
    me = lax.axis_index("section")
    z, core = me // 2, me % 2
    tok_block, dt = teacher_hidden.shape
    ds = student_hidden.shape[1]
    voc_local = teacher_head.shape[1]
    half = voc_local // 2

    def along(x, step):
        perm = [
            (s, ((s // 2 + step) % chips) * 2 + s % 2) for s in range(section_size)
        ]
        return lax.ppermute(x, "section", perm)

    def swap(x):
        return lax.ppermute(x, "section", [(s, s ^ 1) for s in range(section_size)])

    student_head_sib = swap(student_head)
    teacher_head_sib = swap(teacher_head)
    hidden = spread(jnp.concatenate([teacher_hidden, student_hidden], axis=1), "tensor")

    start = chips - half_way + 2
    order = [(start + i) % chips for i in range(chips)]
    count = chips - 3

    def rolled(x, which):
        pair = x.reshape((chips, 2) + x.shape[1:])
        twice = jnp.concatenate([pair, pair], axis=0)
        out = lax.dynamic_slice(
            twice, ((z + start) % chips, which, 0, 0), (chips, 1) + x.shape[1:]
        )
        return out.reshape((chips * x.shape[1],) + x.shape[2:])

    mine, others = rolled(hidden, core), rolled(hidden, 1 - core)
    mine_sib = swap(others)
    student_part = product(
        mine[:, dt:], mine_sib[:, dt:], student_head, student_head_sib, chips
    )
    teacher_part = product(
        mine[:, :dt], mine_sib[:, :dt], teacher_head, teacher_head_sib, chips
    )

    place = jnp.stack([z, core]).astype(jnp.int32)
    split = count * tok_block
    near_t = [x[:split, dt:].T for x in (mine, others)]
    far_t = [x[split:, dt:].T for x in (mine, others)]

    def ring(parts, meanwhile):
        parts = dict(zip(order, parts))
        right, left = first(parts[half_way])
        right, left = along(right, 1), along(left, -1)
        for step in range(1, half_way):
            right, left = hop(
                right, left, parts[half_way - step], parts[half_way + step]
            )
            if step in meanwhile:
                right, left, meanwhile[step] = lax.optimization_barrier(
                    (right, left, meanwhile[step])
                )
            right, left = along(right, 1), along(left, -1)
        return (right, left, parts[0]), meanwhile

    offset = lax.axis_index("tensor") * voc_local
    target_here = jnp.broadcast_to((targets - offset)[:, None], (tok_block, 128))

    student, made = ring(student_part, {half_way - 2: student_head.T})
    head_t = made[half_way - 2]
    teacher, made = ring(teacher_part, {half_way - 2: near_t, half_way - 1: far_t})
    near_t, far_t = made[half_way - 2], made[half_way - 1]
    teacher_logits, student_logits, stats = meet(teacher, student, target_here)
    own = payload(teacher_logits, student_logits, spread(stats, "tensor"), target_here)

    pieces = [[None] * chips, [None] * chips]
    right, left = list(own), list(own)
    pieces[0][0], pieces[1][0] = own
    for step in range(1, half_way):
        for side in range(2):
            right[side] = along(right[side], 1)
            left[side] = along(left[side], -1)
            pieces[side][chips - step], pieces[side][step] = right[side], left[side]

    def gathered(js):
        group = [jnp.concatenate([x[j] for j in js], axis=0) for x in pieces]
        return group, [swap(x) for x in group]

    last = along(right[0], 1), along(left[1], -1)
    pieces = lax.optimization_barrier(pieces)
    near = gathered(order[:count])
    sums = near_products(head_t, near_t, near)
    pieces[0][half_way], pieces[1][half_way], sums = lax.optimization_barrier(
        (*last, sums)
    )
    far = gathered(order[count:])
    rows, grad_head = far_products(
        order, place, head_t, sums, far_t, far, tok_block
    )
    rows, grad_head = lax.optimization_barrier((rows, grad_head))
    extra = sum(
        jnp.sum(g[1][:, half:].astype(f32), axis=0) for group in (near, far) for g in group
    )
    loss = (extra[0] + extra[1] + extra[2]) / (tok_block * section_size)
    grad_hidden = jnp.sum(lax.all_to_all(rows, "tensor", 0, 0), axis=0).astype(bf16)
    return (loss, grad_hidden, grad_head), extra[3]


def shards(*arrays):
    fine, too_coarse = steps(*arrays)
    return lax.cond(too_coarse > 0.0, lambda: plain(*arrays), lambda: fine)


def solution(mesh):
    placed = (
        P("tensor", "section"),
        P("tensor", "section"),
        P("section", "tensor"),
        P("section", "tensor"),
        P("section"),
    )
    return jax.shard_map(
        shards,
        mesh=mesh,
        in_specs=placed,
        out_specs=(P(), P("tensor", "section"), P("section", "tensor")),
        check_vma=False,
    )
```

```python
import functools

import jax
import jax.numpy as jnp
from jax import lax
from jax.experimental import pallas as pl
from jax.experimental.pallas import tpu as pltpu
from jax.sharding import PartitionSpec as P

tau = 2.0
f32 = jnp.float32
bf16 = jnp.bfloat16
i16 = jnp.int16

LEVELS = 32767.0
CODES = 128
LIMIT = 1000.0
STRIP = 512
PARAMS = pltpu.CompilerParams(vmem_limit_bytes=20 * 1024 * 1024)


def row_codes(ref):
    w = ref.shape[1] - CODES
    codes = ref[:, w:].astype(jnp.int32).astype(f32)
    middle = codes[:, 0:1] * 0.25
    scale = codes[:, 32:33] * (0.5 / LEVELS)
    return middle, scale, codes[:, 64:65]


def encode(x_ref, columns, o_ref, spent):
    lo, hi = columns
    top = bottom = None
    for at in range(lo, hi, STRIP):
        x = x_ref[:, at : at + STRIP]
        top = x if top is None else jnp.maximum(top, x)
        bottom = x if bottom is None else jnp.minimum(bottom, x)
    top = jnp.max(top, axis=1, keepdims=True)
    bottom = jnp.min(bottom, axis=1, keepdims=True)
    middle_code = jnp.round((top + bottom) * 2.0)
    middle = middle_code * 0.25
    reach = jnp.maximum(top - middle, middle - bottom)
    reach_code = jnp.floor(reach * 2.0) + 1.0
    spent_code = jnp.minimum(spent + reach_code, LEVELS)
    inverse = (2.0 * LEVELS) / reach_code
    for at in range(lo, hi, STRIP):
        code = jnp.round((x_ref[:, at : at + STRIP] - middle) * inverse)
        o_ref[:, at - lo : at - lo + STRIP] = code.astype(jnp.int32).astype(i16)
    lane = lax.broadcasted_iota(jnp.int32, (x_ref.shape[0], CODES), 1)
    codes = jnp.where(lane < 32, middle_code, jnp.where(lane < 64, reach_code, spent_code))
    o_ref[:, hi - lo :] = codes.astype(jnp.int32).astype(i16)


def first_kernel(part_ref, right_ref, left_ref):
    rows, width = part_ref.shape
    none = jnp.zeros((rows, 1), f32)
    encode(part_ref, (0, width // 2), right_ref, none)
    encode(part_ref, (width // 2, width), left_ref, none)


def hop_kernel(r_ref, l_ref, pr_ref, pl_ref, ro_ref, lo_ref, sum_ref):
    width = pr_ref.shape[1]
    for in_ref, part_ref, out_ref, at_end in (
        (r_ref, pr_ref, ro_ref, False),
        (l_ref, pl_ref, lo_ref, True),
    ):
        carried = in_ref.shape[1] - CODES
        start = width - carried if at_end else 0
        middle, scale, spent = row_codes(in_ref)
        for at in range(0, width, STRIP):
            x = part_ref[:, at : at + STRIP]
            if start <= at < start + carried:
                code = in_ref[:, at - start : at - start + STRIP]
                x = x + (middle + code.astype(jnp.int32).astype(f32) * scale)
            sum_ref[:, at : at + STRIP] = x
        encode(sum_ref, (0, width), out_ref, spent)


def meet_kernel(
    rt_ref, lt_ref, pt_ref, rs_ref, ls_ref, ps_ref, target_ref, t_ref, s_ref, stats_ref
):
    rows, width = t_ref.shape
    tops, spents = [], []
    for r_ref, l_ref, part_ref, out_ref in (
        (rt_ref, lt_ref, pt_ref, t_ref),
        (rs_ref, ls_ref, ps_ref, s_ref),
    ):
        r_middle, r_scale, r_spent = row_codes(r_ref)
        l_middle, l_scale, l_spent = row_codes(l_ref)
        top = None
        for at in range(0, width, STRIP):
            strip = slice(at, at + STRIP)
            x = (
                part_ref[:, strip]
                + (r_middle + r_ref[:, strip].astype(jnp.int32).astype(f32) * r_scale)
                + (l_middle + l_ref[:, strip].astype(jnp.int32).astype(f32) * l_scale)
            )
            out_ref[:, strip] = x
            top = x if top is None else jnp.maximum(top, x)
        tops.append(jnp.max(top, axis=1, keepdims=True))
        spents.append((r_spent + l_spent) * 0.5)
    t_max, s_max = tops
    target = target_ref[:, 0:1]
    sums = None
    for at in range(0, width, 128):
        t, s = t_ref[:, at : at + 128], s_ref[:, at : at + 128]
        p = jnp.exp((t - t_max) * (1.0 / tau))
        q = jnp.exp((s - s_max) * (1.0 / tau))
        ids = at + lax.broadcasted_iota(jnp.int32, t.shape, 1)
        terms = (p, q, q * q, p * (t - s), jnp.where(ids == target, s, 0.0))
        sums = terms if sums is None else [a + b for a, b in zip(sums, terms)]
    lane = lax.broadcasted_iota(jnp.int32, (rows, 128), 1)
    kinds = [t_max, s_max] + [jnp.sum(a, axis=1, keepdims=True) for a in sums]
    kinds.append(jnp.maximum(spents[0], spents[1]))
    table = jnp.zeros((rows, 128), f32)
    for k, value in enumerate(kinds):
        table = jnp.where(lane == k, value, table)
    table = jnp.concatenate([table, jnp.zeros((128 - rows, 128), f32)], axis=0)
    stats_ref[...] = table.T[0:8, :]


def grad_kernel(t_ref, s_ref, every_ref, target_ref, a_ref, b_ref):
    rows, width = t_ref.shape
    t_tops, s_tops = every_ref[:, 0, :], every_ref[:, 1, :]
    t_max = jnp.max(t_tops, axis=0, keepdims=True)
    s_max = jnp.max(s_tops, axis=0, keepdims=True)
    t_weight = jnp.exp((t_tops - t_max) * (1.0 / tau))
    q_weight = jnp.exp((s_tops - s_max) * (1.0 / tau))
    s_weight = jnp.exp(s_tops - s_max)

    def total(k, weight):
        return jnp.sum(every_ref[:, k, :] * weight, axis=0, keepdims=True)

    p_total, q_total = total(2, t_weight), total(3, q_weight)
    s_total, cross = total(4, s_weight), total(5, t_weight)
    picked = jnp.sum(every_ref[:, 6, :], axis=0, keepdims=True)
    spent = jnp.max(every_ref[:, 7, :], axis=0, keepdims=True)
    kl_rows = (
        cross / (tau * p_total)
        - (t_max - s_max) / tau
        - jnp.log(p_total)
        + jnp.log(q_total)
    )
    row_loss = tau * tau * kl_rows + s_max + jnp.log(s_total) - picked
    flag = jnp.where(spent > LIMIT, 1.0, 0.0)
    lines = [t_max, s_max, tau / p_total, tau / q_total, 1.0 / s_total, row_loss, flag]
    lines.append(jnp.zeros((128 - len(lines), 128), f32))
    table = jnp.concatenate(lines, axis=0).T[:rows]
    t_max, s_max, p_scale, q_scale, s_scale, row_loss, flag = (
        table[:, k : k + 1] for k in range(7)
    )
    target = target_ref[:, 0:1]
    for at in range(0, width, STRIP):
        t, s = t_ref[:, at : at + STRIP], s_ref[:, at : at + STRIP]
        p = jnp.exp((t - t_max) * (1.0 / tau))
        q = jnp.exp((s - s_max) * (1.0 / tau))
        ids = at + lax.broadcasted_iota(jnp.int32, t.shape, 1)
        grad = q * q_scale - p * p_scale + (q * q) * s_scale
        grad = grad - jnp.where(ids == target, 1.0, 0.0)
        o_ref, to = (a_ref, at) if at < width // 2 else (b_ref, at - width // 2)
        o_ref[:, to : to + STRIP] = grad.astype(bf16)
    high = row_loss.astype(bf16).astype(f32)
    mid = (row_loss - high).astype(bf16).astype(f32)
    low = row_loss - high - mid
    lane = lax.broadcasted_iota(jnp.int32, (rows, CODES), 1)
    extra = jnp.where(
        lane == 0,
        high,
        jnp.where(lane == 1, mid, jnp.where(lane == 2, low, jnp.where(lane == 3, flag, 0.0))),
    )
    b_ref[:, width // 2 :] = extra.astype(bf16)


VMEM = pl.BlockSpec(memory_space=pltpu.VMEM)


def call(kernel, name, out, *operands, flops=0, **more):
    leaves = jax.tree.leaves((out, operands))
    return pl.pallas_call(
        kernel,
        out_shape=out,
        in_specs=[VMEM] * len(operands),
        out_specs=jax.tree.map(lambda _: VMEM, out),
        compiler_params=PARAMS,
        cost_estimate=pl.CostEstimate(
            flops=flops,
            bytes_accessed=sum(x.size * x.dtype.itemsize for x in leaves),
            transcendentals=0,
        ),
        name=name,
        **more,
    )(*operands)


def first(part):
    rows, width = part.shape
    out = jax.ShapeDtypeStruct((rows, width // 2 + CODES), i16)
    return call(first_kernel, "first", (out, out), part)


def hop(right, left, part_right, part_left):
    rows, width = part_right.shape
    out = jax.ShapeDtypeStruct((rows, width + CODES), i16)
    return call(
        hop_kernel, "hop", (out, out), right, left, part_right, part_left,
        scratch_shapes=[pltpu.VMEM((rows, width), f32)],
    )


def meet(teacher, student, target):
    rows, width = teacher[2].shape
    logits = jax.ShapeDtypeStruct((rows, width), f32)
    stats = jax.ShapeDtypeStruct((8, 128), f32)
    return call(meet_kernel, "meet", (logits, logits, stats), *teacher, *student, target)


def payload(teacher_logits, student_logits, every, target):
    rows, width = teacher_logits.shape
    out = (
        jax.ShapeDtypeStruct((rows, width // 2), bf16),
        jax.ShapeDtypeStruct((rows, width // 2 + CODES), bf16),
    )
    return call(
        grad_kernel, "payload", out, teacher_logits, student_logits, every, target
    )


def product_kernel(own_ref, sib_ref, head_ref, head_sib_ref, *o_refs):
    rows, width = o_refs[0].shape
    step = min(width, 2 * STRIP)
    for at in range(0, width, step):
        strip = slice(at, at + step)
        x = jnp.dot(own_ref[...], head_ref[:, strip], preferred_element_type=f32)
        x = x + jnp.dot(sib_ref[...], head_sib_ref[:, strip], preferred_element_type=f32)
        for k, o_ref in enumerate(o_refs):
            o_ref[:, strip] = x[k * rows : (k + 1) * rows]


def product(own, sib, head, head_sib, blocks):
    tokens, depth = own.shape
    width = head.shape[1]
    out = jax.ShapeDtypeStruct((tokens // blocks, width), f32)
    return call(
        product_kernel, "product", (out,) * blocks, own, sib, head, head_sib,
        flops=4 * tokens * depth * width,
    )


def back(group, head_ref):
    depth = head_ref.shape[1] // 2
    turned = (((1,), (1,)), ((), ()))
    return lax.dot_general(
        group[0][...], head_ref[:, :depth], turned, preferred_element_type=f32
    ) + lax.dot_general(
        group[1][:, :depth], head_ref[:, depth:], turned, preferred_element_type=f32
    )


def outer(hidden, groups, store):
    half = groups[0][0].shape[1]
    for side in range(2):
        for at in range(0, half, STRIP):
            total = sum(
                lax.dot_general(
                    x[...],
                    group[side][:, at : at + STRIP],
                    (((0,), (0,)), ((), ())),
                    preferred_element_type=f32,
                )
                for x, group in zip(hidden, groups)
            )
            store(side * half + at, total)


def near_kernel(head_ref, h0, h1, a0, b0, a1, b1, rows0_ref, rows1_ref, acc_ref):
    rows0_ref[...] = back((a0, b0), head_ref)
    rows1_ref[...] = back((a1, b1), head_ref)

    def store(at, total):
        acc_ref[:, at : at + STRIP] = total

    outer((h0, h1), ((a0, b0), (a1, b1)), store)


def far_kernel(
    order, place_ref, head_ref, near0, near1, acc_ref, h0, h1, a0, b0, a1, b1,
    rows_ref, o_ref,
):
    z, core = place_ref[0], place_ref[1]
    blocks, rows = rows_ref.shape[:2]
    chips = blocks // 2
    for near, group, which in (
        (near0, (a0, b0), core), (near1, (a1, b1), 1 - core)
    ):
        far = back(group, head_ref)
        count = near.shape[0] // rows
        for i, j in enumerate(order):
            x = near[i * rows : (i + 1) * rows] if i < count else (
                far[(i - count) * rows : (i - count + 1) * rows]
            )
            at = 2 * lax.rem(z + j, chips) + which
            rows_ref[pl.ds(at, 1)] = x[None]

    def store(at, total):
        o_ref[:, at : at + STRIP] = (acc_ref[:, at : at + STRIP] + total).astype(bf16)

    outer((h0, h1), ((a0, b0), (a1, b1)), store)


def near_products(head, hidden, groups):
    depth, width = head.shape
    rows = jax.ShapeDtypeStruct((hidden[0].shape[0], depth), f32)
    acc = jax.ShapeDtypeStruct((depth, width), f32)
    return call(
        near_kernel, "near", (rows, rows, acc), head, *hidden, *groups[0], *groups[1],
        flops=8 * rows.size * width,
    )


def far_products(order, place, head, near, hidden, groups, rows):
    depth, width = head.shape
    blocks = 2 * len(order)
    return pl.pallas_call(
        functools.partial(far_kernel, order),
        out_shape=(
            jax.ShapeDtypeStruct((blocks, rows, depth), f32),
            jax.ShapeDtypeStruct((depth, width), bf16),
        ),
        in_specs=[pl.BlockSpec(memory_space=pltpu.SMEM)] + [VMEM] * 10,
        out_specs=(VMEM, VMEM),
        compiler_params=PARAMS,
        name="far",
    )(place, head, *near, *hidden, *groups[0], *groups[1])


def spread(x, axis):
    n = lax.axis_size(axis)
    return lax.all_to_all(jnp.broadcast_to(x[None], (n,) + x.shape), axis, 0, 0)


def summed(x, axis):
    n = lax.axis_size(axis)
    blocks = x.reshape((n, x.shape[0] // n) + x.shape[1:])
    return jnp.sum(lax.all_to_all(blocks, axis, 0, 0), axis=0)


def plain(teacher_hidden, student_hidden, teacher_head, student_head, targets):
    tok_block, voc_local = targets.shape[0], teacher_head.shape[1]
    teacher_all = spread(teacher_hidden, "tensor").reshape(-1, teacher_hidden.shape[1])
    student_all = spread(student_hidden, "tensor").reshape(-1, student_hidden.shape[1])
    teacher_logits = summed(
        jnp.dot(teacher_all, teacher_head, preferred_element_type=f32), "section"
    )
    student_logits = summed(
        jnp.dot(student_all, student_head, preferred_element_type=f32), "section"
    )
    tops = jnp.stack([jnp.max(teacher_logits, axis=1), jnp.max(student_logits, axis=1)])
    teacher_max, student_max = jnp.max(spread(tops, "tensor"), axis=0)
    offset = lax.axis_index("tensor") * voc_local
    column_ids = offset + lax.broadcasted_iota(jnp.int32, (tok_block, voc_local), 1)
    onehot = (column_ids == targets[:, None]).astype(f32)
    p_terms = jnp.exp((teacher_logits - teacher_max[:, None]) / tau)
    q_terms = jnp.exp((student_logits - student_max[:, None]) / tau)
    s_terms = jnp.exp(student_logits - student_max[:, None])
    sums = jnp.stack(
        [
            jnp.sum(p_terms, axis=1),
            jnp.sum(q_terms, axis=1),
            jnp.sum(s_terms, axis=1),
            jnp.sum(p_terms * (teacher_logits - student_logits), axis=1),
            jnp.sum(onehot * student_logits, axis=1),
        ]
    )
    p_total, q_total, s_total, cross, picked = jnp.sum(spread(sums, "tensor"), axis=0)
    kl_rows = (
        cross / (tau * p_total)
        - (teacher_max - student_max) / tau
        - jnp.log(p_total)
        + jnp.log(q_total)
    )
    row_loss = tau * tau * kl_rows + student_max + jnp.log(s_total) - picked
    loss = jnp.mean(spread(row_loss, "section"))
    p_prob = p_terms / p_total[:, None]
    q_prob = q_terms / q_total[:, None]
    s_prob = s_terms / s_total[:, None]
    grad = (tau * (q_prob - p_prob) + s_prob - onehot).astype(bf16)
    grad = spread(grad, "section").reshape(-1, voc_local)
    grad_head = lax.dot_general(
        student_all, grad, (((0,), (0,)), ((), ())), preferred_element_type=f32
    )
    rows = lax.dot_general(
        grad, student_head, (((1,), (1,)), ((), ())), preferred_element_type=f32
    )
    return loss, summed(rows, "tensor").astype(bf16), grad_head.astype(bf16)


def steps(teacher_hidden, student_hidden, teacher_head, student_head, targets):
    section_size = lax.axis_size("section")
    chips = section_size // 2
    half_way = chips // 2
    me = lax.axis_index("section")
    z, core = me // 2, me % 2
    tok_block, dt = teacher_hidden.shape
    ds = student_hidden.shape[1]
    voc_local = teacher_head.shape[1]
    half = voc_local // 2

    def along(x, step):
        perm = [
            (s, ((s // 2 + step) % chips) * 2 + s % 2) for s in range(section_size)
        ]
        return lax.ppermute(x, "section", perm)

    def swap(x):
        return lax.ppermute(x, "section", [(s, s ^ 1) for s in range(section_size)])

    student_head_sib = swap(student_head)
    teacher_head_sib = swap(teacher_head)
    hidden = spread(jnp.concatenate([teacher_hidden, student_hidden], axis=1), "tensor")

    start = chips - half_way + 2
    order = [(start + i) % chips for i in range(chips)]
    count = chips - 3

    def rolled(x, which):
        pair = x.reshape((chips, 2) + x.shape[1:])
        twice = jnp.concatenate([pair, pair], axis=0)
        out = lax.dynamic_slice(
            twice, ((z + start) % chips, which, 0, 0), (chips, 1) + x.shape[1:]
        )
        return out.reshape((chips * x.shape[1],) + x.shape[2:])

    mine, others = rolled(hidden, core), rolled(hidden, 1 - core)
    mine_sib = swap(others)
    student_part = product(
        mine[:, dt:], mine_sib[:, dt:], student_head, student_head_sib, chips
    )
    teacher_part = product(
        mine[:, :dt], mine_sib[:, :dt], teacher_head, teacher_head_sib, chips
    )

    place = jnp.stack([z, core]).astype(jnp.int32)
    split = count * tok_block
    hidden_near = (mine[:split, dt:], others[:split, dt:])
    hidden_far = (mine[split:, dt:], others[split:, dt:])

    def ring(parts, meanwhile=()):
        parts = dict(zip(order, parts))
        right, left = first(parts[half_way])
        right, left = along(right, 1), along(left, -1)
        for step in range(1, half_way):
            right, left = hop(
                right, left, parts[half_way - step], parts[half_way + step]
            )
            if step == half_way - 1:
                right, left, meanwhile = lax.optimization_barrier((right, left, meanwhile))
            right, left = along(right, 1), along(left, -1)
        return (right, left, parts[0]), meanwhile

    offset = lax.axis_index("tensor") * voc_local
    target_here = jnp.broadcast_to((targets - offset)[:, None], (tok_block, 128))

    student, _ = ring(student_part)
    teacher, (hidden_near, hidden_far) = ring(teacher_part, (hidden_near, hidden_far))
    teacher_logits, student_logits, stats = meet(teacher, student, target_here)
    own = payload(teacher_logits, student_logits, spread(stats, "tensor"), target_here)

    pieces = [[None] * chips, [None] * chips]
    right, left = list(own), list(own)
    pieces[0][0], pieces[1][0] = own
    for step in range(1, half_way):
        for side in range(2):
            right[side] = along(right[side], 1)
            left[side] = along(left[side], -1)
            pieces[side][chips - step], pieces[side][step] = right[side], left[side]

    def gathered(js):
        group = [jnp.concatenate([x[j] for j in js], axis=0) for x in pieces]
        return group, [swap(x) for x in group]

    last = along(right[0], 1), along(left[1], -1)
    early = {j: [x[j] for x in pieces] for j in order[:count]}
    early, right[1] = lax.optimization_barrier((early, right[1]))
    pieces[1][order[-1]] = right[1]
    for j, pair in early.items():
        pieces[0][j], pieces[1][j] = pair
    near = gathered(order[:count])
    sums = near_products(student_head, hidden_near, near)
    pieces[0][half_way], pieces[1][half_way], sums = lax.optimization_barrier(
        (*last, sums)
    )
    far = gathered(order[count:])
    rows, grad_head = far_products(
        order, place, student_head, sums, hidden_far, far, tok_block
    )
    rows, grad_head = lax.optimization_barrier((rows, grad_head))
    extra = sum(
        jnp.sum(g[1][:, half:].astype(f32), axis=0) for group in (near, far) for g in group
    )
    loss = (extra[0] + extra[1] + extra[2]) / (tok_block * section_size)
    grad_hidden = jnp.sum(lax.all_to_all(rows, "tensor", 0, 0), axis=0).astype(bf16)
    return (loss, grad_hidden, grad_head), extra[3]


def shards(*arrays):
    fine, too_coarse = steps(*arrays)
    return lax.cond(too_coarse > 0.0, lambda: plain(*arrays), lambda: fine)


def solution(mesh):
    placed = (
        P("tensor", "section"),
        P("tensor", "section"),
        P("section", "tensor"),
        P("section", "tensor"),
        P("section"),
    )
    return jax.shard_map(
        shards,
        mesh=mesh,
        in_specs=placed,
        out_specs=(P(), P("tensor", "section"), P("section", "tensor")),
        check_vma=False,
    )
```

```python
import functools

import jax
import jax.numpy as jnp
from jax import lax
from jax.experimental import pallas as pl
from jax.experimental.pallas import tpu as pltpu
from jax.sharding import PartitionSpec as P

tau = 2.0
f32 = jnp.float32
bf16 = jnp.bfloat16
i16 = jnp.int16

LEVELS = 32767.0
CODES = 128
LIMIT = 1000.0
STRIP = 512
PARAMS = pltpu.CompilerParams(vmem_limit_bytes=20 * 1024 * 1024)


def row_codes(ref):
    w = ref.shape[1] - CODES
    codes = ref[:, w:].astype(jnp.int32).astype(f32)
    middle = codes[:, 0:1] * 0.25
    scale = codes[:, 32:33] * (0.5 / LEVELS)
    return middle, scale, codes[:, 64:65]


def encode(x_ref, columns, o_ref, spent):
    lo, hi = columns
    top = bottom = None
    for at in range(lo, hi, STRIP):
        x = x_ref[:, at : at + STRIP]
        top = x if top is None else jnp.maximum(top, x)
        bottom = x if bottom is None else jnp.minimum(bottom, x)
    top = jnp.max(top, axis=1, keepdims=True)
    bottom = jnp.min(bottom, axis=1, keepdims=True)
    middle_code = jnp.round((top + bottom) * 2.0)
    middle = middle_code * 0.25
    reach = jnp.maximum(top - middle, middle - bottom)
    reach_code = jnp.floor(reach * 2.0) + 1.0
    spent_code = jnp.minimum(spent + reach_code, LEVELS)
    inverse = (2.0 * LEVELS) / reach_code
    for at in range(lo, hi, STRIP):
        code = jnp.round((x_ref[:, at : at + STRIP] - middle) * inverse)
        o_ref[:, at - lo : at - lo + STRIP] = code.astype(jnp.int32).astype(i16)
    lane = lax.broadcasted_iota(jnp.int32, (x_ref.shape[0], CODES), 1)
    codes = jnp.where(lane < 32, middle_code, jnp.where(lane < 64, reach_code, spent_code))
    o_ref[:, hi - lo :] = codes.astype(jnp.int32).astype(i16)


def first_kernel(part_ref, right_ref, left_ref):
    rows, width = part_ref.shape
    none = jnp.zeros((rows, 1), f32)
    encode(part_ref, (0, width // 2), right_ref, none)
    encode(part_ref, (width // 2, width), left_ref, none)


def hop_kernel(r_ref, l_ref, pr_ref, pl_ref, ro_ref, lo_ref, sum_ref):
    width = pr_ref.shape[1]
    for in_ref, part_ref, out_ref, at_end in (
        (r_ref, pr_ref, ro_ref, False),
        (l_ref, pl_ref, lo_ref, True),
    ):
        carried = in_ref.shape[1] - CODES
        start = width - carried if at_end else 0
        middle, scale, spent = row_codes(in_ref)
        for at in range(0, width, STRIP):
            x = part_ref[:, at : at + STRIP]
            if start <= at < start + carried:
                code = in_ref[:, at - start : at - start + STRIP]
                x = x + (middle + code.astype(jnp.int32).astype(f32) * scale)
            sum_ref[:, at : at + STRIP] = x
        encode(sum_ref, (0, width), out_ref, spent)


def meet_kernel(
    rt_ref, lt_ref, pt_ref, rs_ref, ls_ref, ps_ref, target_ref, t_ref, s_ref, stats_ref
):
    rows, width = t_ref.shape
    tops, spents = [], []
    for r_ref, l_ref, part_ref, out_ref in (
        (rt_ref, lt_ref, pt_ref, t_ref),
        (rs_ref, ls_ref, ps_ref, s_ref),
    ):
        r_middle, r_scale, r_spent = row_codes(r_ref)
        l_middle, l_scale, l_spent = row_codes(l_ref)
        top = None
        for at in range(0, width, STRIP):
            strip = slice(at, at + STRIP)
            x = (
                part_ref[:, strip]
                + (r_middle + r_ref[:, strip].astype(jnp.int32).astype(f32) * r_scale)
                + (l_middle + l_ref[:, strip].astype(jnp.int32).astype(f32) * l_scale)
            )
            out_ref[:, strip] = x
            top = x if top is None else jnp.maximum(top, x)
        tops.append(jnp.max(top, axis=1, keepdims=True))
        spents.append((r_spent + l_spent) * 0.5)
    t_max, s_max = tops
    target = target_ref[:, 0:1]
    sums = None
    for at in range(0, width, 128):
        t, s = t_ref[:, at : at + 128], s_ref[:, at : at + 128]
        p = jnp.exp((t - t_max) * (1.0 / tau))
        q = jnp.exp((s - s_max) * (1.0 / tau))
        ids = at + lax.broadcasted_iota(jnp.int32, t.shape, 1)
        terms = (p, q, q * q, p * (t - s), jnp.where(ids == target, s, 0.0))
        sums = terms if sums is None else [a + b for a, b in zip(sums, terms)]
    lane = lax.broadcasted_iota(jnp.int32, (rows, 128), 1)
    kinds = [t_max, s_max] + [jnp.sum(a, axis=1, keepdims=True) for a in sums]
    kinds.append(jnp.maximum(spents[0], spents[1]))
    table = jnp.zeros((rows, 128), f32)
    for k, value in enumerate(kinds):
        table = jnp.where(lane == k, value, table)
    table = jnp.concatenate([table, jnp.zeros((128 - rows, 128), f32)], axis=0)
    stats_ref[...] = table.T[0:8, :]


def grad_kernel(t_ref, s_ref, every_ref, target_ref, a_ref, b_ref):
    rows, width = t_ref.shape
    t_tops, s_tops = every_ref[:, 0, :], every_ref[:, 1, :]
    t_max = jnp.max(t_tops, axis=0, keepdims=True)
    s_max = jnp.max(s_tops, axis=0, keepdims=True)
    t_weight = jnp.exp((t_tops - t_max) * (1.0 / tau))
    q_weight = jnp.exp((s_tops - s_max) * (1.0 / tau))
    s_weight = jnp.exp(s_tops - s_max)

    def total(k, weight):
        return jnp.sum(every_ref[:, k, :] * weight, axis=0, keepdims=True)

    p_total, q_total = total(2, t_weight), total(3, q_weight)
    s_total, cross = total(4, s_weight), total(5, t_weight)
    picked = jnp.sum(every_ref[:, 6, :], axis=0, keepdims=True)
    spent = jnp.max(every_ref[:, 7, :], axis=0, keepdims=True)
    kl_rows = (
        cross / (tau * p_total)
        - (t_max - s_max) / tau
        - jnp.log(p_total)
        + jnp.log(q_total)
    )
    row_loss = tau * tau * kl_rows + s_max + jnp.log(s_total) - picked
    flag = jnp.where(spent > LIMIT, 1.0, 0.0)
    lines = [t_max, s_max, tau / p_total, tau / q_total, 1.0 / s_total, row_loss, flag]
    lines.append(jnp.zeros((128 - len(lines), 128), f32))
    table = jnp.concatenate(lines, axis=0).T[:rows]
    t_max, s_max, p_scale, q_scale, s_scale, row_loss, flag = (
        table[:, k : k + 1] for k in range(7)
    )
    target = target_ref[:, 0:1]
    for at in range(0, width, STRIP):
        t, s = t_ref[:, at : at + STRIP], s_ref[:, at : at + STRIP]
        p = jnp.exp((t - t_max) * (1.0 / tau))
        q = jnp.exp((s - s_max) * (1.0 / tau))
        ids = at + lax.broadcasted_iota(jnp.int32, t.shape, 1)
        grad = q * q_scale - p * p_scale + (q * q) * s_scale
        grad = grad - jnp.where(ids == target, 1.0, 0.0)
        o_ref, to = (a_ref, at) if at < width // 2 else (b_ref, at - width // 2)
        o_ref[:, to : to + STRIP] = grad.astype(bf16)
    high = row_loss.astype(bf16).astype(f32)
    mid = (row_loss - high).astype(bf16).astype(f32)
    low = row_loss - high - mid
    lane = lax.broadcasted_iota(jnp.int32, (rows, CODES), 1)
    extra = jnp.where(
        lane == 0,
        high,
        jnp.where(lane == 1, mid, jnp.where(lane == 2, low, jnp.where(lane == 3, flag, 0.0))),
    )
    b_ref[:, width // 2 :] = extra.astype(bf16)


VMEM = pl.BlockSpec(memory_space=pltpu.VMEM)


def call(kernel, name, out, *operands, flops=0, **more):
    leaves = jax.tree.leaves((out, operands))
    return pl.pallas_call(
        kernel,
        out_shape=out,
        in_specs=[VMEM] * len(operands),
        out_specs=jax.tree.map(lambda _: VMEM, out),
        compiler_params=PARAMS,
        cost_estimate=pl.CostEstimate(
            flops=flops,
            bytes_accessed=sum(x.size * x.dtype.itemsize for x in leaves),
            transcendentals=0,
        ),
        name=name,
        **more,
    )(*operands)


def first(part):
    rows, width = part.shape
    out = jax.ShapeDtypeStruct((rows, width // 2 + CODES), i16)
    return call(first_kernel, "first", (out, out), part)


def hop(right, left, part_right, part_left):
    rows, width = part_right.shape
    out = jax.ShapeDtypeStruct((rows, width + CODES), i16)
    return call(
        hop_kernel, "hop", (out, out), right, left, part_right, part_left,
        scratch_shapes=[pltpu.VMEM((rows, width), f32)],
    )


def meet(teacher, student, target):
    rows, width = teacher[2].shape
    logits = jax.ShapeDtypeStruct((rows, width), f32)
    stats = jax.ShapeDtypeStruct((8, 128), f32)
    return call(meet_kernel, "meet", (logits, logits, stats), *teacher, *student, target)


def payload(teacher_logits, student_logits, every, target):
    rows, width = teacher_logits.shape
    out = (
        jax.ShapeDtypeStruct((rows, width // 2), bf16),
        jax.ShapeDtypeStruct((rows, width // 2 + CODES), bf16),
    )
    return call(
        grad_kernel, "payload", out, teacher_logits, student_logits, every, target
    )


def product_kernel(own_ref, sib_ref, head_ref, head_sib_ref, *o_refs):
    rows, width = o_refs[0].shape
    step = min(width, 2 * STRIP)
    for at in range(0, width, step):
        strip = slice(at, at + step)
        x = jnp.dot(own_ref[...], head_ref[:, strip], preferred_element_type=f32)
        x = x + jnp.dot(sib_ref[...], head_sib_ref[:, strip], preferred_element_type=f32)
        for k, o_ref in enumerate(o_refs):
            o_ref[:, strip] = x[k * rows : (k + 1) * rows]


def product(own, sib, head, head_sib, blocks):
    tokens, depth = own.shape
    width = head.shape[1]
    out = jax.ShapeDtypeStruct((tokens // blocks, width), f32)
    return call(
        product_kernel, "product", (out,) * blocks, own, sib, head, head_sib,
        flops=4 * tokens * depth * width,
    )


def back(group, head_ref):
    depth = head_ref.shape[1] // 2
    turned = (((1,), (1,)), ((), ()))
    return lax.dot_general(
        group[0][...], head_ref[:, :depth], turned, preferred_element_type=f32
    ) + lax.dot_general(
        group[1][:, :depth], head_ref[:, depth:], turned, preferred_element_type=f32
    )


def outer(hidden, groups, store):
    half = groups[0][0].shape[1]
    for side in range(2):
        for at in range(0, half, STRIP):
            total = sum(
                lax.dot_general(
                    x[...],
                    group[side][:, at : at + STRIP],
                    (((0,), (0,)), ((), ())),
                    preferred_element_type=f32,
                )
                for x, group in zip(hidden, groups)
            )
            store(side * half + at, total)


def near_kernel(head_ref, h0, h1, a0, b0, a1, b1, rows0_ref, rows1_ref, acc_ref):
    rows0_ref[...] = back((a0, b0), head_ref)
    rows1_ref[...] = back((a1, b1), head_ref)

    def store(at, total):
        acc_ref[:, at : at + STRIP] = total

    outer((h0, h1), ((a0, b0), (a1, b1)), store)


def far_kernel(
    order, place_ref, head_ref, near0, near1, acc_ref, h0, h1, a0, b0, a1, b1,
    rows_ref, o_ref,
):
    z, core = place_ref[0], place_ref[1]
    blocks, rows = rows_ref.shape[:2]
    chips = blocks // 2
    for near, group, which in (
        (near0, (a0, b0), core), (near1, (a1, b1), 1 - core)
    ):
        far = back(group, head_ref)
        count = near.shape[0] // rows
        for i, j in enumerate(order):
            x = near[i * rows : (i + 1) * rows] if i < count else (
                far[(i - count) * rows : (i - count + 1) * rows]
            )
            at = 2 * lax.rem(z + j, chips) + which
            rows_ref[pl.ds(at, 1)] = x[None]

    def store(at, total):
        o_ref[:, at : at + STRIP] = (acc_ref[:, at : at + STRIP] + total).astype(bf16)

    outer((h0, h1), ((a0, b0), (a1, b1)), store)


def near_products(head, hidden, groups):
    depth, width = head.shape
    rows = jax.ShapeDtypeStruct((hidden[0].shape[0], depth), f32)
    acc = jax.ShapeDtypeStruct((depth, width), f32)
    return call(
        near_kernel, "near", (rows, rows, acc), head, *hidden, *groups[0], *groups[1],
        flops=8 * rows.size * width,
    )


def far_products(order, place, head, near, hidden, groups, rows):
    depth, width = head.shape
    blocks = 2 * len(order)
    return pl.pallas_call(
        functools.partial(far_kernel, order),
        out_shape=(
            jax.ShapeDtypeStruct((blocks, rows, depth), f32),
            jax.ShapeDtypeStruct((depth, width), bf16),
        ),
        in_specs=[pl.BlockSpec(memory_space=pltpu.SMEM)] + [VMEM] * 10,
        out_specs=(VMEM, VMEM),
        compiler_params=PARAMS,
        name="far",
    )(place, head, *near, *hidden, *groups[0], *groups[1])


def spread(x, axis):
    n = lax.axis_size(axis)
    return lax.all_to_all(jnp.broadcast_to(x[None], (n,) + x.shape), axis, 0, 0)


def summed(x, axis):
    n = lax.axis_size(axis)
    blocks = x.reshape((n, x.shape[0] // n) + x.shape[1:])
    return jnp.sum(lax.all_to_all(blocks, axis, 0, 0), axis=0)


def plain(teacher_hidden, student_hidden, teacher_head, student_head, targets):
    tok_block, voc_local = targets.shape[0], teacher_head.shape[1]
    teacher_all = spread(teacher_hidden, "tensor").reshape(-1, teacher_hidden.shape[1])
    student_all = spread(student_hidden, "tensor").reshape(-1, student_hidden.shape[1])
    teacher_logits = summed(
        jnp.dot(teacher_all, teacher_head, preferred_element_type=f32), "section"
    )
    student_logits = summed(
        jnp.dot(student_all, student_head, preferred_element_type=f32), "section"
    )
    tops = jnp.stack([jnp.max(teacher_logits, axis=1), jnp.max(student_logits, axis=1)])
    teacher_max, student_max = jnp.max(spread(tops, "tensor"), axis=0)
    offset = lax.axis_index("tensor") * voc_local
    column_ids = offset + lax.broadcasted_iota(jnp.int32, (tok_block, voc_local), 1)
    onehot = (column_ids == targets[:, None]).astype(f32)
    p_terms = jnp.exp((teacher_logits - teacher_max[:, None]) / tau)
    q_terms = jnp.exp((student_logits - student_max[:, None]) / tau)
    s_terms = jnp.exp(student_logits - student_max[:, None])
    sums = jnp.stack(
        [
            jnp.sum(p_terms, axis=1),
            jnp.sum(q_terms, axis=1),
            jnp.sum(s_terms, axis=1),
            jnp.sum(p_terms * (teacher_logits - student_logits), axis=1),
            jnp.sum(onehot * student_logits, axis=1),
        ]
    )
    p_total, q_total, s_total, cross, picked = jnp.sum(spread(sums, "tensor"), axis=0)
    kl_rows = (
        cross / (tau * p_total)
        - (teacher_max - student_max) / tau
        - jnp.log(p_total)
        + jnp.log(q_total)
    )
    row_loss = tau * tau * kl_rows + student_max + jnp.log(s_total) - picked
    loss = jnp.mean(spread(row_loss, "section"))
    p_prob = p_terms / p_total[:, None]
    q_prob = q_terms / q_total[:, None]
    s_prob = s_terms / s_total[:, None]
    grad = (tau * (q_prob - p_prob) + s_prob - onehot).astype(bf16)
    grad = spread(grad, "section").reshape(-1, voc_local)
    grad_head = lax.dot_general(
        student_all, grad, (((0,), (0,)), ((), ())), preferred_element_type=f32
    )
    rows = lax.dot_general(
        grad, student_head, (((1,), (1,)), ((), ())), preferred_element_type=f32
    )
    return loss, summed(rows, "tensor").astype(bf16), grad_head.astype(bf16)


def steps(teacher_hidden, student_hidden, teacher_head, student_head, targets):
    section_size = lax.axis_size("section")
    chips = section_size // 2
    half_way = chips // 2
    me = lax.axis_index("section")
    z, core = me // 2, me % 2
    tok_block, dt = teacher_hidden.shape
    ds = student_hidden.shape[1]
    voc_local = teacher_head.shape[1]
    half = voc_local // 2

    def along(x, step):
        perm = [
            (s, ((s // 2 + step) % chips) * 2 + s % 2) for s in range(section_size)
        ]
        return lax.ppermute(x, "section", perm)

    def swap(x):
        return lax.ppermute(x, "section", [(s, s ^ 1) for s in range(section_size)])

    student_head_sib = swap(student_head)
    teacher_head_sib = swap(teacher_head)
    hidden = spread(jnp.concatenate([teacher_hidden, student_hidden], axis=1), "tensor")

    start = chips - half_way + 2
    order = [(start + i) % chips for i in range(chips)]
    count = chips - 3

    def rolled(x, which):
        pair = x.reshape((chips, 2) + x.shape[1:])
        twice = jnp.concatenate([pair, pair], axis=0)
        out = lax.dynamic_slice(
            twice, ((z + start) % chips, which, 0, 0), (chips, 1) + x.shape[1:]
        )
        return out.reshape((chips * x.shape[1],) + x.shape[2:])

    mine, others = rolled(hidden, core), rolled(hidden, 1 - core)
    mine_sib = swap(others)
    student_part = product(
        mine[:, dt:], mine_sib[:, dt:], student_head, student_head_sib, chips
    )
    teacher_part = product(
        mine[:, :dt], mine_sib[:, :dt], teacher_head, teacher_head_sib, chips
    )

    place = jnp.stack([z, core]).astype(jnp.int32)
    split = count * tok_block
    hidden_near = (mine[:split, dt:], others[:split, dt:])
    hidden_far = (mine[split:, dt:], others[split:, dt:])

    def ring(parts, meanwhile=()):
        parts = dict(zip(order, parts))
        right, left = first(parts[half_way])
        right, left = along(right, 1), along(left, -1)
        for step in range(1, half_way):
            right, left = hop(
                right, left, parts[half_way - step], parts[half_way + step]
            )
            if step == half_way - 1:
                right, left, meanwhile = lax.optimization_barrier((right, left, meanwhile))
            right, left = along(right, 1), along(left, -1)
        return (right, left, parts[0]), meanwhile

    offset = lax.axis_index("tensor") * voc_local
    target_here = jnp.broadcast_to((targets - offset)[:, None], (tok_block, 128))

    student, _ = ring(student_part)
    teacher, (hidden_near, hidden_far) = ring(teacher_part, (hidden_near, hidden_far))
    teacher_logits, student_logits, stats = meet(teacher, student, target_here)
    own = payload(teacher_logits, student_logits, spread(stats, "tensor"), target_here)

    pieces = [[None] * chips, [None] * chips]
    right, left = list(own), list(own)
    pieces[0][0], pieces[1][0] = own
    for step in range(1, half_way):
        for side in range(2):
            right[side] = along(right[side], 1)
            left[side] = along(left[side], -1)
            pieces[side][chips - step], pieces[side][step] = right[side], left[side]

    def gathered(js):
        group = [jnp.concatenate([x[j] for j in js], axis=0) for x in pieces]
        return group, [swap(x) for x in group]

    last = [along(right[0], 1), along(left[1], -1)]
    early = {j: [x[j] for x in pieces] for j in order[:count]}
    early, last[1] = lax.optimization_barrier((early, last[1]))
    for j, pair in early.items():
        pieces[0][j], pieces[1][j] = pair
    near = gathered(order[:count])
    pieces[0][half_way], pieces[1][half_way] = last
    far = gathered(order[count:])
    sums = near_products(student_head, hidden_near, near)
    rows, grad_head = far_products(
        order, place, student_head, sums, hidden_far, far, tok_block
    )
    rows, grad_head = lax.optimization_barrier((rows, grad_head))
    extra = sum(
        jnp.sum(g[1][:, half:].astype(f32), axis=0) for group in (near, far) for g in group
    )
    loss = (extra[0] + extra[1] + extra[2]) / (tok_block * section_size)
    grad_hidden = jnp.sum(lax.all_to_all(rows, "tensor", 0, 0), axis=0).astype(bf16)
    return (loss, grad_hidden, grad_head), extra[3]


def shards(*arrays):
    fine, too_coarse = steps(*arrays)
    return lax.cond(too_coarse > 0.0, lambda: plain(*arrays), lambda: fine)


def solution(mesh):
    placed = (
        P("tensor", "section"),
        P("tensor", "section"),
        P("section", "tensor"),
        P("section", "tensor"),
        P("section"),
    )
    return jax.shard_map(
        shards,
        mesh=mesh,
        in_specs=placed,
        out_specs=(P(), P("tensor", "section"), P("section", "tensor")),
        check_vma=False,
    )
```

```python
import functools

import jax
import jax.numpy as jnp
from jax import lax
from jax.experimental import pallas as pl
from jax.experimental.pallas import tpu as pltpu
from jax.sharding import PartitionSpec as P

tau = 2.0
f32 = jnp.float32
bf16 = jnp.bfloat16
i16 = jnp.int16

LEVELS = 32767.0
CODES = 128
LIMIT = 1000.0
STRIP = 512
PARAMS = pltpu.CompilerParams(vmem_limit_bytes=20 * 1024 * 1024)


def row_codes(ref):
    w = ref.shape[1] - CODES
    codes = ref[:, w:].astype(jnp.int32).astype(f32)
    middle = codes[:, 0:1] * 0.25
    scale = codes[:, 32:33] * (0.5 / LEVELS)
    return middle, scale, codes[:, 64:65]


def encode(x_ref, columns, o_ref, spent):
    lo, hi = columns
    top = bottom = None
    for at in range(lo, hi, STRIP):
        x = x_ref[:, at : at + STRIP]
        top = x if top is None else jnp.maximum(top, x)
        bottom = x if bottom is None else jnp.minimum(bottom, x)
    top = jnp.max(top, axis=1, keepdims=True)
    bottom = jnp.min(bottom, axis=1, keepdims=True)
    middle_code = jnp.round((top + bottom) * 2.0)
    middle = middle_code * 0.25
    reach = jnp.maximum(top - middle, middle - bottom)
    reach_code = jnp.floor(reach * 2.0) + 1.0
    spent_code = jnp.minimum(spent + reach_code, LEVELS)
    inverse = (2.0 * LEVELS) / reach_code
    for at in range(lo, hi, STRIP):
        code = jnp.round((x_ref[:, at : at + STRIP] - middle) * inverse)
        o_ref[:, at - lo : at - lo + STRIP] = code.astype(jnp.int32).astype(i16)
    lane = lax.broadcasted_iota(jnp.int32, (x_ref.shape[0], CODES), 1)
    codes = jnp.where(lane < 32, middle_code, jnp.where(lane < 64, reach_code, spent_code))
    o_ref[:, hi - lo :] = codes.astype(jnp.int32).astype(i16)


def first_kernel(part_ref, right_ref, left_ref):
    rows, width = part_ref.shape
    none = jnp.zeros((rows, 1), f32)
    encode(part_ref, (0, width // 2), right_ref, none)
    encode(part_ref, (width // 2, width), left_ref, none)


def hop_kernel(r_ref, l_ref, pr_ref, pl_ref, ro_ref, lo_ref, sum_ref):
    width = pr_ref.shape[1]
    for in_ref, part_ref, out_ref, at_end in (
        (r_ref, pr_ref, ro_ref, False),
        (l_ref, pl_ref, lo_ref, True),
    ):
        carried = in_ref.shape[1] - CODES
        start = width - carried if at_end else 0
        middle, scale, spent = row_codes(in_ref)
        for at in range(0, width, STRIP):
            x = part_ref[:, at : at + STRIP]
            if start <= at < start + carried:
                code = in_ref[:, at - start : at - start + STRIP]
                x = x + (middle + code.astype(jnp.int32).astype(f32) * scale)
            sum_ref[:, at : at + STRIP] = x
        encode(sum_ref, (0, width), out_ref, spent)


def meet_kernel(
    rt_ref, lt_ref, pt_ref, rs_ref, ls_ref, ps_ref, target_ref, t_ref, s_ref, stats_ref
):
    rows, width = t_ref.shape
    tops, spents = [], []
    for r_ref, l_ref, part_ref, out_ref in (
        (rt_ref, lt_ref, pt_ref, t_ref),
        (rs_ref, ls_ref, ps_ref, s_ref),
    ):
        r_middle, r_scale, r_spent = row_codes(r_ref)
        l_middle, l_scale, l_spent = row_codes(l_ref)
        top = None
        for at in range(0, width, STRIP):
            strip = slice(at, at + STRIP)
            x = (
                part_ref[:, strip]
                + (r_middle + r_ref[:, strip].astype(jnp.int32).astype(f32) * r_scale)
                + (l_middle + l_ref[:, strip].astype(jnp.int32).astype(f32) * l_scale)
            )
            out_ref[:, strip] = x
            top = x if top is None else jnp.maximum(top, x)
        tops.append(jnp.max(top, axis=1, keepdims=True))
        spents.append((r_spent + l_spent) * 0.5)
    t_max, s_max = tops
    target = target_ref[:, 0:1]
    sums = None
    for at in range(0, width, 128):
        t, s = t_ref[:, at : at + 128], s_ref[:, at : at + 128]
        p = jnp.exp((t - t_max) * (1.0 / tau))
        q = jnp.exp((s - s_max) * (1.0 / tau))
        ids = at + lax.broadcasted_iota(jnp.int32, t.shape, 1)
        terms = (p, q, q * q, p * (t - s), jnp.where(ids == target, s, 0.0))
        sums = terms if sums is None else [a + b for a, b in zip(sums, terms)]
    lane = lax.broadcasted_iota(jnp.int32, (rows, 128), 1)
    kinds = [t_max, s_max] + [jnp.sum(a, axis=1, keepdims=True) for a in sums]
    kinds.append(jnp.maximum(spents[0], spents[1]))
    table = jnp.zeros((rows, 128), f32)
    for k, value in enumerate(kinds):
        table = jnp.where(lane == k, value, table)
    table = jnp.concatenate([table, jnp.zeros((128 - rows, 128), f32)], axis=0)
    stats_ref[...] = table.T[0:8, :]


def grad_kernel(t_ref, s_ref, every_ref, target_ref, a_ref, b_ref):
    rows, width = t_ref.shape
    t_tops, s_tops = every_ref[:, 0, :], every_ref[:, 1, :]
    t_max = jnp.max(t_tops, axis=0, keepdims=True)
    s_max = jnp.max(s_tops, axis=0, keepdims=True)
    t_weight = jnp.exp((t_tops - t_max) * (1.0 / tau))
    q_weight = jnp.exp((s_tops - s_max) * (1.0 / tau))
    s_weight = jnp.exp(s_tops - s_max)

    def total(k, weight):
        return jnp.sum(every_ref[:, k, :] * weight, axis=0, keepdims=True)

    p_total, q_total = total(2, t_weight), total(3, q_weight)
    s_total, cross = total(4, s_weight), total(5, t_weight)
    picked = jnp.sum(every_ref[:, 6, :], axis=0, keepdims=True)
    spent = jnp.max(every_ref[:, 7, :], axis=0, keepdims=True)
    kl_rows = (
        cross / (tau * p_total)
        - (t_max - s_max) / tau
        - jnp.log(p_total)
        + jnp.log(q_total)
    )
    row_loss = tau * tau * kl_rows + s_max + jnp.log(s_total) - picked
    flag = jnp.where(spent > LIMIT, 1.0, 0.0)
    lines = [t_max, s_max, tau / p_total, tau / q_total, 1.0 / s_total, row_loss, flag]
    lines.append(jnp.zeros((128 - len(lines), 128), f32))
    table = jnp.concatenate(lines, axis=0).T[:rows]
    t_max, s_max, p_scale, q_scale, s_scale, row_loss, flag = (
        table[:, k : k + 1] for k in range(7)
    )
    target = target_ref[:, 0:1]
    for at in range(0, width, STRIP):
        t, s = t_ref[:, at : at + STRIP], s_ref[:, at : at + STRIP]
        p = jnp.exp((t - t_max) * (1.0 / tau))
        q = jnp.exp((s - s_max) * (1.0 / tau))
        ids = at + lax.broadcasted_iota(jnp.int32, t.shape, 1)
        grad = q * q_scale - p * p_scale + (q * q) * s_scale
        grad = grad - jnp.where(ids == target, 1.0, 0.0)
        o_ref, to = (a_ref, at) if at < width // 2 else (b_ref, at - width // 2)
        o_ref[:, to : to + STRIP] = grad.astype(bf16)
    high = row_loss.astype(bf16).astype(f32)
    mid = (row_loss - high).astype(bf16).astype(f32)
    low = row_loss - high - mid
    lane = lax.broadcasted_iota(jnp.int32, (rows, CODES), 1)
    extra = jnp.where(
        lane == 0,
        high,
        jnp.where(lane == 1, mid, jnp.where(lane == 2, low, jnp.where(lane == 3, flag, 0.0))),
    )
    b_ref[:, width // 2 :] = extra.astype(bf16)


VMEM = pl.BlockSpec(memory_space=pltpu.VMEM)


def call(kernel, name, out, *operands, flops=0, **more):
    leaves = jax.tree.leaves((out, operands))
    return pl.pallas_call(
        kernel,
        out_shape=out,
        in_specs=[VMEM] * len(operands),
        out_specs=jax.tree.map(lambda _: VMEM, out),
        compiler_params=PARAMS,
        cost_estimate=pl.CostEstimate(
            flops=flops,
            bytes_accessed=sum(x.size * x.dtype.itemsize for x in leaves),
            transcendentals=0,
        ),
        name=name,
        **more,
    )(*operands)


def first(part):
    rows, width = part.shape
    out = jax.ShapeDtypeStruct((rows, width // 2 + CODES), i16)
    return call(first_kernel, "first", (out, out), part)


def hop(right, left, part_right, part_left):
    rows, width = part_right.shape
    out = jax.ShapeDtypeStruct((rows, width + CODES), i16)
    return call(
        hop_kernel, "hop", (out, out), right, left, part_right, part_left,
        scratch_shapes=[pltpu.VMEM((rows, width), f32)],
    )


def meet(teacher, student, target):
    rows, width = teacher[2].shape
    logits = jax.ShapeDtypeStruct((rows, width), f32)
    stats = jax.ShapeDtypeStruct((8, 128), f32)
    return call(meet_kernel, "meet", (logits, logits, stats), *teacher, *student, target)


def payload(teacher_logits, student_logits, every, target):
    rows, width = teacher_logits.shape
    out = (
        jax.ShapeDtypeStruct((rows, width // 2), bf16),
        jax.ShapeDtypeStruct((rows, width // 2 + CODES), bf16),
    )
    return call(
        grad_kernel, "payload", out, teacher_logits, student_logits, every, target
    )


def product_kernel(own_ref, sib_ref, head_ref, head_sib_ref, *o_refs):
    rows, width = o_refs[0].shape
    step = min(width, 2 * STRIP)
    for at in range(0, width, step):
        strip = slice(at, at + step)
        x = jnp.dot(own_ref[...], head_ref[:, strip], preferred_element_type=f32)
        x = x + jnp.dot(sib_ref[...], head_sib_ref[:, strip], preferred_element_type=f32)
        for k, o_ref in enumerate(o_refs):
            o_ref[:, strip] = x[k * rows : (k + 1) * rows]


def product(own, sib, head, head_sib, blocks):
    tokens, depth = own.shape
    width = head.shape[1]
    out = jax.ShapeDtypeStruct((tokens // blocks, width), f32)
    return call(
        product_kernel, "product", (out,) * blocks, own, sib, head, head_sib,
        flops=4 * tokens * depth * width,
    )


def back(group, head_ref):
    depth = head_ref.shape[1] // 2
    turned = (((1,), (1,)), ((), ()))
    return lax.dot_general(
        group[0][...], head_ref[:, :depth], turned, preferred_element_type=f32
    ) + lax.dot_general(
        group[1][:, :depth], head_ref[:, depth:], turned, preferred_element_type=f32
    )


def outer(hidden, groups, store):
    half = groups[0][0].shape[1]
    for side in range(2):
        for at in range(0, half, STRIP):
            total = sum(
                lax.dot_general(
                    x[...],
                    group[side][:, at : at + STRIP],
                    (((0,), (0,)), ((), ())),
                    preferred_element_type=f32,
                )
                for x, group in zip(hidden, groups)
            )
            store(side * half + at, total)


def near_kernel(head_ref, h0, h1, a0, b0, a1, b1, rows0_ref, rows1_ref, acc_ref):
    rows0_ref[...] = back((a0, b0), head_ref)
    rows1_ref[...] = back((a1, b1), head_ref)

    def store(at, total):
        acc_ref[:, at : at + STRIP] = total

    outer((h0, h1), ((a0, b0), (a1, b1)), store)


def far_kernel(
    order, place_ref, head_ref, near0, near1, acc_ref, h0, h1, a0, b0, a1, b1,
    rows_ref, o_ref,
):
    z, core = place_ref[0], place_ref[1]
    blocks, rows = rows_ref.shape[:2]
    chips = blocks // 2
    for near, group, which in (
        (near0, (a0, b0), core), (near1, (a1, b1), 1 - core)
    ):
        far = back(group, head_ref)
        count = near.shape[0] // rows
        for i, j in enumerate(order):
            x = near[i * rows : (i + 1) * rows] if i < count else (
                far[(i - count) * rows : (i - count + 1) * rows]
            )
            at = 2 * lax.rem(z + j, chips) + which
            rows_ref[pl.ds(at, 1)] = x[None]

    def store(at, total):
        o_ref[:, at : at + STRIP] = (acc_ref[:, at : at + STRIP] + total).astype(bf16)

    outer((h0, h1), ((a0, b0), (a1, b1)), store)


def near_products(head, hidden, groups):
    depth, width = head.shape
    rows = jax.ShapeDtypeStruct((hidden[0].shape[0], depth), f32)
    acc = jax.ShapeDtypeStruct((depth, width), f32)
    return call(
        near_kernel, "near", (rows, rows, acc), head, *hidden, *groups[0], *groups[1],
        flops=8 * rows.size * width,
    )


def far_products(order, place, head, near, hidden, groups, rows):
    depth, width = head.shape
    blocks = 2 * len(order)
    return pl.pallas_call(
        functools.partial(far_kernel, order),
        out_shape=(
            jax.ShapeDtypeStruct((blocks, rows, depth), f32),
            jax.ShapeDtypeStruct((depth, width), bf16),
        ),
        in_specs=[pl.BlockSpec(memory_space=pltpu.SMEM)] + [VMEM] * 10,
        out_specs=(VMEM, VMEM),
        compiler_params=PARAMS,
        name="far",
    )(place, head, *near, *hidden, *groups[0], *groups[1])


def spread(x, axis):
    n = lax.axis_size(axis)
    return lax.all_to_all(jnp.broadcast_to(x[None], (n,) + x.shape), axis, 0, 0)


def summed(x, axis):
    n = lax.axis_size(axis)
    blocks = x.reshape((n, x.shape[0] // n) + x.shape[1:])
    return jnp.sum(lax.all_to_all(blocks, axis, 0, 0), axis=0)


def plain(teacher_hidden, student_hidden, teacher_head, student_head, targets):
    tok_block, voc_local = targets.shape[0], teacher_head.shape[1]
    teacher_all = spread(teacher_hidden, "tensor").reshape(-1, teacher_hidden.shape[1])
    student_all = spread(student_hidden, "tensor").reshape(-1, student_hidden.shape[1])
    teacher_logits = summed(
        jnp.dot(teacher_all, teacher_head, preferred_element_type=f32), "section"
    )
    student_logits = summed(
        jnp.dot(student_all, student_head, preferred_element_type=f32), "section"
    )
    tops = jnp.stack([jnp.max(teacher_logits, axis=1), jnp.max(student_logits, axis=1)])
    teacher_max, student_max = jnp.max(spread(tops, "tensor"), axis=0)
    offset = lax.axis_index("tensor") * voc_local
    column_ids = offset + lax.broadcasted_iota(jnp.int32, (tok_block, voc_local), 1)
    onehot = (column_ids == targets[:, None]).astype(f32)
    p_terms = jnp.exp((teacher_logits - teacher_max[:, None]) / tau)
    q_terms = jnp.exp((student_logits - student_max[:, None]) / tau)
    s_terms = jnp.exp(student_logits - student_max[:, None])
    sums = jnp.stack(
        [
            jnp.sum(p_terms, axis=1),
            jnp.sum(q_terms, axis=1),
            jnp.sum(s_terms, axis=1),
            jnp.sum(p_terms * (teacher_logits - student_logits), axis=1),
            jnp.sum(onehot * student_logits, axis=1),
        ]
    )
    p_total, q_total, s_total, cross, picked = jnp.sum(spread(sums, "tensor"), axis=0)
    kl_rows = (
        cross / (tau * p_total)
        - (teacher_max - student_max) / tau
        - jnp.log(p_total)
        + jnp.log(q_total)
    )
    row_loss = tau * tau * kl_rows + student_max + jnp.log(s_total) - picked
    loss = jnp.mean(spread(row_loss, "section"))
    p_prob = p_terms / p_total[:, None]
    q_prob = q_terms / q_total[:, None]
    s_prob = s_terms / s_total[:, None]
    grad = (tau * (q_prob - p_prob) + s_prob - onehot).astype(bf16)
    grad = spread(grad, "section").reshape(-1, voc_local)
    grad_head = lax.dot_general(
        student_all, grad, (((0,), (0,)), ((), ())), preferred_element_type=f32
    )
    rows = lax.dot_general(
        grad, student_head, (((1,), (1,)), ((), ())), preferred_element_type=f32
    )
    return loss, summed(rows, "tensor").astype(bf16), grad_head.astype(bf16)


def steps(teacher_hidden, student_hidden, teacher_head, student_head, targets):
    section_size = lax.axis_size("section")
    chips = section_size // 2
    half_way = chips // 2
    me = lax.axis_index("section")
    z, core = me // 2, me % 2
    tok_block, dt = teacher_hidden.shape
    ds = student_hidden.shape[1]
    voc_local = teacher_head.shape[1]
    half = voc_local // 2

    def along(x, step):
        perm = [
            (s, ((s // 2 + step) % chips) * 2 + s % 2) for s in range(section_size)
        ]
        return lax.ppermute(x, "section", perm)

    def swap(x):
        return lax.ppermute(x, "section", [(s, s ^ 1) for s in range(section_size)])

    student_head_sib = swap(student_head)
    teacher_head_sib = swap(teacher_head)
    hidden = spread(jnp.concatenate([teacher_hidden, student_hidden], axis=1), "tensor")

    start = chips - half_way + 2
    order = [(start + i) % chips for i in range(chips)]
    count = chips - 3

    def rolled(x, which):
        pair = x.reshape((chips, 2) + x.shape[1:])
        twice = jnp.concatenate([pair, pair], axis=0)
        out = lax.dynamic_slice(
            twice, ((z + start) % chips, which, 0, 0), (chips, 1) + x.shape[1:]
        )
        return out.reshape((chips * x.shape[1],) + x.shape[2:])

    mine, others = rolled(hidden, core), rolled(hidden, 1 - core)
    mine_sib = swap(others)
    student_part = product(
        mine[:, dt:], mine_sib[:, dt:], student_head, student_head_sib, chips
    )
    teacher_part = product(
        mine[:, :dt], mine_sib[:, :dt], teacher_head, teacher_head_sib, chips
    )

    place = jnp.stack([z, core]).astype(jnp.int32)
    split = count * tok_block
    hidden_near = (mine[:split, dt:], others[:split, dt:])
    hidden_far = (mine[split:, dt:], others[split:, dt:])

    def ring(parts, meanwhile=()):
        parts = dict(zip(order, parts))
        right, left = first(parts[half_way])
        right, left = along(right, 1), along(left, -1)
        for step in range(1, half_way):
            right, left = hop(
                right, left, parts[half_way - step], parts[half_way + step]
            )
            if step == half_way - 1:
                right, left, meanwhile = lax.optimization_barrier((right, left, meanwhile))
            right, left = along(right, 1), along(left, -1)
        return (right, left, parts[0]), meanwhile

    offset = lax.axis_index("tensor") * voc_local
    target_here = jnp.broadcast_to((targets - offset)[:, None], (tok_block, 128))

    student, _ = ring(student_part)
    teacher, (hidden_near, hidden_far) = ring(teacher_part, (hidden_near, hidden_far))
    teacher_logits, student_logits, stats = meet(teacher, student, target_here)
    own = payload(teacher_logits, student_logits, spread(stats, "tensor"), target_here)

    pieces = [[None] * chips, [None] * chips]
    right, left = list(own), list(own)
    pieces[0][0], pieces[1][0] = own
    for step in range(1, half_way):
        for side in range(2):
            right[side] = along(right[side], 1)
            left[side] = along(left[side], -1)
            pieces[side][chips - step], pieces[side][step] = right[side], left[side]

    def gathered(js):
        group = [jnp.concatenate([x[j] for j in js], axis=0) for x in pieces]
        return group, [swap(x) for x in group]

    last = [along(right[0], 1), along(left[1], -1)]
    early = {j: [x[j] for x in pieces] for j in order[:count]}
    early, pieces[0][half_way + 1], pieces[0][half_way - 1], pieces[1][half_way + 1] = lax.optimization_barrier((early, pieces[0][half_way + 1], pieces[0][half_way - 1], pieces[1][half_way + 1]))
    for j, pair in early.items():
        pieces[0][j], pieces[1][j] = pair
    near = gathered(order[:count])
    sums = near_products(student_head, hidden_near, near)
    last, sums = lax.optimization_barrier((last, sums))
    pieces[0][half_way], pieces[1][half_way] = last
    far = gathered(order[count:])
    rows, grad_head = far_products(
        order, place, student_head, sums, hidden_far, far, tok_block
    )
    rows, grad_head = lax.optimization_barrier((rows, grad_head))
    extra = sum(
        jnp.sum(g[1][:, half:].astype(f32), axis=0) for group in (near, far) for g in group
    )
    loss = (extra[0] + extra[1] + extra[2]) / (tok_block * section_size)
    grad_hidden = jnp.sum(lax.all_to_all(rows, "tensor", 0, 0), axis=0).astype(bf16)
    return (loss, grad_hidden, grad_head), extra[3]


def shards(*arrays):
    fine, too_coarse = steps(*arrays)
    return lax.cond(too_coarse > 0.0, lambda: plain(*arrays), lambda: fine)


def solution(mesh):
    placed = (
        P("tensor", "section"),
        P("tensor", "section"),
        P("section", "tensor"),
        P("section", "tensor"),
        P("section"),
    )
    return jax.shard_map(
        shards,
        mesh=mesh,
        in_specs=placed,
        out_specs=(P(), P("tensor", "section"), P("section", "tensor")),
        check_vma=False,
    )
```

```python
import functools

import jax
import jax.numpy as jnp
from jax import lax
from jax.experimental import pallas as pl
from jax.experimental.pallas import tpu as pltpu
from jax.sharding import PartitionSpec as P

tau = 2.0
f32 = jnp.float32
bf16 = jnp.bfloat16
i16 = jnp.int16

LEVELS = 32767.0
CODES = 128
LIMIT = 1000.0
STRIP = 512
PARAMS = pltpu.CompilerParams(vmem_limit_bytes=20 * 1024 * 1024)


def row_codes(ref):
    w = ref.shape[1] - CODES
    codes = ref[:, w:].astype(jnp.int32).astype(f32)
    middle = codes[:, 0:1] * 0.25
    scale = codes[:, 32:33] * (0.5 / LEVELS)
    return middle, scale, codes[:, 64:65]


def encode(x_ref, columns, o_ref, spent):
    lo, hi = columns
    top = bottom = None
    for at in range(lo, hi, STRIP):
        x = x_ref[:, at : at + STRIP]
        top = x if top is None else jnp.maximum(top, x)
        bottom = x if bottom is None else jnp.minimum(bottom, x)
    top = jnp.max(top, axis=1, keepdims=True)
    bottom = jnp.min(bottom, axis=1, keepdims=True)
    middle_code = jnp.round((top + bottom) * 2.0)
    middle = middle_code * 0.25
    reach = jnp.maximum(top - middle, middle - bottom)
    reach_code = jnp.floor(reach * 2.0) + 1.0
    spent_code = jnp.minimum(spent + reach_code, LEVELS)
    inverse = (2.0 * LEVELS) / reach_code
    for at in range(lo, hi, STRIP):
        code = jnp.round((x_ref[:, at : at + STRIP] - middle) * inverse)
        o_ref[:, at - lo : at - lo + STRIP] = code.astype(jnp.int32).astype(i16)
    lane = lax.broadcasted_iota(jnp.int32, (x_ref.shape[0], CODES), 1)
    codes = jnp.where(lane < 32, middle_code, jnp.where(lane < 64, reach_code, spent_code))
    o_ref[:, hi - lo :] = codes.astype(jnp.int32).astype(i16)


def first_kernel(part_ref, right_ref, left_ref):
    rows, width = part_ref.shape
    none = jnp.zeros((rows, 1), f32)
    encode(part_ref, (0, width // 2), right_ref, none)
    encode(part_ref, (width // 2, width), left_ref, none)


def hop_kernel(r_ref, l_ref, pr_ref, pl_ref, ro_ref, lo_ref, sum_ref):
    width = pr_ref.shape[1]
    for in_ref, part_ref, out_ref, at_end in (
        (r_ref, pr_ref, ro_ref, False),
        (l_ref, pl_ref, lo_ref, True),
    ):
        carried = in_ref.shape[1] - CODES
        start = width - carried if at_end else 0
        middle, scale, spent = row_codes(in_ref)
        for at in range(0, width, STRIP):
            x = part_ref[:, at : at + STRIP]
            if start <= at < start + carried:
                code = in_ref[:, at - start : at - start + STRIP]
                x = x + (middle + code.astype(jnp.int32).astype(f32) * scale)
            sum_ref[:, at : at + STRIP] = x
        encode(sum_ref, (0, width), out_ref, spent)


def meet_kernel(
    rt_ref, lt_ref, pt_ref, rs_ref, ls_ref, ps_ref, target_ref, t_ref, s_ref, stats_ref
):
    rows, width = t_ref.shape
    tops, spents = [], []
    for r_ref, l_ref, part_ref, out_ref in (
        (rt_ref, lt_ref, pt_ref, t_ref),
        (rs_ref, ls_ref, ps_ref, s_ref),
    ):
        r_middle, r_scale, r_spent = row_codes(r_ref)
        l_middle, l_scale, l_spent = row_codes(l_ref)
        top = None
        for at in range(0, width, STRIP):
            strip = slice(at, at + STRIP)
            x = (
                part_ref[:, strip]
                + (r_middle + r_ref[:, strip].astype(jnp.int32).astype(f32) * r_scale)
                + (l_middle + l_ref[:, strip].astype(jnp.int32).astype(f32) * l_scale)
            )
            out_ref[:, strip] = x
            top = x if top is None else jnp.maximum(top, x)
        tops.append(jnp.max(top, axis=1, keepdims=True))
        spents.append((r_spent + l_spent) * 0.5)
    t_max, s_max = tops
    target = target_ref[:, 0:1]
    sums = None
    for at in range(0, width, 128):
        t, s = t_ref[:, at : at + 128], s_ref[:, at : at + 128]
        p = jnp.exp((t - t_max) * (1.0 / tau))
        q = jnp.exp((s - s_max) * (1.0 / tau))
        ids = at + lax.broadcasted_iota(jnp.int32, t.shape, 1)
        terms = (p, q, q * q, p * (t - s), jnp.where(ids == target, s, 0.0))
        sums = terms if sums is None else [a + b for a, b in zip(sums, terms)]
    lane = lax.broadcasted_iota(jnp.int32, (rows, 128), 1)
    kinds = [t_max, s_max] + [jnp.sum(a, axis=1, keepdims=True) for a in sums]
    kinds.append(jnp.maximum(spents[0], spents[1]))
    table = jnp.zeros((rows, 128), f32)
    for k, value in enumerate(kinds):
        table = jnp.where(lane == k, value, table)
    table = jnp.concatenate([table, jnp.zeros((128 - rows, 128), f32)], axis=0)
    stats_ref[...] = table.T[0:8, :]


def grad_kernel(t_ref, s_ref, every_ref, target_ref, a_ref, b_ref):
    rows, width = t_ref.shape
    t_tops, s_tops = every_ref[:, 0, :], every_ref[:, 1, :]
    t_max = jnp.max(t_tops, axis=0, keepdims=True)
    s_max = jnp.max(s_tops, axis=0, keepdims=True)
    t_weight = jnp.exp((t_tops - t_max) * (1.0 / tau))
    q_weight = jnp.exp((s_tops - s_max) * (1.0 / tau))
    s_weight = jnp.exp(s_tops - s_max)

    def total(k, weight):
        return jnp.sum(every_ref[:, k, :] * weight, axis=0, keepdims=True)

    p_total, q_total = total(2, t_weight), total(3, q_weight)
    s_total, cross = total(4, s_weight), total(5, t_weight)
    picked = jnp.sum(every_ref[:, 6, :], axis=0, keepdims=True)
    spent = jnp.max(every_ref[:, 7, :], axis=0, keepdims=True)
    kl_rows = (
        cross / (tau * p_total)
        - (t_max - s_max) / tau
        - jnp.log(p_total)
        + jnp.log(q_total)
    )
    row_loss = tau * tau * kl_rows + s_max + jnp.log(s_total) - picked
    flag = jnp.where(spent > LIMIT, 1.0, 0.0)
    lines = [t_max, s_max, tau / p_total, tau / q_total, 1.0 / s_total, row_loss, flag]
    lines.append(jnp.zeros((128 - len(lines), 128), f32))
    table = jnp.concatenate(lines, axis=0).T[:rows]
    t_max, s_max, p_scale, q_scale, s_scale, row_loss, flag = (
        table[:, k : k + 1] for k in range(7)
    )
    target = target_ref[:, 0:1]
    for at in range(0, width, STRIP):
        t, s = t_ref[:, at : at + STRIP], s_ref[:, at : at + STRIP]
        p = jnp.exp((t - t_max) * (1.0 / tau))
        q = jnp.exp((s - s_max) * (1.0 / tau))
        ids = at + lax.broadcasted_iota(jnp.int32, t.shape, 1)
        grad = q * q_scale - p * p_scale + (q * q) * s_scale
        grad = grad - jnp.where(ids == target, 1.0, 0.0)
        o_ref, to = (a_ref, at) if at < width // 2 else (b_ref, at - width // 2)
        o_ref[:, to : to + STRIP] = grad.astype(bf16)
    high = row_loss.astype(bf16).astype(f32)
    mid = (row_loss - high).astype(bf16).astype(f32)
    low = row_loss - high - mid
    lane = lax.broadcasted_iota(jnp.int32, (rows, CODES), 1)
    extra = jnp.where(
        lane == 0,
        high,
        jnp.where(lane == 1, mid, jnp.where(lane == 2, low, jnp.where(lane == 3, flag, 0.0))),
    )
    b_ref[:, width // 2 :] = extra.astype(bf16)


VMEM = pl.BlockSpec(memory_space=pltpu.VMEM)


def call(kernel, name, out, *operands, flops=0, **more):
    leaves = jax.tree.leaves((out, operands))
    return pl.pallas_call(
        kernel,
        out_shape=out,
        in_specs=[VMEM] * len(operands),
        out_specs=jax.tree.map(lambda _: VMEM, out),
        compiler_params=PARAMS,
        cost_estimate=pl.CostEstimate(
            flops=flops,
            bytes_accessed=sum(x.size * x.dtype.itemsize for x in leaves),
            transcendentals=0,
        ),
        name=name,
        **more,
    )(*operands)


def first(part):
    rows, width = part.shape
    out = jax.ShapeDtypeStruct((rows, width // 2 + CODES), i16)
    return call(first_kernel, "first", (out, out), part)


def hop(right, left, part_right, part_left):
    rows, width = part_right.shape
    out = jax.ShapeDtypeStruct((rows, width + CODES), i16)
    return call(
        hop_kernel, "hop", (out, out), right, left, part_right, part_left,
        scratch_shapes=[pltpu.VMEM((rows, width), f32)],
    )


def meet(teacher, student, target):
    rows, width = teacher[2].shape
    logits = jax.ShapeDtypeStruct((rows, width), f32)
    stats = jax.ShapeDtypeStruct((8, 128), f32)
    return call(meet_kernel, "meet", (logits, logits, stats), *teacher, *student, target)


def payload(teacher_logits, student_logits, every, target):
    rows, width = teacher_logits.shape
    out = (
        jax.ShapeDtypeStruct((rows, width // 2), bf16),
        jax.ShapeDtypeStruct((rows, width // 2 + CODES), bf16),
    )
    return call(
        grad_kernel, "payload", out, teacher_logits, student_logits, every, target
    )


def product_kernel(own_ref, sib_ref, head_ref, head_sib_ref, *o_refs):
    rows, width = o_refs[0].shape
    step = min(width, 2 * STRIP)
    for at in range(0, width, step):
        strip = slice(at, at + step)
        x = jnp.dot(own_ref[...], head_ref[:, strip], preferred_element_type=f32)
        x = x + jnp.dot(sib_ref[...], head_sib_ref[:, strip], preferred_element_type=f32)
        for k, o_ref in enumerate(o_refs):
            o_ref[:, strip] = x[k * rows : (k + 1) * rows]


def product(own, sib, head, head_sib, blocks):
    tokens, depth = own.shape
    width = head.shape[1]
    out = jax.ShapeDtypeStruct((tokens // blocks, width), f32)
    return call(
        product_kernel, "product", (out,) * blocks, own, sib, head, head_sib,
        flops=4 * tokens * depth * width,
    )


def back(group, head_ref):
    depth = head_ref.shape[1] // 2
    turned = (((1,), (1,)), ((), ()))
    return lax.dot_general(
        group[0][...], head_ref[:, :depth], turned, preferred_element_type=f32
    ) + lax.dot_general(
        group[1][:, :depth], head_ref[:, depth:], turned, preferred_element_type=f32
    )


def outer(hidden, groups, store):
    half = groups[0][0].shape[1]
    for side in range(2):
        for at in range(0, half, STRIP):
            total = sum(
                lax.dot_general(
                    x[...],
                    group[side][:, at : at + STRIP],
                    (((0,), (0,)), ((), ())),
                    preferred_element_type=f32,
                )
                for x, group in zip(hidden, groups)
            )
            store(side * half + at, total)


def near_kernel(head_ref, h0, h1, a0, b0, a1, b1, rows0_ref, rows1_ref, acc_ref):
    rows0_ref[...] = back((a0, b0), head_ref)
    rows1_ref[...] = back((a1, b1), head_ref)

    def store(at, total):
        acc_ref[:, at : at + STRIP] = total

    outer((h0, h1), ((a0, b0), (a1, b1)), store)


def far_kernel(
    order, place_ref, head_ref, near0, near1, acc_ref, h0, h1, a0, b0, a1, b1,
    rows_hbm, o_hbm, rows_ref, o_ref, sems,
):
    z, core = place_ref[0], place_ref[1]
    blocks, rows = rows_ref.shape[:2]
    chips = blocks // 2
    for near, group, which in (
        (near0, (a0, b0), core), (near1, (a1, b1), 1 - core)
    ):
        far = back(group, head_ref)
        count = near.shape[0] // rows
        for i, j in enumerate(order):
            x = near[i * rows : (i + 1) * rows] if i < count else (
                far[(i - count) * rows : (i - count + 1) * rows]
            )
            at = 2 * lax.rem(z + j, chips) + which
            rows_ref[pl.ds(at, 1)] = x[None]
    copies = [pltpu.make_async_copy(rows_ref, rows_hbm, sems.at[0])]
    copies[0].start()

    def store(at, total):
        o_ref[:, at : at + STRIP] = (acc_ref[:, at : at + STRIP] + total).astype(bf16)
        strip = pl.ds(at, STRIP)
        copies.append(
            pltpu.make_async_copy(
                o_ref.at[:, strip], o_hbm.at[:, strip], sems.at[len(copies)]
            )
        )
        copies[-1].start()

    outer((h0, h1), ((a0, b0), (a1, b1)), store)
    for copy in copies:
        copy.wait()


def near_products(head, hidden, groups):
    depth, width = head.shape
    rows = jax.ShapeDtypeStruct((hidden[0].shape[0], depth), f32)
    acc = jax.ShapeDtypeStruct((depth, width), f32)
    return call(
        near_kernel, "near", (rows, rows, acc), head, *hidden, *groups[0], *groups[1],
        flops=8 * rows.size * width,
    )


def far_products(order, place, head, near, hidden, groups, rows):
    depth, width = head.shape
    blocks = 2 * len(order)
    hbm = pl.BlockSpec(memory_space=pltpu.HBM)
    return pl.pallas_call(
        functools.partial(far_kernel, order),
        out_shape=(
            jax.ShapeDtypeStruct((blocks, rows, depth), f32),
            jax.ShapeDtypeStruct((depth, width), bf16),
        ),
        in_specs=[pl.BlockSpec(memory_space=pltpu.SMEM)] + [VMEM] * 10,
        out_specs=(hbm, hbm),
        scratch_shapes=[
            pltpu.VMEM((blocks, rows, depth), f32),
            pltpu.VMEM((depth, width), bf16),
            pltpu.SemaphoreType.DMA((1 + width // STRIP,)),
        ],
        compiler_params=PARAMS,
        name="far",
    )(place, head, *near, *hidden, *groups[0], *groups[1])


def spread(x, axis):
    n = lax.axis_size(axis)
    return lax.all_to_all(jnp.broadcast_to(x[None], (n,) + x.shape), axis, 0, 0)


def summed(x, axis):
    n = lax.axis_size(axis)
    blocks = x.reshape((n, x.shape[0] // n) + x.shape[1:])
    return jnp.sum(lax.all_to_all(blocks, axis, 0, 0), axis=0)


def plain(teacher_hidden, student_hidden, teacher_head, student_head, targets):
    tok_block, voc_local = targets.shape[0], teacher_head.shape[1]
    teacher_all = spread(teacher_hidden, "tensor").reshape(-1, teacher_hidden.shape[1])
    student_all = spread(student_hidden, "tensor").reshape(-1, student_hidden.shape[1])
    teacher_logits = summed(
        jnp.dot(teacher_all, teacher_head, preferred_element_type=f32), "section"
    )
    student_logits = summed(
        jnp.dot(student_all, student_head, preferred_element_type=f32), "section"
    )
    tops = jnp.stack([jnp.max(teacher_logits, axis=1), jnp.max(student_logits, axis=1)])
    teacher_max, student_max = jnp.max(spread(tops, "tensor"), axis=0)
    offset = lax.axis_index("tensor") * voc_local
    column_ids = offset + lax.broadcasted_iota(jnp.int32, (tok_block, voc_local), 1)
    onehot = (column_ids == targets[:, None]).astype(f32)
    p_terms = jnp.exp((teacher_logits - teacher_max[:, None]) / tau)
    q_terms = jnp.exp((student_logits - student_max[:, None]) / tau)
    s_terms = jnp.exp(student_logits - student_max[:, None])
    sums = jnp.stack(
        [
            jnp.sum(p_terms, axis=1),
            jnp.sum(q_terms, axis=1),
            jnp.sum(s_terms, axis=1),
            jnp.sum(p_terms * (teacher_logits - student_logits), axis=1),
            jnp.sum(onehot * student_logits, axis=1),
        ]
    )
    p_total, q_total, s_total, cross, picked = jnp.sum(spread(sums, "tensor"), axis=0)
    kl_rows = (
        cross / (tau * p_total)
        - (teacher_max - student_max) / tau
        - jnp.log(p_total)
        + jnp.log(q_total)
    )
    row_loss = tau * tau * kl_rows + student_max + jnp.log(s_total) - picked
    loss = jnp.mean(spread(row_loss, "section"))
    p_prob = p_terms / p_total[:, None]
    q_prob = q_terms / q_total[:, None]
    s_prob = s_terms / s_total[:, None]
    grad = (tau * (q_prob - p_prob) + s_prob - onehot).astype(bf16)
    grad = spread(grad, "section").reshape(-1, voc_local)
    grad_head = lax.dot_general(
        student_all, grad, (((0,), (0,)), ((), ())), preferred_element_type=f32
    )
    rows = lax.dot_general(
        grad, student_head, (((1,), (1,)), ((), ())), preferred_element_type=f32
    )
    return loss, summed(rows, "tensor").astype(bf16), grad_head.astype(bf16)


def steps(teacher_hidden, student_hidden, teacher_head, student_head, targets):
    section_size = lax.axis_size("section")
    chips = section_size // 2
    half_way = chips // 2
    me = lax.axis_index("section")
    z, core = me // 2, me % 2
    tok_block, dt = teacher_hidden.shape
    ds = student_hidden.shape[1]
    voc_local = teacher_head.shape[1]
    half = voc_local // 2

    def along(x, step):
        perm = [
            (s, ((s // 2 + step) % chips) * 2 + s % 2) for s in range(section_size)
        ]
        return lax.ppermute(x, "section", perm)

    def swap(x):
        return lax.ppermute(x, "section", [(s, s ^ 1) for s in range(section_size)])

    student_head_sib = swap(student_head)
    teacher_head_sib = swap(teacher_head)
    hidden = spread(jnp.concatenate([teacher_hidden, student_hidden], axis=1), "tensor")

    start = chips - half_way + 2
    order = [(start + i) % chips for i in range(chips)]
    count = chips - 3

    def rolled(x, which):
        pair = x.reshape((chips, 2) + x.shape[1:])
        twice = jnp.concatenate([pair, pair], axis=0)
        out = lax.dynamic_slice(
            twice, ((z + start) % chips, which, 0, 0), (chips, 1) + x.shape[1:]
        )
        return out.reshape((chips * x.shape[1],) + x.shape[2:])

    mine, others = rolled(hidden, core), rolled(hidden, 1 - core)
    mine_sib = swap(others)
    student_part = product(
        mine[:, dt:], mine_sib[:, dt:], student_head, student_head_sib, chips
    )
    teacher_part = product(
        mine[:, :dt], mine_sib[:, :dt], teacher_head, teacher_head_sib, chips
    )

    place = jnp.stack([z, core]).astype(jnp.int32)
    split = count * tok_block
    hidden_near = (mine[:split, dt:], others[:split, dt:])
    hidden_far = (mine[split:, dt:], others[split:, dt:])

    def ring(parts, meanwhile=()):
        parts = dict(zip(order, parts))
        right, left = first(parts[half_way])
        right, left = along(right, 1), along(left, -1)
        for step in range(1, half_way):
            right, left = hop(
                right, left, parts[half_way - step], parts[half_way + step]
            )
            if step == half_way - 1:
                right, left, meanwhile = lax.optimization_barrier((right, left, meanwhile))
            right, left = along(right, 1), along(left, -1)
        return (right, left, parts[0]), meanwhile

    offset = lax.axis_index("tensor") * voc_local
    target_here = jnp.broadcast_to((targets - offset)[:, None], (tok_block, 128))

    student, _ = ring(student_part)
    teacher, (hidden_near, hidden_far) = ring(teacher_part, (hidden_near, hidden_far))
    teacher_logits, student_logits, stats = meet(teacher, student, target_here)
    own = payload(teacher_logits, student_logits, spread(stats, "tensor"), target_here)

    pieces = [[None] * chips, [None] * chips]
    right, left = list(own), list(own)
    pieces[0][0], pieces[1][0] = own
    for step in range(1, half_way):
        for side in range(2):
            right[side] = along(right[side], 1)
            left[side] = along(left[side], -1)
            pieces[side][chips - step], pieces[side][step] = right[side], left[side]

    def gathered(js):
        group = [jnp.concatenate([x[j] for j in js], axis=0) for x in pieces]
        return group, [swap(x) for x in group]

    last = [along(right[0], 1), along(left[1], -1)]
    early = {j: [x[j] for x in pieces] for j in order[:count]}
    early, last[0] = lax.optimization_barrier((early, last[0]))
    for j, pair in early.items():
        pieces[0][j], pieces[1][j] = pair
    near = gathered(order[:count])
    pieces[0][half_way], pieces[1][half_way] = last
    far = gathered(order[count:])
    sums = near_products(student_head, hidden_near, near)
    rows, grad_head = far_products(
        order, place, student_head, sums, hidden_far, far, tok_block
    )
    rows, grad_head = lax.optimization_barrier((rows, grad_head))
    extra = sum(
        jnp.sum(g[1][:, half:].astype(f32), axis=0) for group in (near, far) for g in group
    )
    loss = (extra[0] + extra[1] + extra[2]) / (tok_block * section_size)
    grad_hidden = jnp.sum(lax.all_to_all(rows, "tensor", 0, 0), axis=0).astype(bf16)
    return (loss, grad_hidden, grad_head), extra[3]


def shards(*arrays):
    fine, too_coarse = steps(*arrays)
    return lax.cond(too_coarse > 0.0, lambda: plain(*arrays), lambda: fine)


def solution(mesh):
    placed = (
        P("tensor", "section"),
        P("tensor", "section"),
        P("section", "tensor"),
        P("section", "tensor"),
        P("section"),
    )
    return jax.shard_map(
        shards,
        mesh=mesh,
        in_specs=placed,
        out_specs=(P(), P("tensor", "section"), P("section", "tensor")),
        check_vma=False,
    )
```

```python
import functools

import jax
import jax.numpy as jnp
from jax import lax
from jax.experimental import pallas as pl
from jax.experimental.pallas import tpu as pltpu
from jax.sharding import PartitionSpec as P

tau = 2.0
f32 = jnp.float32
bf16 = jnp.bfloat16
i16 = jnp.int16

LEVELS = 32767.0
CODES = 128
LIMIT = 1000.0
STRIP = 512
PARAMS = pltpu.CompilerParams(vmem_limit_bytes=20 * 1024 * 1024)


def row_codes(ref):
    w = ref.shape[1] - CODES
    codes = ref[:, w:].astype(jnp.int32).astype(f32)
    middle = codes[:, 0:1] * 0.25
    scale = codes[:, 32:33] * (0.5 / LEVELS)
    return middle, scale, codes[:, 64:65]


def encode(x_ref, columns, o_ref, spent):
    lo, hi = columns
    top = bottom = None
    for at in range(lo, hi, STRIP):
        x = x_ref[:, at : at + STRIP]
        top = x if top is None else jnp.maximum(top, x)
        bottom = x if bottom is None else jnp.minimum(bottom, x)
    top = jnp.max(top, axis=1, keepdims=True)
    bottom = jnp.min(bottom, axis=1, keepdims=True)
    middle_code = jnp.round((top + bottom) * 2.0)
    middle = middle_code * 0.25
    reach = jnp.maximum(top - middle, middle - bottom)
    reach_code = jnp.floor(reach * 2.0) + 1.0
    spent_code = jnp.minimum(spent + reach_code, LEVELS)
    inverse = (2.0 * LEVELS) / reach_code
    for at in range(lo, hi, STRIP):
        code = jnp.round((x_ref[:, at : at + STRIP] - middle) * inverse)
        o_ref[:, at - lo : at - lo + STRIP] = code.astype(jnp.int32).astype(i16)
    lane = lax.broadcasted_iota(jnp.int32, (x_ref.shape[0], CODES), 1)
    codes = jnp.where(lane < 32, middle_code, jnp.where(lane < 64, reach_code, spent_code))
    o_ref[:, hi - lo :] = codes.astype(jnp.int32).astype(i16)


def first_kernel(part_ref, right_ref, left_ref):
    rows, width = part_ref.shape
    none = jnp.zeros((rows, 1), f32)
    encode(part_ref, (0, width // 2), right_ref, none)
    encode(part_ref, (width // 2, width), left_ref, none)


def hop_kernel(r_ref, l_ref, pr_ref, pl_ref, ro_ref, lo_ref, sum_ref):
    width = pr_ref.shape[1]
    for in_ref, part_ref, out_ref, at_end in (
        (r_ref, pr_ref, ro_ref, False),
        (l_ref, pl_ref, lo_ref, True),
    ):
        carried = in_ref.shape[1] - CODES
        start = width - carried if at_end else 0
        middle, scale, spent = row_codes(in_ref)
        for at in range(0, width, STRIP):
            x = part_ref[:, at : at + STRIP]
            if start <= at < start + carried:
                code = in_ref[:, at - start : at - start + STRIP]
                x = x + (middle + code.astype(jnp.int32).astype(f32) * scale)
            sum_ref[:, at : at + STRIP] = x
        encode(sum_ref, (0, width), out_ref, spent)


def meet_kernel(
    rt_ref, lt_ref, pt_ref, rs_ref, ls_ref, ps_ref, target_ref, t_ref, s_ref, stats_ref
):
    rows, width = t_ref.shape
    tops, spents = [], []
    for r_ref, l_ref, part_ref, out_ref in (
        (rt_ref, lt_ref, pt_ref, t_ref),
        (rs_ref, ls_ref, ps_ref, s_ref),
    ):
        r_middle, r_scale, r_spent = row_codes(r_ref)
        l_middle, l_scale, l_spent = row_codes(l_ref)
        top = None
        for at in range(0, width, STRIP):
            strip = slice(at, at + STRIP)
            x = (
                part_ref[:, strip]
                + (r_middle + r_ref[:, strip].astype(jnp.int32).astype(f32) * r_scale)
                + (l_middle + l_ref[:, strip].astype(jnp.int32).astype(f32) * l_scale)
            )
            out_ref[:, strip] = x
            top = x if top is None else jnp.maximum(top, x)
        tops.append(jnp.max(top, axis=1, keepdims=True))
        spents.append((r_spent + l_spent) * 0.5)
    t_max, s_max = tops
    target = target_ref[:, 0:1]
    sums = None
    for at in range(0, width, 128):
        t, s = t_ref[:, at : at + 128], s_ref[:, at : at + 128]
        p = jnp.exp((t - t_max) * (1.0 / tau))
        q = jnp.exp((s - s_max) * (1.0 / tau))
        ids = at + lax.broadcasted_iota(jnp.int32, t.shape, 1)
        terms = (p, q, q * q, p * (t - s), jnp.where(ids == target, s, 0.0))
        sums = terms if sums is None else [a + b for a, b in zip(sums, terms)]
    lane = lax.broadcasted_iota(jnp.int32, (rows, 128), 1)
    kinds = [t_max, s_max] + [jnp.sum(a, axis=1, keepdims=True) for a in sums]
    kinds.append(jnp.maximum(spents[0], spents[1]))
    table = jnp.zeros((rows, 128), f32)
    for k, value in enumerate(kinds):
        table = jnp.where(lane == k, value, table)
    table = jnp.concatenate([table, jnp.zeros((128 - rows, 128), f32)], axis=0)
    stats_ref[...] = table.T[0:8, :]


def grad_kernel(t_ref, s_ref, every_ref, target_ref, a_ref, b_ref):
    rows, width = t_ref.shape
    t_tops, s_tops = every_ref[:, 0, :], every_ref[:, 1, :]
    t_max = jnp.max(t_tops, axis=0, keepdims=True)
    s_max = jnp.max(s_tops, axis=0, keepdims=True)
    t_weight = jnp.exp((t_tops - t_max) * (1.0 / tau))
    q_weight = jnp.exp((s_tops - s_max) * (1.0 / tau))
    s_weight = jnp.exp(s_tops - s_max)

    def total(k, weight):
        return jnp.sum(every_ref[:, k, :] * weight, axis=0, keepdims=True)

    p_total, q_total = total(2, t_weight), total(3, q_weight)
    s_total, cross = total(4, s_weight), total(5, t_weight)
    picked = jnp.sum(every_ref[:, 6, :], axis=0, keepdims=True)
    spent = jnp.max(every_ref[:, 7, :], axis=0, keepdims=True)
    kl_rows = (
        cross / (tau * p_total)
        - (t_max - s_max) / tau
        - jnp.log(p_total)
        + jnp.log(q_total)
    )
    row_loss = tau * tau * kl_rows + s_max + jnp.log(s_total) - picked
    flag = jnp.where(spent > LIMIT, 1.0, 0.0)
    lines = [t_max, s_max, tau / p_total, tau / q_total, 1.0 / s_total, row_loss, flag]
    lines.append(jnp.zeros((128 - len(lines), 128), f32))
    table = jnp.concatenate(lines, axis=0).T[:rows]
    t_max, s_max, p_scale, q_scale, s_scale, row_loss, flag = (
        table[:, k : k + 1] for k in range(7)
    )
    target = target_ref[:, 0:1]
    for at in range(0, width, STRIP):
        t, s = t_ref[:, at : at + STRIP], s_ref[:, at : at + STRIP]
        p = jnp.exp((t - t_max) * (1.0 / tau))
        q = jnp.exp((s - s_max) * (1.0 / tau))
        ids = at + lax.broadcasted_iota(jnp.int32, t.shape, 1)
        grad = q * q_scale - p * p_scale + (q * q) * s_scale
        grad = grad - jnp.where(ids == target, 1.0, 0.0)
        o_ref, to = (a_ref, at) if at < width // 2 else (b_ref, at - width // 2)
        o_ref[:, to : to + STRIP] = grad.astype(bf16)
    high = row_loss.astype(bf16).astype(f32)
    mid = (row_loss - high).astype(bf16).astype(f32)
    low = row_loss - high - mid
    lane = lax.broadcasted_iota(jnp.int32, (rows, CODES), 1)
    extra = jnp.where(
        lane == 0,
        high,
        jnp.where(lane == 1, mid, jnp.where(lane == 2, low, jnp.where(lane == 3, flag, 0.0))),
    )
    b_ref[:, width // 2 :] = extra.astype(bf16)


VMEM = pl.BlockSpec(memory_space=pltpu.VMEM)


def call(kernel, name, out, *operands, flops=0, **more):
    leaves = jax.tree.leaves((out, operands))
    return pl.pallas_call(
        kernel,
        out_shape=out,
        in_specs=[VMEM] * len(operands),
        out_specs=jax.tree.map(lambda _: VMEM, out),
        compiler_params=PARAMS,
        cost_estimate=pl.CostEstimate(
            flops=flops,
            bytes_accessed=sum(x.size * x.dtype.itemsize for x in leaves),
            transcendentals=0,
        ),
        name=name,
        **more,
    )(*operands)


def first(part):
    rows, width = part.shape
    out = jax.ShapeDtypeStruct((rows, width // 2 + CODES), i16)
    return call(first_kernel, "first", (out, out), part)


def hop(right, left, part_right, part_left):
    rows, width = part_right.shape
    out = jax.ShapeDtypeStruct((rows, width + CODES), i16)
    return call(
        hop_kernel, "hop", (out, out), right, left, part_right, part_left,
        scratch_shapes=[pltpu.VMEM((rows, width), f32)],
    )


def meet(teacher, student, target):
    rows, width = teacher[2].shape
    logits = jax.ShapeDtypeStruct((rows, width), f32)
    stats = jax.ShapeDtypeStruct((8, 128), f32)
    return call(meet_kernel, "meet", (logits, logits, stats), *teacher, *student, target)


def payload(teacher_logits, student_logits, every, target):
    rows, width = teacher_logits.shape
    out = (
        jax.ShapeDtypeStruct((rows, width // 2), bf16),
        jax.ShapeDtypeStruct((rows, width // 2 + CODES), bf16),
    )
    return call(
        grad_kernel, "payload", out, teacher_logits, student_logits, every, target
    )


def fan_kernel(t_ref, s_ref, o_ref):
    dt = t_ref.shape[1]
    for k in range(o_ref.shape[0]):
        o_ref[k, :, :dt] = t_ref[...]
        o_ref[k, :, dt:] = s_ref[...]


def product_kernel(own_ref, sib_ref, head_ref, head_sib_ref, *o_refs):
    rows, width = o_refs[0].shape
    step = min(width, 2 * STRIP)
    for at in range(0, width, step):
        strip = slice(at, at + step)
        x = jnp.dot(own_ref[...], head_ref[:, strip], preferred_element_type=f32)
        x = x + jnp.dot(sib_ref[...], head_sib_ref[:, strip], preferred_element_type=f32)
        for k, o_ref in enumerate(o_refs):
            o_ref[:, strip] = x[k * rows : (k + 1) * rows]


def product(own, sib, head, head_sib, blocks):
    tokens, depth = own.shape
    width = head.shape[1]
    out = jax.ShapeDtypeStruct((tokens // blocks, width), f32)
    return call(
        product_kernel, "product", (out,) * blocks, own, sib, head, head_sib,
        flops=4 * tokens * depth * width,
    )


def back(group, head_ref):
    depth = head_ref.shape[1] // 2
    turned = (((1,), (1,)), ((), ()))
    return lax.dot_general(
        group[0][...], head_ref[:, :depth], turned, preferred_element_type=f32
    ) + lax.dot_general(
        group[1][:, :depth], head_ref[:, depth:], turned, preferred_element_type=f32
    )


def outer(hidden, groups, store, ready):
    half = groups[0][0].shape[1]
    for side in range(2):
        ready(side)
        for at in range(0, half, STRIP):
            total = sum(
                lax.dot_general(
                    x[...],
                    group[side][:, at : at + STRIP],
                    (((0,), (0,)), ((), ())),
                    preferred_element_type=f32,
                )
                for x, group in zip(hidden, groups)
            )
            store(side * half + at, total)


def near_kernel(head_ref, a0, b0, a1, b1, rows0_ref, rows1_ref):
    rows0_ref[...] = back((a0, b0), head_ref)
    rows1_ref[...] = back((a1, b1), head_ref)


def far_kernel(order, place_ref, head_ref, near0, near1, a0, b0, a1, b1, rows_ref):
    z, core = place_ref[0], place_ref[1]
    blocks, rows = rows_ref.shape[:2]
    chips = blocks // 2
    for near, group, which in (
        (near0, (a0, b0), core), (near1, (a1, b1), 1 - core)
    ):
        far = back(group, head_ref)
        count = near.shape[0] // rows
        for i, j in enumerate(order):
            x = near[i * rows : (i + 1) * rows] if i < count else (
                far[(i - count) * rows : (i - count + 1) * rows]
            )
            at = 2 * lax.rem(z + j, chips) + which
            rows_ref[pl.ds(at, 1)] = x[None]


def outer_kernel(n, *refs):
    hidden, sources, refs = refs[:n], refs[n : 3 * n], refs[3 * n :]
    o_hbm, *held, o_ref, in_sems, out_sems = refs
    loads = [
        pltpu.make_async_copy(x, y, in_sems.at[k])
        for k, (x, y) in enumerate(zip(sources, held))
    ]
    for load in loads[0::2] + loads[1::2]:
        load.start()
    stores = []

    def store(at, total):
        o_ref[:, at : at + STRIP] = total.astype(bf16)
        strip = pl.ds(at, STRIP)
        stores.append(
            pltpu.make_async_copy(
                o_ref.at[:, strip], o_hbm.at[:, strip], out_sems.at[len(stores)]
            )
        )
        stores[-1].start()

    groups = list(zip(held[0::2], held[1::2]))
    outer(hidden, groups, store, lambda side: [x.wait() for x in loads[side::2]])
    for copy in stores:
        copy.wait()


def near_products(head, groups):
    rows = jax.ShapeDtypeStruct((groups[0][0].shape[0], head.shape[0]), f32)
    return call(
        near_kernel, "near", (rows, rows), head, *groups[0], *groups[1],
        flops=4 * rows.size * head.shape[1],
    )


def far_products(order, place, head, near, groups, rows):
    out = jax.ShapeDtypeStruct((2 * len(order), rows, head.shape[0]), f32)
    return pl.pallas_call(
        functools.partial(far_kernel, order),
        out_shape=out,
        in_specs=[pl.BlockSpec(memory_space=pltpu.SMEM)] + [VMEM] * 7,
        out_specs=VMEM,
        compiler_params=PARAMS,
        name="far",
    )(place, head, *near, *groups[0], *groups[1])


def outer_products(hidden, groups):
    arrays = [x for group in groups for x in group]
    n = len(hidden)
    out = jax.ShapeDtypeStruct((hidden[0].shape[1], 2 * arrays[0].shape[1]), bf16)
    hbm = pl.BlockSpec(memory_space=pltpu.HBM)
    return pl.pallas_call(
        functools.partial(outer_kernel, n),
        out_shape=out,
        in_specs=[VMEM] * n + [hbm] * len(arrays),
        out_specs=hbm,
        scratch_shapes=[pltpu.VMEM(x.shape, x.dtype) for x in arrays]
        + [
            pltpu.VMEM(out.shape, bf16),
            pltpu.SemaphoreType.DMA((len(arrays),)),
            pltpu.SemaphoreType.DMA((out.shape[1] // STRIP,)),
        ],
        compiler_params=PARAMS,
        cost_estimate=pl.CostEstimate(
            flops=2 * out.size * sum(x.shape[0] for x in hidden),
            bytes_accessed=sum(2 * x.size for x in arrays) + 2 * out.size,
            transcendentals=0,
        ),
        name="outer",
    )(*hidden, *arrays)


def spread(x, axis):
    n = lax.axis_size(axis)
    return lax.all_to_all(jnp.broadcast_to(x[None], (n,) + x.shape), axis, 0, 0)


def summed(x, axis):
    n = lax.axis_size(axis)
    blocks = x.reshape((n, x.shape[0] // n) + x.shape[1:])
    return jnp.sum(lax.all_to_all(blocks, axis, 0, 0), axis=0)


def plain(teacher_hidden, student_hidden, teacher_head, student_head, targets):
    tok_block, voc_local = targets.shape[0], teacher_head.shape[1]
    teacher_all = spread(teacher_hidden, "tensor").reshape(-1, teacher_hidden.shape[1])
    student_all = spread(student_hidden, "tensor").reshape(-1, student_hidden.shape[1])
    teacher_logits = summed(
        jnp.dot(teacher_all, teacher_head, preferred_element_type=f32), "section"
    )
    student_logits = summed(
        jnp.dot(student_all, student_head, preferred_element_type=f32), "section"
    )
    tops = jnp.stack([jnp.max(teacher_logits, axis=1), jnp.max(student_logits, axis=1)])
    teacher_max, student_max = jnp.max(spread(tops, "tensor"), axis=0)
    offset = lax.axis_index("tensor") * voc_local
    column_ids = offset + lax.broadcasted_iota(jnp.int32, (tok_block, voc_local), 1)
    onehot = (column_ids == targets[:, None]).astype(f32)
    p_terms = jnp.exp((teacher_logits - teacher_max[:, None]) / tau)
    q_terms = jnp.exp((student_logits - student_max[:, None]) / tau)
    s_terms = jnp.exp(student_logits - student_max[:, None])
    sums = jnp.stack(
        [
            jnp.sum(p_terms, axis=1),
            jnp.sum(q_terms, axis=1),
            jnp.sum(s_terms, axis=1),
            jnp.sum(p_terms * (teacher_logits - student_logits), axis=1),
            jnp.sum(onehot * student_logits, axis=1),
        ]
    )
    p_total, q_total, s_total, cross, picked = jnp.sum(spread(sums, "tensor"), axis=0)
    kl_rows = (
        cross / (tau * p_total)
        - (teacher_max - student_max) / tau
        - jnp.log(p_total)
        + jnp.log(q_total)
    )
    row_loss = tau * tau * kl_rows + student_max + jnp.log(s_total) - picked
    loss = jnp.mean(spread(row_loss, "section"))
    p_prob = p_terms / p_total[:, None]
    q_prob = q_terms / q_total[:, None]
    s_prob = s_terms / s_total[:, None]
    grad = (tau * (q_prob - p_prob) + s_prob - onehot).astype(bf16)
    grad = spread(grad, "section").reshape(-1, voc_local)
    grad_head = lax.dot_general(
        student_all, grad, (((0,), (0,)), ((), ())), preferred_element_type=f32
    )
    rows = lax.dot_general(
        grad, student_head, (((1,), (1,)), ((), ())), preferred_element_type=f32
    )
    return loss, summed(rows, "tensor").astype(bf16), grad_head.astype(bf16)


def steps(teacher_hidden, student_hidden, teacher_head, student_head, targets):
    section_size = lax.axis_size("section")
    chips = section_size // 2
    half_way = chips // 2
    me = lax.axis_index("section")
    z, core = me // 2, me % 2
    tok_block, dt = teacher_hidden.shape
    ds = student_hidden.shape[1]
    voc_local = teacher_head.shape[1]
    half = voc_local // 2

    def along(x, step):
        perm = [
            (s, ((s // 2 + step) % chips) * 2 + s % 2) for s in range(section_size)
        ]
        return lax.ppermute(x, "section", perm)

    def swap(x):
        return lax.ppermute(x, "section", [(s, s ^ 1) for s in range(section_size)])

    student_head_sib = swap(student_head)
    teacher_head_sib = swap(teacher_head)
    copies = jax.ShapeDtypeStruct((lax.axis_size("tensor"), tok_block, dt + ds), bf16)
    hidden = lax.all_to_all(
        call(fan_kernel, "fan", copies, teacher_hidden, student_hidden), "tensor", 0, 0
    )

    start = chips - half_way + 2
    order = [(start + i) % chips for i in range(chips)]
    count = chips - 3

    def rolled(x, which):
        pair = x.reshape((chips, 2) + x.shape[1:])
        twice = jnp.concatenate([pair, pair], axis=0)
        out = lax.dynamic_slice(
            twice, ((z + start) % chips, which, 0, 0), (chips, 1) + x.shape[1:]
        )
        return out.reshape((chips * x.shape[1],) + x.shape[2:])

    mine, others = rolled(hidden, core), rolled(hidden, 1 - core)
    mine_sib = swap(others)
    student_part = product(
        mine[:, dt:], mine_sib[:, dt:], student_head, student_head_sib, chips
    )
    teacher_part = product(
        mine[:, :dt], mine_sib[:, :dt], teacher_head, teacher_head_sib, chips
    )

    place = jnp.stack([z, core]).astype(jnp.int32)
    split = count * tok_block
    hidden_near = (mine[:split, dt:], others[:split, dt:])
    hidden_far = (mine[split:, dt:], others[split:, dt:])

    def ring(parts, meanwhile=()):
        parts = dict(zip(order, parts))
        right, left = first(parts[half_way])
        right, left = along(right, 1), along(left, -1)
        for step in range(1, half_way):
            right, left = hop(
                right, left, parts[half_way - step], parts[half_way + step]
            )
            if step == half_way - 1:
                right, left, meanwhile = lax.optimization_barrier((right, left, meanwhile))
            right, left = along(right, 1), along(left, -1)
        return (right, left, parts[0]), meanwhile

    offset = lax.axis_index("tensor") * voc_local
    target_here = jnp.broadcast_to((targets - offset)[:, None], (tok_block, 128))

    student, _ = ring(student_part)
    teacher, (hidden_near, hidden_far) = ring(teacher_part, (hidden_near, hidden_far))
    teacher_logits, student_logits, stats = meet(teacher, student, target_here)
    own = payload(teacher_logits, student_logits, spread(stats, "tensor"), target_here)

    pieces = [[None] * chips, [None] * chips]
    right, left = list(own), list(own)
    pieces[0][0], pieces[1][0] = own
    for step in range(1, half_way):
        for side in range(2):
            right[side] = along(right[side], 1)
            left[side] = along(left[side], -1)
            pieces[side][chips - step], pieces[side][step] = right[side], left[side]

    def gathered(js):
        group = [jnp.concatenate([x[j] for j in js], axis=0) for x in pieces]
        return group, [swap(x) for x in group]

    last = [along(right[0], 1), along(left[1], -1)]
    early = {j: [x[j] for x in pieces] for j in order[:count]}
    early, last[0] = lax.optimization_barrier((early, last[0]))
    for j, pair in early.items():
        pieces[0][j], pieces[1][j] = pair
    near = gathered(order[:count])
    pieces[0][half_way], pieces[1][half_way] = last
    far = gathered(order[count:])
    sums = near_products(student_head, near)
    rows = far_products(order, place, student_head, sums, far, tok_block)
    grad_head = outer_products((*hidden_near, *hidden_far), (*near, *far))
    extra = sum(
        jnp.sum(g[1][:, half:].astype(f32), axis=0) for group in (near, far) for g in group
    )
    loss = (extra[0] + extra[1] + extra[2]) / (tok_block * section_size)
    grad_hidden = jnp.sum(lax.all_to_all(rows, "tensor", 0, 0), axis=0).astype(bf16)
    return (loss, grad_hidden, grad_head), extra[3]


def shards(*arrays):
    fine, too_coarse = steps(*arrays)
    return lax.cond(too_coarse > 0.0, lambda: plain(*arrays), lambda: fine)


def solution(mesh):
    placed = (
        P("tensor", "section"),
        P("tensor", "section"),
        P("section", "tensor"),
        P("section", "tensor"),
        P("section"),
    )
    return jax.shard_map(
        shards,
        mesh=mesh,
        in_specs=placed,
        out_specs=(P(), P("tensor", "section"), P("section", "tensor")),
        check_vma=False,
    )
```

```python
import functools

import jax
import jax.numpy as jnp
from jax import lax
from jax.experimental import pallas as pl
from jax.experimental.pallas import tpu as pltpu
from jax.sharding import PartitionSpec as P

tau = 2.0
f32 = jnp.float32
bf16 = jnp.bfloat16
i16 = jnp.int16

LEVELS = 32767.0
CODES = 128
LIMIT = 1000.0
STRIP = 512
PARAMS = pltpu.CompilerParams(vmem_limit_bytes=20 * 1024 * 1024)


def row_codes(ref):
    w = ref.shape[1] - CODES
    codes = ref[:, w:].astype(jnp.int32).astype(f32)
    middle = codes[:, 0:1] * 0.25
    scale = codes[:, 32:33] * (0.5 / LEVELS)
    return middle, scale, codes[:, 64:65]


def encode(x_ref, columns, o_ref, spent):
    lo, hi = columns
    top = bottom = None
    for at in range(lo, hi, STRIP):
        x = x_ref[:, at : at + STRIP]
        top = x if top is None else jnp.maximum(top, x)
        bottom = x if bottom is None else jnp.minimum(bottom, x)
    top = jnp.max(top, axis=1, keepdims=True)
    bottom = jnp.min(bottom, axis=1, keepdims=True)
    middle_code = jnp.round((top + bottom) * 2.0)
    middle = middle_code * 0.25
    reach = jnp.maximum(top - middle, middle - bottom)
    reach_code = jnp.floor(reach * 2.0) + 1.0
    spent_code = jnp.minimum(spent + reach_code, LEVELS)
    inverse = (2.0 * LEVELS) / reach_code
    for at in range(lo, hi, STRIP):
        code = jnp.round((x_ref[:, at : at + STRIP] - middle) * inverse)
        o_ref[:, at - lo : at - lo + STRIP] = code.astype(jnp.int32).astype(i16)
    lane = lax.broadcasted_iota(jnp.int32, (x_ref.shape[0], CODES), 1)
    codes = jnp.where(lane < 32, middle_code, jnp.where(lane < 64, reach_code, spent_code))
    o_ref[:, hi - lo :] = codes.astype(jnp.int32).astype(i16)


def first_kernel(part_ref, right_ref, left_ref):
    rows, width = part_ref.shape
    none = jnp.zeros((rows, 1), f32)
    encode(part_ref, (0, width // 2), right_ref, none)
    encode(part_ref, (width // 2, width), left_ref, none)


def hop_kernel(r_ref, l_ref, pr_ref, pl_ref, ro_ref, lo_ref, sum_ref):
    width = pr_ref.shape[1]
    for in_ref, part_ref, out_ref, at_end in (
        (r_ref, pr_ref, ro_ref, False),
        (l_ref, pl_ref, lo_ref, True),
    ):
        carried = in_ref.shape[1] - CODES
        start = width - carried if at_end else 0
        middle, scale, spent = row_codes(in_ref)
        for at in range(0, width, STRIP):
            x = part_ref[:, at : at + STRIP]
            if start <= at < start + carried:
                code = in_ref[:, at - start : at - start + STRIP]
                x = x + (middle + code.astype(jnp.int32).astype(f32) * scale)
            sum_ref[:, at : at + STRIP] = x
        encode(sum_ref, (0, width), out_ref, spent)


def meet_kernel(
    rt_ref, lt_ref, pt_ref, rs_ref, ls_ref, ps_ref, target_ref, t_ref, s_ref, stats_ref
):
    rows, width = t_ref.shape
    tops, spents = [], []
    for r_ref, l_ref, part_ref, out_ref in (
        (rt_ref, lt_ref, pt_ref, t_ref),
        (rs_ref, ls_ref, ps_ref, s_ref),
    ):
        r_middle, r_scale, r_spent = row_codes(r_ref)
        l_middle, l_scale, l_spent = row_codes(l_ref)
        top = None
        for at in range(0, width, STRIP):
            strip = slice(at, at + STRIP)
            x = (
                part_ref[:, strip]
                + (r_middle + r_ref[:, strip].astype(jnp.int32).astype(f32) * r_scale)
                + (l_middle + l_ref[:, strip].astype(jnp.int32).astype(f32) * l_scale)
            )
            out_ref[:, strip] = x
            top = x if top is None else jnp.maximum(top, x)
        tops.append(jnp.max(top, axis=1, keepdims=True))
        spents.append((r_spent + l_spent) * 0.5)
    t_max, s_max = tops
    target = target_ref[:, 0:1]
    sums = None
    for at in range(0, width, 128):
        t, s = t_ref[:, at : at + 128], s_ref[:, at : at + 128]
        p = jnp.exp((t - t_max) * (1.0 / tau))
        q = jnp.exp((s - s_max) * (1.0 / tau))
        ids = at + lax.broadcasted_iota(jnp.int32, t.shape, 1)
        terms = (p, q, q * q, p * (t - s), jnp.where(ids == target, s, 0.0))
        sums = terms if sums is None else [a + b for a, b in zip(sums, terms)]
    lane = lax.broadcasted_iota(jnp.int32, (rows, 128), 1)
    kinds = [t_max, s_max] + [jnp.sum(a, axis=1, keepdims=True) for a in sums]
    kinds.append(jnp.maximum(spents[0], spents[1]))
    table = jnp.zeros((rows, 128), f32)
    for k, value in enumerate(kinds):
        table = jnp.where(lane == k, value, table)
    table = jnp.concatenate([table, jnp.zeros((128 - rows, 128), f32)], axis=0)
    stats_ref[...] = table.T[0:8, :]


def grad_kernel(t_ref, s_ref, every_ref, target_ref, a_ref, b_ref):
    rows, width = t_ref.shape
    t_tops, s_tops = every_ref[:, 0, :], every_ref[:, 1, :]
    t_max = jnp.max(t_tops, axis=0, keepdims=True)
    s_max = jnp.max(s_tops, axis=0, keepdims=True)
    t_weight = jnp.exp((t_tops - t_max) * (1.0 / tau))
    q_weight = jnp.exp((s_tops - s_max) * (1.0 / tau))
    s_weight = jnp.exp(s_tops - s_max)

    def total(k, weight):
        return jnp.sum(every_ref[:, k, :] * weight, axis=0, keepdims=True)

    p_total, q_total = total(2, t_weight), total(3, q_weight)
    s_total, cross = total(4, s_weight), total(5, t_weight)
    picked = jnp.sum(every_ref[:, 6, :], axis=0, keepdims=True)
    spent = jnp.max(every_ref[:, 7, :], axis=0, keepdims=True)
    kl_rows = (
        cross / (tau * p_total)
        - (t_max - s_max) / tau
        - jnp.log(p_total)
        + jnp.log(q_total)
    )
    row_loss = tau * tau * kl_rows + s_max + jnp.log(s_total) - picked
    flag = jnp.where(spent > LIMIT, 1.0, 0.0)
    lines = [t_max, s_max, tau / p_total, tau / q_total, 1.0 / s_total, row_loss, flag]
    lines.append(jnp.zeros((128 - len(lines), 128), f32))
    table = jnp.concatenate(lines, axis=0).T[:rows]
    t_max, s_max, p_scale, q_scale, s_scale, row_loss, flag = (
        table[:, k : k + 1] for k in range(7)
    )
    target = target_ref[:, 0:1]
    for at in range(0, width, STRIP):
        t, s = t_ref[:, at : at + STRIP], s_ref[:, at : at + STRIP]
        p = jnp.exp((t - t_max) * (1.0 / tau))
        q = jnp.exp((s - s_max) * (1.0 / tau))
        ids = at + lax.broadcasted_iota(jnp.int32, t.shape, 1)
        grad = q * q_scale - p * p_scale + (q * q) * s_scale
        grad = grad - jnp.where(ids == target, 1.0, 0.0)
        o_ref, to = (a_ref, at) if at < width // 2 else (b_ref, at - width // 2)
        o_ref[:, to : to + STRIP] = grad.astype(bf16)
    high = row_loss.astype(bf16).astype(f32)
    mid = (row_loss - high).astype(bf16).astype(f32)
    low = row_loss - high - mid
    lane = lax.broadcasted_iota(jnp.int32, (rows, CODES), 1)
    extra = jnp.where(
        lane == 0,
        high,
        jnp.where(lane == 1, mid, jnp.where(lane == 2, low, jnp.where(lane == 3, flag, 0.0))),
    )
    b_ref[:, width // 2 :] = extra.astype(bf16)


VMEM = pl.BlockSpec(memory_space=pltpu.VMEM)


def call(kernel, name, out, *operands, flops=0, **more):
    leaves = jax.tree.leaves((out, operands))
    return pl.pallas_call(
        kernel,
        out_shape=out,
        in_specs=[VMEM] * len(operands),
        out_specs=jax.tree.map(lambda _: VMEM, out),
        compiler_params=PARAMS,
        cost_estimate=pl.CostEstimate(
            flops=flops,
            bytes_accessed=sum(x.size * x.dtype.itemsize for x in leaves),
            transcendentals=0,
        ),
        name=name,
        **more,
    )(*operands)


def first(part):
    rows, width = part.shape
    out = jax.ShapeDtypeStruct((rows, width // 2 + CODES), i16)
    return call(first_kernel, "first", (out, out), part)


def hop(right, left, part_right, part_left):
    rows, width = part_right.shape
    out = jax.ShapeDtypeStruct((rows, width + CODES), i16)
    return call(
        hop_kernel, "hop", (out, out), right, left, part_right, part_left,
        scratch_shapes=[pltpu.VMEM((rows, width), f32)],
    )


def meet(teacher, student, target):
    rows, width = teacher[2].shape
    logits = jax.ShapeDtypeStruct((rows, width), f32)
    stats = jax.ShapeDtypeStruct((8, 128), f32)
    return call(meet_kernel, "meet", (logits, logits, stats), *teacher, *student, target)


def payload(teacher_logits, student_logits, every, target):
    rows, width = teacher_logits.shape
    out = (
        jax.ShapeDtypeStruct((rows, width // 2), bf16),
        jax.ShapeDtypeStruct((rows, width // 2 + CODES), bf16),
    )
    return call(
        grad_kernel, "payload", out, teacher_logits, student_logits, every, target
    )


def product_kernel(own_ref, sib_ref, head_ref, head_sib_ref, *o_refs):
    rows, width = o_refs[0].shape
    step = min(width, 2 * STRIP)
    for at in range(0, width, step):
        strip = slice(at, at + step)
        x = jnp.dot(own_ref[...], head_ref[:, strip], preferred_element_type=f32)
        x = x + jnp.dot(sib_ref[...], head_sib_ref[:, strip], preferred_element_type=f32)
        for k, o_ref in enumerate(o_refs):
            o_ref[:, strip] = x[k * rows : (k + 1) * rows]


def product(own, sib, head, head_sib, blocks):
    tokens, depth = own.shape
    width = head.shape[1]
    out = jax.ShapeDtypeStruct((tokens // blocks, width), f32)
    return call(
        product_kernel, "product", (out,) * blocks, own, sib, head, head_sib,
        flops=4 * tokens * depth * width,
    )


def back(group, head_ref):
    depth = head_ref.shape[1] // 2
    turned = (((1,), (1,)), ((), ()))
    return lax.dot_general(
        group[0][...], head_ref[:, :depth], turned, preferred_element_type=f32
    ) + lax.dot_general(
        group[1][:, :depth], head_ref[:, depth:], turned, preferred_element_type=f32
    )


def outer(hidden, groups, store):
    half = groups[0][0].shape[1]
    for side in range(2):
        for at in range(0, half, STRIP):
            total = sum(
                lax.dot_general(
                    x[...],
                    group[side][:, at : at + STRIP],
                    (((0,), (0,)), ((), ())),
                    preferred_element_type=f32,
                )
                for x, group in zip(hidden, groups)
            )
            store(side * half + at, total)


def own_kernel(head_ref, h0, h1, a0, b0, a1, b1, rows0_ref, rows1_ref, acc_ref):
    rows0_ref[...] = back((a0, b0), head_ref)
    rows1_ref[...] = back((a1, b1), head_ref)

    def store(at, total):
        acc_ref[:, at : at + STRIP] = total

    outer((h0, h1), ((a0, b0), (a1, b1)), store)


def sib_kernel(
    order, place_ref, head_ref, near0, near1, acc_ref, h0, h1, a0, b0, a1, b1,
    rows_hbm, o_hbm, rows_ref, o_ref, sems,
):
    z, core = place_ref[0], place_ref[1]
    blocks, rows = rows_ref.shape[:2]
    chips = blocks // 2
    own = (near0[...], near1[...])
    sib = (back((a0, b0), head_ref), back((a1, b1), head_ref))
    count = near0.shape[0] // rows
    for (near, far), which in ((own, core), (sib, 1 - core)):
        for i, j in enumerate(order):
            x = near[i * rows : (i + 1) * rows] if i < count else (
                far[(i - count) * rows : (i - count + 1) * rows]
            )
            at = 2 * lax.rem(z + j, chips) + which
            rows_ref[pl.ds(at, 1)] = x[None]
    copies = [pltpu.make_async_copy(rows_ref, rows_hbm, sems.at[0])]
    copies[0].start()

    def store(at, total):
        o_ref[:, at : at + STRIP] = (acc_ref[:, at : at + STRIP] + total).astype(bf16)
        strip = pl.ds(at, STRIP)
        copies.append(
            pltpu.make_async_copy(
                o_ref.at[:, strip], o_hbm.at[:, strip], sems.at[len(copies)]
            )
        )
        copies[-1].start()

    outer((h0, h1), ((a0, b0), (a1, b1)), store)
    for copy in copies:
        copy.wait()


def own_products(head, hidden, groups):
    depth, width = head.shape
    rows = tuple(jax.ShapeDtypeStruct((x.shape[0], depth), f32) for x in hidden)
    acc = jax.ShapeDtypeStruct((depth, width), f32)
    return call(
        own_kernel, "own", (*rows, acc), head, *hidden, *groups[0], *groups[1],
        flops=4 * depth * width * sum(x.shape[0] for x in hidden),
    )


def sib_products(order, place, head, own, hidden, groups, rows):
    depth, width = head.shape
    blocks = 2 * len(order)
    hbm = pl.BlockSpec(memory_space=pltpu.HBM)
    return pl.pallas_call(
        functools.partial(sib_kernel, order),
        out_shape=(
            jax.ShapeDtypeStruct((blocks, rows, depth), f32),
            jax.ShapeDtypeStruct((depth, width), bf16),
        ),
        in_specs=[pl.BlockSpec(memory_space=pltpu.SMEM)] + [VMEM] * 10,
        out_specs=(hbm, hbm),
        scratch_shapes=[
            pltpu.VMEM((blocks, rows, depth), f32),
            pltpu.VMEM((depth, width), bf16),
            pltpu.SemaphoreType.DMA((1 + width // STRIP,)),
        ],
        compiler_params=PARAMS,
        name="sib",
    )(place, head, *own, *hidden, *groups[0], *groups[1])


def spread(x, axis):
    n = lax.axis_size(axis)
    return lax.all_to_all(jnp.broadcast_to(x[None], (n,) + x.shape), axis, 0, 0)


def summed(x, axis):
    n = lax.axis_size(axis)
    blocks = x.reshape((n, x.shape[0] // n) + x.shape[1:])
    return jnp.sum(lax.all_to_all(blocks, axis, 0, 0), axis=0)


def plain(teacher_hidden, student_hidden, teacher_head, student_head, targets):
    tok_block, voc_local = targets.shape[0], teacher_head.shape[1]
    teacher_all = spread(teacher_hidden, "tensor").reshape(-1, teacher_hidden.shape[1])
    student_all = spread(student_hidden, "tensor").reshape(-1, student_hidden.shape[1])
    teacher_logits = summed(
        jnp.dot(teacher_all, teacher_head, preferred_element_type=f32), "section"
    )
    student_logits = summed(
        jnp.dot(student_all, student_head, preferred_element_type=f32), "section"
    )
    tops = jnp.stack([jnp.max(teacher_logits, axis=1), jnp.max(student_logits, axis=1)])
    teacher_max, student_max = jnp.max(spread(tops, "tensor"), axis=0)
    offset = lax.axis_index("tensor") * voc_local
    column_ids = offset + lax.broadcasted_iota(jnp.int32, (tok_block, voc_local), 1)
    onehot = (column_ids == targets[:, None]).astype(f32)
    p_terms = jnp.exp((teacher_logits - teacher_max[:, None]) / tau)
    q_terms = jnp.exp((student_logits - student_max[:, None]) / tau)
    s_terms = jnp.exp(student_logits - student_max[:, None])
    sums = jnp.stack(
        [
            jnp.sum(p_terms, axis=1),
            jnp.sum(q_terms, axis=1),
            jnp.sum(s_terms, axis=1),
            jnp.sum(p_terms * (teacher_logits - student_logits), axis=1),
            jnp.sum(onehot * student_logits, axis=1),
        ]
    )
    p_total, q_total, s_total, cross, picked = jnp.sum(spread(sums, "tensor"), axis=0)
    kl_rows = (
        cross / (tau * p_total)
        - (teacher_max - student_max) / tau
        - jnp.log(p_total)
        + jnp.log(q_total)
    )
    row_loss = tau * tau * kl_rows + student_max + jnp.log(s_total) - picked
    loss = jnp.mean(spread(row_loss, "section"))
    p_prob = p_terms / p_total[:, None]
    q_prob = q_terms / q_total[:, None]
    s_prob = s_terms / s_total[:, None]
    grad = (tau * (q_prob - p_prob) + s_prob - onehot).astype(bf16)
    grad = spread(grad, "section").reshape(-1, voc_local)
    grad_head = lax.dot_general(
        student_all, grad, (((0,), (0,)), ((), ())), preferred_element_type=f32
    )
    rows = lax.dot_general(
        grad, student_head, (((1,), (1,)), ((), ())), preferred_element_type=f32
    )
    return loss, summed(rows, "tensor").astype(bf16), grad_head.astype(bf16)


def steps(teacher_hidden, student_hidden, teacher_head, student_head, targets):
    section_size = lax.axis_size("section")
    chips = section_size // 2
    half_way = chips // 2
    me = lax.axis_index("section")
    z, core = me // 2, me % 2
    tok_block, dt = teacher_hidden.shape
    ds = student_hidden.shape[1]
    voc_local = teacher_head.shape[1]
    half = voc_local // 2

    def along(x, step):
        perm = [
            (s, ((s // 2 + step) % chips) * 2 + s % 2) for s in range(section_size)
        ]
        return lax.ppermute(x, "section", perm)

    def swap(x):
        return lax.ppermute(x, "section", [(s, s ^ 1) for s in range(section_size)])

    student_head_sib = swap(student_head)
    teacher_head_sib = swap(teacher_head)
    hidden = spread(jnp.concatenate([teacher_hidden, student_hidden], axis=1), "tensor")

    start = chips - half_way + 2
    order = [(start + i) % chips for i in range(chips)]
    count = chips - 3

    def rolled(x, which):
        pair = x.reshape((chips, 2) + x.shape[1:])
        twice = jnp.concatenate([pair, pair], axis=0)
        out = lax.dynamic_slice(
            twice, ((z + start) % chips, which, 0, 0), (chips, 1) + x.shape[1:]
        )
        return out.reshape((chips * x.shape[1],) + x.shape[2:])

    mine, others = rolled(hidden, core), rolled(hidden, 1 - core)
    mine_sib = swap(others)
    student_part = product(
        mine[:, dt:], mine_sib[:, dt:], student_head, student_head_sib, chips
    )
    teacher_part = product(
        mine[:, :dt], mine_sib[:, :dt], teacher_head, teacher_head_sib, chips
    )

    place = jnp.stack([z, core]).astype(jnp.int32)
    split = count * tok_block
    hidden_near = (mine[:split, dt:], others[:split, dt:])
    hidden_far = (mine[split:, dt:], others[split:, dt:])

    def ring(parts, meanwhile=()):
        parts = dict(zip(order, parts))
        right, left = first(parts[half_way])
        right, left = along(right, 1), along(left, -1)
        for step in range(1, half_way):
            right, left = hop(
                right, left, parts[half_way - step], parts[half_way + step]
            )
            if step == half_way - 1:
                right, left, meanwhile = lax.optimization_barrier((right, left, meanwhile))
            right, left = along(right, 1), along(left, -1)
        return (right, left, parts[0]), meanwhile

    offset = lax.axis_index("tensor") * voc_local
    target_here = jnp.broadcast_to((targets - offset)[:, None], (tok_block, 128))

    student, _ = ring(student_part)
    teacher, (hidden_near, hidden_far) = ring(teacher_part, (hidden_near, hidden_far))
    teacher_logits, student_logits, stats = meet(teacher, student, target_here)
    own = payload(teacher_logits, student_logits, spread(stats, "tensor"), target_here)

    pieces = [[None] * chips, [None] * chips]
    right, left = list(own), list(own)
    pieces[0][0], pieces[1][0] = own
    for step in range(1, half_way):
        for side in range(2):
            right[side] = along(right[side], 1)
            left[side] = along(left[side], -1)
            pieces[side][chips - step], pieces[side][step] = right[side], left[side]

    def gathered(js):
        group = [jnp.concatenate([x[j] for j in js], axis=0) for x in pieces]
        return group, [swap(x) for x in group]

    last = [along(right[0], 1), along(left[1], -1)]
    early = {j: [x[j] for x in pieces] for j in order[:count]}
    early, last[0] = lax.optimization_barrier((early, last[0]))
    for j, pair in early.items():
        pieces[0][j], pieces[1][j] = pair
    near = gathered(order[:count])
    pieces[0][half_way], pieces[1][half_way] = last
    far = gathered(order[count:])
    sums = own_products(
        student_head, (hidden_near[0], hidden_far[0]), (near[0], far[0])
    )
    rows, grad_head = sib_products(
        order, place, student_head, sums,
        (hidden_near[1], hidden_far[1]), (near[1], far[1]), tok_block,
    )
    rows, grad_head = lax.optimization_barrier((rows, grad_head))
    extra = sum(
        jnp.sum(g[1][:, half:].astype(f32), axis=0) for group in (near, far) for g in group
    )
    loss = (extra[0] + extra[1] + extra[2]) / (tok_block * section_size)
    grad_hidden = jnp.sum(lax.all_to_all(rows, "tensor", 0, 0), axis=0).astype(bf16)
    return (loss, grad_hidden, grad_head), extra[3]


def shards(*arrays):
    fine, too_coarse = steps(*arrays)
    return lax.cond(too_coarse > 0.0, lambda: plain(*arrays), lambda: fine)


def solution(mesh):
    placed = (
        P("tensor", "section"),
        P("tensor", "section"),
        P("section", "tensor"),
        P("section", "tensor"),
        P("section"),
    )
    return jax.shard_map(
        shards,
        mesh=mesh,
        in_specs=placed,
        out_specs=(P(), P("tensor", "section"), P("section", "tensor")),
        check_vma=False,
    )
```
